32 devices in a mesh: pipe: 2 (over core), tensor: 4 (over z), dp: 4 (over y, x).
Axes of the slice: x: 2, y: 2, z: 4, core: 2. Of those that a mesh axis runs over, the one named last changes fastest.
Arguments:
- inputs: bfloat16 [8, 1024, 2048], P('dp'), may hold values from -6 to 6
- cotangent: bfloat16 [8, 1024, 2048], P('dp'), may hold values from -6 to 6
- ln_gain: bfloat16 [2, 2048], P('pipe'), may hold values from 0.5 to 1.5
- ln_bias: bfloat16 [2, 2048], P('pipe'), may hold values from -3 to 3
- w_qkv: bfloat16 [2, 3, 2048, 2048], P('pipe', None, None, 'tensor'), may hold values from -0.1875 to 0.1875
- b_qkv: bfloat16 [2, 3, 2048], P('pipe', None, 'tensor'), may hold values from -4 to 4
- w_dense: bfloat16 [2, 2048, 2048], P('pipe', 'tensor'), may hold values from -0.5 to 0.5
- b_dense: bfloat16 [2, 2048], P('pipe'), may hold values from -3 to 3
- w_fc1: bfloat16 [2, 2048, 8192], P('pipe', None, 'tensor'), may hold values from -0.125 to 0.125
- b_fc1: bfloat16 [2, 8192], P('pipe', 'tensor'), may hold values from -4 to 4
- w_fc2: bfloat16 [2, 8192, 2048], P('pipe', 'tensor'), may hold values from -0.09375 to 0.09375
- b_fc2: bfloat16 [2, 2048], P('pipe'), may hold values from -3 to 3
Outputs:
- acts: bfloat16 [2, 8, 1024, 2048], P('pipe', 'dp', 'tensor')
- input_grads: bfloat16 [2, 8, 1024, 2048], P('pipe', 'dp', 'tensor')
- grad_ln_gain: float32 [2, 2048], P('pipe', ('tensor', 'dp'))
- grad_ln_bias: float32 [2, 2048], P('pipe', ('tensor', 'dp'))
- grad_w_qkv: float32 [2, 3, 2048, 2048], P('pipe', None, 'dp', 'tensor')
- grad_b_qkv: float32 [2, 3, 2048], P('pipe', None, ('tensor', 'dp'))
- grad_w_dense: float32 [2, 2048, 2048], P('pipe', 'tensor', 'dp')
- grad_b_dense: float32 [2, 2048], P('pipe', 'dp')
- grad_w_fc1: float32 [2, 2048, 8192], P('pipe', 'dp', 'tensor')
- grad_b_fc1: float32 [2, 8192], P('pipe', ('tensor', 'dp'))
- grad_w_fc2: float32 [2, 8192, 2048], P('pipe', 'tensor', 'dp')
- grad_b_fc2: float32 [2, 2048], P('pipe', 'dp')
The draws below stay inside these ranges and needn't reach their ends.
All inputs are finite; a program needn't handle non-finite values.
Results may differ from the reference program's by a relative error of at most 0.03.
Values may be sent and summed in bfloat16 or wider, within the bound.
A program may use at most 704 MiB of HBM per device.

```python
import jax
import jax.numpy as jnp
from jax import lax

D = 2048
HEADS = 32
HEAD_DIM = 64
ROT = 32
FF = 8192
SEQ_LEN = 1024
LAYERS = 2
SEQS = 8
QKV_WIDTH = 2048


def raised(entries, key, source, target, parts, factor):
    def block_of(dim):
        return (jnp.arange(entries.shape[dim]) // (entries.shape[dim] // parts)).reshape((-1,) + (1,) * (entries.ndim - 1 - dim))

    one_side = jax.random.permutation(key, parts)[block_of(target)]
    second = (block_of(target) + parts // 2) % parts
    return jnp.where((block_of(source) == one_side) | (block_of(source) == second), factor * entries, entries)


def shard_levels(own_key, extent, pieces, smallest, largest):
    def one(axis_at, shards_of):
        steps = jax.random.uniform(jax.random.fold_in(jax.random.fold_in(own_key, 6), axis_at), (shards_of,), jnp.float32, smallest / len(pieces), largest / len(pieces))
        return jnp.repeat(jnp.exp(steps), extent[axis_at] // shards_of).reshape((-1,) + (1,) * (len(extent) - axis_at - 1))

    loudness = one(*pieces[0])
    for cut in pieces[1:]:
        loudness = loudness * one(*cut)
    return loudness


def normal_values(own_key, extent, deviation, bound, pieces=(), held_as=jnp.bfloat16):
    entries = deviation * jax.random.normal(own_key, extent, jnp.float32)
    if pieces:
        entries = entries * shard_levels(own_key, extent, pieces, -0.22, 0.18)
    return jnp.clip(entries, -bound, bound).astype(held_as)


def heavy_noise(rng, extent, scale, limit, split, heavy, kind=jnp.bfloat16):
    result = scale * jax.random.normal(rng, extent, jnp.float32)
    if split:
        result = result * shard_levels(rng, extent, split, -0.22, 0.18)
    return jnp.clip(raised(result, jax.random.fold_in(rng, 3), *heavy), -limit, limit).astype(kind)


def setup_inputs(seed: int = 0) -> dict:
    seeds = jax.random.split(jax.random.key(seed), 13)
    return {
        "inputs": heavy_noise(seeds[0], (SEQS, SEQ_LEN, D), 1.0, 6.0, ((0, 4),), (0, 2, 4, 2.0)),
        "cotangent": heavy_noise(seeds[1], (SEQS, SEQ_LEN, D), 1.0, 6.0, ((0, 4),), (0, 2, 4, 2.0)),
        "ln_gain": jnp.clip(1.0 + 0.1 * jax.random.normal(seeds[2], (LAYERS, D), jnp.float32), 0.5, 1.5).astype(jnp.bfloat16),
        "ln_bias": normal_values(seeds[3], (LAYERS, D), 0.2, 3.0, ((0, 2),)),
        "w_qkv": normal_values(seeds[4], (LAYERS, 3, D, QKV_WIDTH), (D // 2) ** -0.5, 0.1875, ((0, 2), (3, 4))),
        "b_qkv": normal_values(seeds[5], (LAYERS, 3, QKV_WIDTH), 0.3, 4.0, ((0, 2), (2, 4))),
        "w_dense": normal_values(seeds[6], (LAYERS, QKV_WIDTH, D), (QKV_WIDTH // 16) ** -0.5, 0.5, ((0, 2), (1, 4))),
        "b_dense": normal_values(seeds[7], (LAYERS, D), 0.2, 3.0, ((0, 2),)),
        "w_fc1": normal_values(seeds[8], (LAYERS, D, FF), D ** -0.5, 0.125, ((0, 2), (2, 4))),
        "b_fc1": normal_values(seeds[9], (LAYERS, FF), 0.3, 4.0, ((0, 2), (1, 4))),
        "w_fc2": normal_values(seeds[10], (LAYERS, FF, D), (FF // 2) ** -0.5, 0.09375, ((0, 2), (1, 4))),
        "b_fc2": normal_values(seeds[11], (LAYERS, D), 0.2, 3.0, ((0, 2),)),
    }


highest = lax.Precision.HIGHEST
ln_eps = 1e-05
rope_base = 10000.0
gelu_coef = 0.7978845608028654
masked_score = -1e+30

@jax.custom_vjp
def low(v):
    return lax.optimization_barrier(v.astype(jnp.bfloat16)).astype(jnp.float32)

@jax.custom_vjp
def low_back(v):
    return v

def low_keep(v):
    return (low(v), None)

def low_pass(kept, grad):
    return (grad,)

def back_keep(v):
    return (v, None)

def back_low(kept, grad):
    return (low(grad),)
low.defvjp(low_keep, low_pass)
low_back.defvjp(back_keep, back_low)

def layer_norm(tok_rows, gain_vec, shift_vec):
    centre = tok_rows - lax.optimization_barrier(jnp.mean(tok_rows, axis=-1, keepdims=True))
    spread = lax.optimization_barrier(jnp.mean(centre * centre, axis=-1, keepdims=True))
    return centre * lax.rsqrt(spread + ln_eps) * gain_vec + shift_vec

def gelu_tanh(values):
    return 0.5 * values * (1.0 + jnp.tanh(gelu_coef * (values + 0.044715 * values * values * values)))

def rotary_tables(length):
    half_rot = ROT // 2
    inverse = rope_base ** (-(jnp.arange(half_rot, dtype=jnp.float32) * 2.0 / ROT))
    angles = jnp.arange(length, dtype=jnp.float32)[:, None] * inverse[None, :]
    return (jnp.cos(angles)[:, None, :], jnp.sin(angles)[:, None, :])

def rotate(head_rows, cosines, sines_tab):
    half_rot = ROT // 2
    leading = head_rows[..., :half_rot]
    trailing = head_rows[..., half_rot:ROT]
    return jnp.concatenate([leading * cosines - trailing * sines_tab, trailing * cosines + leading * sines_tab, head_rows[..., ROT:]], axis=-1)

def attend(queries, keys_all, values_all):
    length = queries.shape[0]
    block_rows = min(512, length)
    score_scale = HEAD_DIM ** (-0.5)
    key_pos = jnp.arange(length, dtype=jnp.int32)

    def one_block(row_start):
        query_block = lax.dynamic_slice_in_dim(queries, row_start, block_rows, 0)
        scores = jnp.einsum('qhd,khd->hqk', query_block, keys_all, precision=highest) * score_scale
        scores = low_back(scores)
        query_pos = row_start + jnp.arange(block_rows, dtype=jnp.int32)
        scores = jnp.where(key_pos[None, None, :] <= query_pos[None, :, None], scores, masked_score)
        top_score = lax.optimization_barrier(jnp.max(scores, axis=-1, keepdims=True))
        expd_scores = jnp.exp(scores - top_score)
        probs = low(expd_scores / lax.optimization_barrier(jnp.sum(expd_scores, axis=-1, keepdims=True)))
        return jnp.einsum('hqk,khd->qhd', probs, values_all, precision=highest)
    starts = jnp.arange(length // block_rows, dtype=jnp.int32) * block_rows
    blocks = lax.map(jax.checkpoint(one_block), starts)
    return blocks.reshape(length, HEADS * HEAD_DIM)

def one_layer(tok_rows, params):
    gain_vec, shift_vec, proj_weight, proj_bias, dense_weight, dense_bias, up_weight, up_bias, down_weight, down_bias = params
    length = tok_rows.shape[0]
    cosines, sines_tab = rotary_tables(length)
    normed = low(layer_norm(tok_rows, gain_vec, shift_vec))
    projected = jnp.einsum('ld,cde->cle', normed, proj_weight, precision=highest) + proj_bias[:, None, :]
    projected = low_back(projected)
    head_shape = (length, HEADS, HEAD_DIM)
    queries = low(rotate(projected[0].reshape(head_shape), cosines, sines_tab))
    keys_all = low(rotate(projected[1].reshape(head_shape), cosines, sines_tab))
    values_all = low(projected[2].reshape(head_shape))
    merged = low(low_back(attend(queries, keys_all, values_all)))
    pre_act = low_back(jnp.dot(normed, up_weight, precision=highest) + up_bias)
    activated = low(gelu_tanh(pre_act))
    attn_part = jnp.dot(merged, dense_weight, precision=highest) + dense_bias
    mlp_part = jnp.dot(activated, down_weight, precision=highest) + down_bias
    return tok_rows + attn_part + mlp_part

def reference(inputs, cotangent, ln_gain, ln_bias, w_qkv, b_qkv, w_dense, b_dense, w_fc1, b_fc1, w_fc2, b_fc2):
    params = tuple((item.astype(jnp.float32) for item in (ln_gain, ln_bias, w_qkv, b_qkv, w_dense, b_dense, w_fc1, b_fc1, w_fc2, b_fc2)))
    layer_count = ln_gain.shape[0]

    def forward(first_rows, inserts, layer_params):
        outputs = []
        tok_rows = first_rows + inserts[0]
        for layer_index in range(layer_count):
            if layer_index > 0:
                tok_rows = low(low_back(tok_rows)) + inserts[layer_index]
            chosen = tuple((item[layer_index] for item in layer_params))
            tok_rows = one_layer(tok_rows, chosen)
            outputs.append(tok_rows)
        return (tok_rows, jnp.stack(outputs))

    def one_sequence(totals, pair):
        seq_rows, seq_cot = pair
        inserts = jnp.zeros((layer_count,) + seq_rows.shape, jnp.float32)
        last_rows, back_fn, stacked = jax.vjp(forward, seq_rows, inserts, params, has_aux=True)
        grads = back_fn(seq_cot)
        totals = jax.tree.map(jnp.add, totals, grads[2])
        return (totals, (stacked.astype(jnp.bfloat16), grads[1].astype(jnp.bfloat16)))
    start_totals = jax.tree.map(jnp.zeros_like, params)
    totals, (acts, in_grads) = lax.scan(one_sequence, start_totals, (inputs.astype(jnp.float32), cotangent.astype(jnp.float32)))
    acts = jnp.transpose(acts, (1, 0, 2, 3))
    in_grads = jnp.transpose(in_grads, (1, 0, 2, 3))
    return (acts, in_grads, totals[0], totals[1], totals[2], totals[3], totals[4], totals[5], totals[6], totals[7], totals[8], totals[9])
```

```python
import functools

import jax
import jax.numpy as jnp
from jax import lax
from jax.experimental import pallas as pl
from jax.experimental.pallas import tpu as pltpu
from jax.sharding import PartitionSpec as P

HEAD_DIM = 64
ROT = 32
LANES = 128
BLOCK = 256
CHUNK = 512
PIECES = 2
MIB = 1024 * 1024

ln_eps = 1e-05
rope_base = 10000.0
gelu_coef = 0.7978845608028654
masked_score = -1e30

BF = jnp.bfloat16
F32 = jnp.float32


def rotary_tables(length):
    half_rot = ROT // 2
    inverse = rope_base ** (-(jnp.arange(half_rot, dtype=F32) * 2.0 / ROT))
    angles = jnp.arange(length, dtype=F32)[:, None] * inverse[None, :]
    cosines, sines = jnp.cos(angles), jnp.sin(angles)
    rest = HEAD_DIM - ROT
    blank = jnp.zeros((length, half_rot), F32)
    tail = jnp.zeros((length, rest), F32)
    cos_head = jnp.concatenate([cosines, cosines, jnp.ones((length, rest), F32)], axis=1)
    near_head = jnp.concatenate([-sines, blank, tail], axis=1)
    far_head = jnp.concatenate([blank, sines, tail], axis=1)
    pair = LANES // HEAD_DIM
    return tuple(jnp.tile(part, (1, pair)) for part in (cos_head, near_head, far_head))


def turn(values, cos, near, far):
    half_rot = ROT // 2
    return (
        values * cos
        + pltpu.roll(values, LANES - half_rot, 1) * near
        + pltpu.roll(values, half_rot, 1) * far
    )


def head_mask(rows, which):
    lanes = lax.broadcasted_iota(jnp.int32, (rows, LANES), 1)
    return (lanes // HEAD_DIM) == which


def as_row(column):
    return jnp.transpose(jnp.broadcast_to(column, (column.shape[0], LANES)))[0:1, :]


def dot_nt(left, right):
    return lax.dot_general(left, right, (((1,), (1,)), ((), ())), preferred_element_type=F32)


def dot_nn(left, right):
    return lax.dot_general(left, right, (((1,), (0,)), ((), ())), preferred_element_type=F32)


def dot_tn(left, right):
    return lax.dot_general(left, right, (((0,), (0,)), ((), ())), preferred_element_type=F32)


def attend_kernel(prev, *refs):
    proj_ref, cos_ref, near_ref, far_ref = refs[:4]
    k_prev = refs[4 : 4 + prev]
    v_prev = refs[4 + prev : 4 + 2 * prev]
    q_ref, k_ref, o_ref, log_ref = refs[4 + 2 * prev :]
    rows = q_ref.shape[0]
    tables = (cos_ref[...], near_ref[...], far_ref[...])
    scale = HEAD_DIM ** (-0.5)
    q_ref[...] = (turn(proj_ref[0].astype(F32), *tables) * scale).astype(BF)
    k_ref[...] = turn(proj_ref[1].astype(F32), *tables).astype(BF)
    keep = lax.broadcasted_iota(jnp.int32, (BLOCK, BLOCK), 1) <= lax.broadcasted_iota(
        jnp.int32, (BLOCK, BLOCK), 0
    )
    for start in range(0, rows, BLOCK):
        here = pl.ds(start, BLOCK)
        query = q_ref[here, :]
        outs = []
        for which in range(LANES // HEAD_DIM):
            mask = head_mask(BLOCK, which)
            mine = jnp.where(mask, query, jnp.zeros_like(query))
            scores = [dot_nt(mine, ref[...]) for ref in k_prev]
            if start:
                scores.append(dot_nt(mine, k_ref[0:start, :]))
            scores.append(jnp.where(keep, dot_nt(mine, k_ref[here, :]), masked_score))
            top = functools.reduce(
                jnp.maximum, [jnp.max(part, axis=1, keepdims=True) for part in scores]
            )
            weights = [jnp.exp(part - top) for part in scores]
            total = functools.reduce(
                jnp.add, [jnp.sum(part, axis=1, keepdims=True) for part in weights]
            )
            values = [ref[0] for ref in v_prev]
            if start:
                values.append(proj_ref[2, 0:start, :])
            values.append(proj_ref[2, here, :])
            merged = functools.reduce(
                jnp.add, [dot_nn(w.astype(BF), v) for w, v in zip(weights, values)]
            )
            outs.append(merged / total)
            log_ref[0, which : which + 1, here] = as_row(top + jnp.log(total))
        o_ref[here, :] = jnp.where(head_mask(BLOCK, 0), outs[0], outs[1]).astype(BF)


def attend(proj, tables, k_prev, proj_prev):
    _, rows, width = proj.shape
    pairs = width // LANES
    prev = len(k_prev)
    tile = pl.BlockSpec((rows, LANES), lambda j: (0, j))
    table = pl.BlockSpec((rows, LANES), lambda j: (0, 0))
    in_specs = [pl.BlockSpec((3, rows, LANES), lambda j: (0, 0, j))] + [table] * 3
    in_specs += [pl.BlockSpec((k.shape[0], LANES), lambda j: (0, j)) for k in k_prev]
    in_specs += [pl.BlockSpec((1, v.shape[1], LANES), lambda j: (2, 0, j)) for v in proj_prev]
    keys = rows + sum(k.shape[0] for k in k_prev)
    flat = jax.ShapeDtypeStruct((rows, width), BF)
    return pl.pallas_call(
        functools.partial(attend_kernel, prev),
        name="attend",
        grid=(pairs,),
        in_specs=in_specs,
        out_specs=[tile, tile, tile, pl.BlockSpec((1, 8, rows), lambda j: (j, 0, 0))],
        out_shape=[flat, flat, flat, jax.ShapeDtypeStruct((pairs, 8, rows), F32)],
        compiler_params=pltpu.CompilerParams(vmem_limit_bytes=40 * MIB),
        cost_estimate=pl.CostEstimate(
            flops=16 * rows * keys * width, bytes_accessed=16 * keys * width, transcendentals=0
        ),
    )(proj, *tables, *k_prev, *proj_prev)


def attend_back_kernel(prev, carried, *refs):
    at = 0

    def take(count):
        nonlocal at
        at += count
        return refs[at - count : at]

    q_ref, do_ref, o_ref, log_ref = take(4)
    cos_ref, near_ref, far_ref = take(3)
    k_refs = take(prev + 1)
    v_refs = take(prev + 1)
    dk_in = take(prev + 1 if carried else 0)
    dv_in = take(prev + 1 if carried else 0)
    (dproj_ref,) = take(1)
    dk_out = take(prev)
    dv_out = take(prev)
    dk_own, dv_own = take(2)
    rows = q_ref.shape[0]
    dk_all = list(dk_out) + [dk_own]
    dv_all = list(dv_out) + [dv_own]
    for index in range(prev + 1):
        if carried:
            dk_all[index][...] = dk_in[index][...]
            dv_all[index][...] = dv_in[index][...]
        else:
            dk_all[index][...] = jnp.zeros_like(dk_all[index])
            dv_all[index][...] = jnp.zeros_like(dv_all[index])
    tables = (cos_ref[...], near_ref[...], far_ref[...])
    keep = lax.broadcasted_iota(jnp.int32, (BLOCK, BLOCK), 0) <= lax.broadcasted_iota(
        jnp.int32, (BLOCK, BLOCK), 1
    )
    scale = HEAD_DIM ** (-0.5)
    for start in range(0, rows, BLOCK):
        here = pl.ds(start, BLOCK)
        query, upstream = q_ref[here, :], do_ref[here, :]
        product = upstream.astype(F32) * o_ref[here, :].astype(F32)
        grads = []
        for which in range(LANES // HEAD_DIM):
            mask = head_mask(BLOCK, which)
            mine = jnp.where(mask, query, jnp.zeros_like(query))
            mine_up = jnp.where(mask, upstream, jnp.zeros_like(upstream))
            logs = log_ref[0, which : which + 1, here]
            centre = as_row(jnp.sum(jnp.where(mask, product, 0.0), axis=1, keepdims=True))
            segments = [(index, pl.ds(0, k_refs[index].shape[0]), False) for index in range(prev)]
            if start:
                segments.append((prev, pl.ds(0, start), False))
            segments.append((prev, here, True))
            grad = jnp.zeros((BLOCK, LANES), F32)
            for index, span, diagonal in segments:
                keys = k_refs[index][span, :]
                probs = jnp.exp(dot_nt(keys, mine) - logs)
                if diagonal:
                    probs = jnp.where(keep, probs, 0.0)
                grad_probs = dot_nt(v_refs[index][0, span, :], mine_up)
                grad_scores = (probs * (grad_probs - centre)).astype(BF)
                dv_all[index][span, :] += dot_nn(probs.astype(BF), mine_up)
                dk_all[index][span, :] += dot_nn(grad_scores, mine)
                grad = grad + dot_tn(grad_scores, keys)
            grads.append(grad)
        merged = jnp.where(head_mask(BLOCK, 0), grads[0], grads[1]) * scale
        near, far = near_ref[here, :], far_ref[here, :]
        dproj_ref[0, here, :] = turn(merged, cos_ref[here, :], -near, -far).astype(BF)
    dproj_ref[1] = turn(dk_own[...], tables[0], -tables[1], -tables[2]).astype(BF)
    dproj_ref[2] = dv_own[...].astype(BF)


def attend_back(query, upstream, merged, logs, tables, keys, projs, dk_in, dv_in):
    rows, width = query.shape
    pairs = width // LANES
    prev = len(keys) - 1
    carried = dk_in is not None
    tile = pl.BlockSpec((rows, LANES), lambda j: (0, j))
    table = pl.BlockSpec((rows, LANES), lambda j: (0, 0))
    of_k = [pl.BlockSpec((k.shape[0], LANES), lambda j: (0, j)) for k in keys]
    of_v = [pl.BlockSpec((1, v.shape[1], LANES), lambda j: (2, 0, j)) for v in projs]
    in_specs = [tile] * 3 + [pl.BlockSpec((1, 8, rows), lambda j: (j, 0, 0))] + [table] * 3
    in_specs += of_k + of_v + (of_k + of_k if carried else [])
    sums = [jax.ShapeDtypeStruct(k.shape, F32) for k in keys[:-1]]
    total = sum(k.shape[0] for k in keys)
    outs = pl.pallas_call(
        functools.partial(attend_back_kernel, prev, carried),
        name="attend_back",
        grid=(pairs,),
        in_specs=in_specs,
        out_specs=[pl.BlockSpec((3, rows, LANES), lambda j: (0, 0, j))] + of_k[:-1] * 2,
        out_shape=[jax.ShapeDtypeStruct((3, rows, width), BF)] + sums * 2,
        scratch_shapes=[pltpu.VMEM((rows, LANES), F32)] * 2,
        compiler_params=pltpu.CompilerParams(vmem_limit_bytes=40 * MIB),
        cost_estimate=pl.CostEstimate(
            flops=40 * rows * total * width, bytes_accessed=20 * total * width, transcendentals=0
        ),
    )(
        query, upstream, merged, logs, *tables, *keys, *projs,
        *((list(dk_in) + list(dv_in)) if carried else []),
    )
    return outs[0], list(outs[1 : 1 + prev]), list(outs[1 + prev :])


def line_scatter_sum(parts, axis, rank):
    left = rank < 2
    far = lax.dynamic_slice_in_dim(parts, jnp.where(left, 2, 0), 2, 0)
    near = lax.dynamic_slice_in_dim(parts, jnp.where(left, 0, 2), 2, 0)
    first = lax.ppermute(far, axis, [(0, 1), (3, 2)])
    beside = lax.ppermute(
        lax.dynamic_index_in_dim(parts, jnp.where(left, 1, 2), 0, keepdims=False),
        axis,
        [(0, 1), (3, 2)],
    )
    middle = (far.astype(F32) + first.astype(F32)).astype(BF)
    second = lax.ppermute(middle, axis, [(1, 2), (2, 1)])
    outer = jnp.where(left, 0, 1)
    last = lax.ppermute(
        (
            lax.dynamic_index_in_dim(near, outer, 0, keepdims=False).astype(F32)
            + lax.dynamic_index_in_dim(second, outer, 0, keepdims=False).astype(F32)
        ).astype(BF),
        axis,
        [(1, 0), (2, 3)],
    )
    slot = rank % 2
    own = lax.dynamic_index_in_dim(near, slot, 0, keepdims=False).astype(F32)
    mid = lax.dynamic_index_in_dim(second, slot, 0, keepdims=False).astype(F32)
    return own + mid + beside.astype(F32) + last.astype(F32)


def line_gather(block, axis, rank):
    right1 = lax.ppermute(block, axis, [(0, 1), (1, 2), (2, 3)])
    left1 = lax.ppermute(block, axis, [(3, 2), (2, 1), (1, 0)])
    right2 = lax.ppermute(right1, axis, [(1, 2), (2, 3)])
    left2 = lax.ppermute(left1, axis, [(2, 1), (1, 0)])
    right3 = lax.ppermute(right2, axis, [(2, 3)])
    left3 = lax.ppermute(left2, axis, [(1, 0)])
    every = jnp.stack([right3, right2, right1, block, left1, left2, left3])
    return lax.dynamic_slice_in_dim(every, 3 - rank, 4, 0)


def bit_pairs(size, bit):
    return [(index, index ^ bit) for index in range(size)]


def halving_sum(grad, axis, rank, size, order):
    rows = grad.shape[0] // size
    bits = []
    bit = 1
    while bit < size:
        bits.append(bit)
        bit *= 2
    if order:
        bits = bits[::-1]
    held = grad.reshape([2] * len(bits) + [rows, grad.shape[1]])
    names = [1 << (len(bits) - 1 - place) for place in range(len(bits))]
    result = held.astype(F32) if not bits else None
    for step, bit in enumerate(bits):
        place = names.index(bit)
        mine = jnp.where((rank & bit) != 0, 1, 0)
        give = lax.dynamic_index_in_dim(held, 1 - mine, place, keepdims=False)
        kept = lax.dynamic_index_in_dim(held, mine, place, keepdims=False)
        got = lax.ppermute(give, axis, bit_pairs(size, bit))
        result = kept.astype(F32) + got.astype(F32)
        held = result.astype(BF)
        names.pop(place)
    return result


def dp_share(grad, axis, rank, size):
    cut = grad.shape[1] // 2
    return jnp.concatenate(
        [
            halving_sum(grad[:, :cut], axis, rank, size, 0),
            halving_sum(grad[:, cut:], axis, rank, size, 1),
        ],
        axis=1,
    ).astype(BF)


def body(
    inputs, cotangent, ln_gain, ln_bias, w_qkv, b_qkv, w_dense, b_dense, w_fc1, b_fc1, w_fc2, b_fc2
):
    core = lax.axis_index("pipe")
    rank = lax.axis_index("tensor")
    dp_size = lax.axis_size("dp")
    dp_rank = lax.axis_index("dp")
    first = core == 0
    _, length, width = inputs.shape
    lines = lax.axis_size("tensor")
    chunk = CHUNK
    chunks = length // chunk
    local = w_qkv.shape[3]
    hidden = w_fc1.shape[2]
    swap_pairs = [(0, 1), (1, 0)]

    def swap(value):
        return lax.ppermute(value, "pipe", swap_pairs)

    def both(own):
        other = swap(own)
        return (jnp.where(first, own, other), jnp.where(first, other, own))

    small = jnp.concatenate(
        [ln_gain[0], ln_bias[0], b_qkv[0].reshape(-1), b_dense[0], b_fc1[0], b_fc2[0]]
    )
    small_pair = both(small)
    weights = [both(w[0]) for w in (w_qkv, w_fc1, w_dense, w_fc2)]

    def layer_params(layer):
        flat = small_pair[layer].astype(F32)
        at = 0
        out = []
        for count in (width, width, 3 * local, width, hidden, width):
            out.append(flat[at : at + count])
            at += count
        gain, shift, bias3, bias_d, bias_u, bias_2 = out
        return gain, shift, bias3.reshape(3, 1, local), bias_u, bias_d + bias_2

    params = [layer_params(layer) for layer in range(2)]
    tables = rotary_tables(length)

    def rows_of(array, index):
        return array[index * chunk : (index + 1) * chunk]

    def normal(rows):
        values = rows.astype(F32)
        centre = values - jnp.mean(values, axis=-1, keepdims=True)
        spread = jnp.mean(centre * centre, axis=-1, keepdims=True)
        return centre * lax.rsqrt(spread + ln_eps)

    def forward_chunk(layer, index, rows, kept):
        gain, shift, bias3, bias_u, _ = params[layer]
        proj_w, up_w, dense_w, down_w = (pair[layer] for pair in weights)
        h = (normal(rows) * gain + shift).astype(BF)
        proj = (
            jnp.einsum("ld,cde->cle", h, proj_w, preferred_element_type=F32) + bias3
        ).astype(BF)
        query, key, merged, logs = attend(
            proj,
            [rows_of(table, index) for table in tables],
            [item["key"] for item in kept],
            [item["proj"] for item in kept],
        )
        u = jnp.dot(h, up_w, preferred_element_type=F32) + bias_u
        inner = jnp.tanh(gelu_coef * (u + 0.044715 * u * u * u))
        act = (0.5 * u * (1.0 + inner)).astype(BF)
        slope = (
            0.5 * (1.0 + inner)
            + 0.5 * u * (1.0 - inner * inner) * gelu_coef * (1.0 + 3.0 * 0.044715 * u * u)
        ).astype(BF)
        part = (
            jnp.dot(merged, dense_w, preferred_element_type=F32)
            + jnp.dot(act, down_w, preferred_element_type=F32)
        ).astype(BF)
        kept.append(
            dict(h=h, proj=proj, query=query, key=key, merged=merged, logs=logs, act=act, slope=slope)
        )
        return part

    def in_pieces(array):
        step = array.shape[-1] // PIECES
        return [array[..., i * step : (i + 1) * step] for i in range(PIECES)]

    def scatter(part):
        blocks = part.reshape(lines, part.shape[0] // lines, width)
        return jnp.concatenate(
            [line_scatter_sum(piece, "tensor", rank) for piece in in_pieces(blocks)], axis=-1
        )

    def gather(share):
        full = jnp.concatenate(
            [line_gather(piece, "tensor", rank) for piece in in_pieces(share)], axis=-1
        )
        return full.reshape(lines * share.shape[0], width)

    def share_of(rows):
        size = rows.shape[0] // lines
        return lax.dynamic_slice_in_dim(rows, rank * size, size, 0)

    x0 = lax.dynamic_index_in_dim(inputs, core, 0, keepdims=False)
    cot = lax.dynamic_index_in_dim(cotangent, core, 0, keepdims=False)
    cot_other = lax.dynamic_index_in_dim(cotangent, 1 - core, 0, keepdims=False)
    kept = [[], []]
    x1 = []
    for index in range(chunks):
        rows = rows_of(x0, index)
        part = forward_chunk(0, index, rows, kept[0])
        share = (share_of(rows).astype(F32) + scatter(part) + params[0][4]).astype(BF)
        x1.append(gather(share))
    parts1 = [forward_chunk(1, index, x1[index], kept[1]) for index in range(chunks)]
    x1_full = jnp.concatenate(x1, axis=0)
    act0 = share_of(x1_full)
    act1 = (act0.astype(F32) + scatter(jnp.concatenate(parts1, axis=0)) + params[1][4]).astype(BF)

    def half_of(array, which):
        size = array.shape[-1] // 2
        return lax.dynamic_slice_in_dim(array, which * size, size, array.ndim - 1)

    def backward_chunk(layer, index, rows, upstream, carry):
        gain, shift, _, _, _ = params[layer]
        proj_w, up_w, dense_w, down_w = (pair[layer] for pair in weights)
        item = kept[layer][index]
        grad_merged = jnp.einsum(
            "ld,ed->le", upstream, dense_w, preferred_element_type=F32
        ).astype(BF)
        grad_act = jnp.einsum("ld,fd->lf", upstream, down_w, preferred_element_type=F32)
        grad_pre = (grad_act * item["slope"].astype(F32)).astype(BF)
        dk_in, dv_in = carry if carry is not None else (None, None)
        grad_proj, dk_out, dv_out = attend_back(
            item["query"],
            grad_merged,
            item["merged"],
            item["logs"],
            [rows_of(table, index) for table in tables],
            [k["key"] for k in kept[layer][: index + 1]],
            [k["proj"] for k in kept[layer][: index + 1]],
            dk_in,
            dv_in,
        )
        grad_h = jnp.einsum(
            "cle,cde->ld", grad_proj, proj_w, preferred_element_type=F32
        ) + jnp.einsum("lf,df->ld", grad_pre, up_w, preferred_element_type=F32)
        gain_term = jnp.sum(grad_h * normal(rows), axis=0)
        shift_term = jnp.sum(grad_h, axis=0)
        return grad_h.astype(BF), grad_proj, grad_pre, gain_term, shift_term, (dk_out, dv_out)

    def norm_back(rows, grad_h, upstream, gain):
        values = rows.astype(F32)
        centre = values - jnp.mean(values, axis=-1, keepdims=True)
        inverse = lax.rsqrt(jnp.mean(centre * centre, axis=-1, keepdims=True) + ln_eps)
        xhat = centre * inverse
        e = grad_h * gain
        back = e - jnp.mean(e, axis=-1, keepdims=True) - xhat * jnp.mean(
            e * xhat, axis=-1, keepdims=True
        )
        return (upstream.astype(F32) + inverse * back).astype(BF)

    def backward(layer, rows_list, upstream_list, after):
        grad_projs, grad_pres = [None] * chunks, [None] * chunks
        gain_total = jnp.zeros((width,), F32)
        shift_total = jnp.zeros((width,), F32)
        carry = None
        for index in reversed(range(chunks)):
            grad_h, grad_projs[index], grad_pres[index], gain_term, shift_term, carry = (
                backward_chunk(layer, index, rows_list[index], upstream_list[index], carry)
            )
            gain_total = gain_total + gain_term
            shift_total = shift_total + shift_term
            after(index, grad_h)
        grad_proj = jnp.concatenate(grad_projs, axis=1)
        grad_pre = jnp.concatenate(grad_pres, axis=0)
        bias_terms = [
            jnp.sum(grad_proj, axis=1, dtype=F32),
            jnp.sum(grad_pre, axis=0, dtype=F32),
        ]
        return grad_proj, grad_pre, gain_total, shift_total, bias_terms

    def pair_dot(left, right):
        return sum(
            jnp.einsum("ld,lf->df", a, b, preferred_element_type=F32) for a, b in zip(left, right)
        ).astype(BF)

    def weight_share(left, right):
        return dp_share(pair_dot(left, right), "dp", dp_rank, dp_size)

    def exchange_half(array):
        return half_of(array, core), swap(half_of(array, 1 - core))

    def kept_rows(layer, name):
        return jnp.concatenate([item[name] for item in kept[layer]], axis=0)

    def down_shares(layer, upstreams):
        act = exchange_half(kept_rows(layer, "act"))
        merged = exchange_half(kept_rows(layer, "merged"))
        return weight_share(upstreams, act), weight_share(upstreams, merged)

    def up_shares(layer, grad_proj, grad_pre):
        h = kept_rows(layer, "h")
        h_pair = (h, swap(h))
        pre_pair = exchange_half(grad_pre)
        proj_own, proj_other = exchange_half(grad_proj)
        side = proj_own.shape[2]

        def flat(three):
            return jnp.concatenate([three[0], three[1], three[2]], axis=1)

        up = weight_share(h_pair, pre_pair)
        proj = weight_share(h_pair, (flat(proj_own), flat(proj_other)))
        return up, proj, side

    down1 = down_shares(1, (cot, cot_other))
    dr1 = [None] * chunks
    dr1_full = [None] * chunks

    def after1(index, grad_h):
        upstream = rows_of(cot, index)
        total = scatter(grad_h)
        dr1[index] = norm_back(share_of(x1[index]), total, share_of(upstream), params[1][0])
        dr1_full[index] = gather(dr1[index])

    grad_proj1, grad_pre1, gain1, shift1, biases1 = backward(
        1, x1, [rows_of(cot, i) for i in range(chunks)], after1
    )
    up1 = up_shares(1, grad_proj1, grad_pre1)
    dy0 = jnp.concatenate(dr1_full, axis=0)
    down0 = down_shares(0, (dy0, swap(dy0)))
    grads_h0 = [None] * chunks

    def after0(index, grad_h):
        grads_h0[index] = grad_h

    grad_proj0, grad_pre0, gain0, shift0, biases0 = backward(
        0, [rows_of(x0, i) for i in range(chunks)], dr1_full, after0
    )
    total0 = scatter(jnp.concatenate(grads_h0, axis=0))
    dr0_share = norm_back(share_of(x0), total0, share_of(dy0), params[0][0])
    dr1_share = share_of(dy0)
    up0 = up_shares(0, grad_proj0, grad_pre0)

    def to_owner(value0, value1):
        from1 = lax.ppermute(value0, "pipe", [(1, 0)])
        from0 = lax.ppermute(value1, "pipe", [(0, 1)])
        return jnp.where(first, value0, value1), jnp.where(first, from1, from0)

    def in_order(own, other, axis):
        return jnp.where(
            first,
            jnp.concatenate([own, other], axis=axis),
            jnp.concatenate([other, own], axis=axis),
        )

    def assembled(value0, value1, axis):
        own, other = to_owner(value0, value1)
        return in_order(own.astype(F32), other.astype(F32), axis)

    def stacked(value0, value1):
        own, other = to_owner(value0, value1)
        return in_order(own[None], other[None], 0)

    acts = stacked(act0, act1)
    grads_in = stacked(dr0_share, dr1_share)
    out_fc2 = assembled(down0[0], down1[0], 1).T
    out_dense = assembled(down0[1], down1[1], 1).T
    out_fc1 = assembled(up0[0], up1[0], 1)
    side = up0[2]
    rows_dp = up0[1].shape[0]

    def split3(value):
        return value.reshape(rows_dp, 3, side)

    out_qkv = jnp.transpose(assembled(split3(up0[1]), split3(up1[1]), 2), (1, 0, 2))

    def vector(layer, gain, shift, biases, upstream):
        out_bias = jnp.sum(upstream, axis=0, dtype=F32)
        return jnp.concatenate(
            [gain, shift, biases[0].reshape(-1), biases[1], out_bias]
        ).reshape(-1, LANES)

    def butterfly(value, axis, size):
        bit = 1
        while bit < size:
            value = value + lax.ppermute(value, axis, bit_pairs(size, bit))
            bit *= 2
        return value

    def small_sums(packed):
        packed = butterfly(butterfly(packed, "pipe", 2), "dp", dp_size)
        cut = 2 * width // LANES
        norm = butterfly(packed[:cut], "tensor", lines)
        return norm.reshape(-1), packed[cut:].reshape(-1)

    norm1, rest1 = small_sums(vector(1, gain1, shift1, biases1, cot))
    norm0, rest0 = small_sums(vector(0, gain0, shift0, biases0, dy0))
    norm = jnp.where(first, norm0, norm1)
    rest = jnp.where(first, rest0, rest1)
    place = rank * dp_size + dp_rank
    norm_size = width // (lines * dp_size)

    def piece(vec, offset, size):
        return lax.dynamic_slice_in_dim(vec, offset, size, 0)

    out_gain = piece(norm, place * norm_size, norm_size)
    out_shift = piece(norm, width + place * norm_size, norm_size)
    bias_size = local // dp_size
    out_bqkv = lax.dynamic_slice_in_dim(
        rest[: 3 * local].reshape(3, local), dp_rank * bias_size, bias_size, 1
    )
    up_size = hidden // dp_size
    out_bfc1 = piece(rest, 3 * local + dp_rank * up_size, up_size)
    out_size = width // dp_size
    out_bout = piece(rest, 3 * local + hidden + dp_rank * out_size, out_size)
    return (
        acts[None],
        grads_in[None],
        out_gain[None],
        out_shift[None],
        out_qkv[None],
        out_bqkv[None],
        out_dense[None],
        out_bout[None],
        out_fc1[None],
        out_bfc1[None],
        out_fc2[None],
        out_bout[None],
    )


def solution(mesh):
    in_specs = (
        P("dp", None, None),
        P("dp", None, None),
        P("pipe", None),
        P("pipe", None),
        P("pipe", None, None, "tensor"),
        P("pipe", None, "tensor"),
        P("pipe", "tensor", None),
        P("pipe", None),
        P("pipe", None, "tensor"),
        P("pipe", "tensor"),
        P("pipe", "tensor", None),
        P("pipe", None),
    )
    out_specs = (
        P("pipe", "dp", "tensor", None),
        P("pipe", "dp", "tensor", None),
        P("pipe", ("tensor", "dp")),
        P("pipe", ("tensor", "dp")),
        P("pipe", None, "dp", "tensor"),
        P("pipe", None, ("tensor", "dp")),
        P("pipe", "tensor", "dp"),
        P("pipe", "dp"),
        P("pipe", "dp", "tensor"),
        P("pipe", ("tensor", "dp")),
        P("pipe", "tensor", "dp"),
        P("pipe", "dp"),
    )
    return jax.shard_map(body, mesh=mesh, in_specs=in_specs, out_specs=out_specs, check_vma=False)
```

```python
import functools

import jax
import jax.numpy as jnp
from jax import lax
from jax.experimental import pallas as pl
from jax.experimental.pallas import tpu as pltpu
from jax.sharding import PartitionSpec as P

HEAD_DIM = 64
ROT = 32
LANES = 128
BLOCK = 256
CHUNK = 512
PIECES = 2
MIB = 1024 * 1024

ln_eps = 1e-05
rope_base = 10000.0
gelu_coef = 0.7978845608028654
masked_score = -1e30

BF = jnp.bfloat16
F32 = jnp.float32


def rotary_tables(length):
    half_rot = ROT // 2
    inverse = rope_base ** (-(jnp.arange(half_rot, dtype=F32) * 2.0 / ROT))
    angles = jnp.arange(length, dtype=F32)[:, None] * inverse[None, :]
    cosines, sines = jnp.cos(angles), jnp.sin(angles)
    rest = HEAD_DIM - ROT
    blank = jnp.zeros((length, half_rot), F32)
    tail = jnp.zeros((length, rest), F32)
    cos_head = jnp.concatenate([cosines, cosines, jnp.ones((length, rest), F32)], axis=1)
    near_head = jnp.concatenate([-sines, blank, tail], axis=1)
    far_head = jnp.concatenate([blank, sines, tail], axis=1)
    pair = LANES // HEAD_DIM
    return tuple(jnp.tile(part, (1, pair)) for part in (cos_head, near_head, far_head))


def turn(values, cos, near, far):
    half_rot = ROT // 2
    return (
        values * cos
        + pltpu.roll(values, LANES - half_rot, 1) * near
        + pltpu.roll(values, half_rot, 1) * far
    )


def head_mask(rows, which):
    lanes = lax.broadcasted_iota(jnp.int32, (rows, LANES), 1)
    return (lanes // HEAD_DIM) == which


def as_row(column):
    return jnp.transpose(jnp.broadcast_to(column, (column.shape[0], LANES)))[0:1, :]


def dot_nt(left, right):
    return lax.dot_general(left, right, (((1,), (1,)), ((), ())), preferred_element_type=F32)


def dot_nn(left, right):
    return lax.dot_general(left, right, (((1,), (0,)), ((), ())), preferred_element_type=F32)


def dot_tn(left, right):
    return lax.dot_general(left, right, (((0,), (0,)), ((), ())), preferred_element_type=F32)


def attend_back_kernel(prev, carried, *refs):
    at = 0

    def take(count):
        nonlocal at
        at += count
        return refs[at - count : at]

    q_ref, do_ref, o_ref, log_ref = take(4)
    cos_ref, near_ref, far_ref = take(3)
    k_refs = take(prev + 1)
    v_refs = take(prev + 1)
    dk_in = take(prev + 1 if carried else 0)
    dv_in = take(prev + 1 if carried else 0)
    (dproj_ref,) = take(1)
    dk_out = take(prev)
    dv_out = take(prev)
    dk_own, dv_own = take(2)
    rows = q_ref.shape[0]
    dk_all = list(dk_out) + [dk_own]
    dv_all = list(dv_out) + [dv_own]
    for index in range(prev + 1):
        if carried:
            dk_all[index][...] = dk_in[index][...]
            dv_all[index][...] = dv_in[index][...]
        else:
            dk_all[index][...] = jnp.zeros_like(dk_all[index])
            dv_all[index][...] = jnp.zeros_like(dv_all[index])
    tables = (cos_ref[...], near_ref[...], far_ref[...])
    keep = lax.broadcasted_iota(jnp.int32, (BLOCK, BLOCK), 0) <= lax.broadcasted_iota(
        jnp.int32, (BLOCK, BLOCK), 1
    )
    scale = HEAD_DIM ** (-0.5)
    for start in range(0, rows, BLOCK):
        here = pl.ds(start, BLOCK)
        query, upstream = q_ref[here, :], do_ref[here, :]
        product = upstream.astype(F32) * o_ref[here, :].astype(F32)
        grads = []
        for which in range(LANES // HEAD_DIM):
            mask = head_mask(BLOCK, which)
            mine = jnp.where(mask, query, jnp.zeros_like(query))
            mine_up = jnp.where(mask, upstream, jnp.zeros_like(upstream))
            logs = log_ref[0, which : which + 1, here]
            centre = as_row(jnp.sum(jnp.where(mask, product, 0.0), axis=1, keepdims=True))
            segments = [(index, pl.ds(0, k_refs[index].shape[0]), False) for index in range(prev)]
            if start:
                segments.append((prev, pl.ds(0, start), False))
            segments.append((prev, here, True))
            grad = jnp.zeros((BLOCK, LANES), F32)
            for index, span, diagonal in segments:
                keys = k_refs[index][span, :]
                probs = jnp.exp(dot_nt(keys, mine) - logs)
                if diagonal:
                    probs = jnp.where(keep, probs, 0.0)
                grad_probs = dot_nt(v_refs[index][span, :], mine_up)
                grad_scores = (probs * (grad_probs - centre)).astype(BF)
                dv_all[index][span, :] += dot_nn(probs.astype(BF), mine_up)
                dk_all[index][span, :] += dot_nn(grad_scores, mine)
                grad = grad + dot_tn(grad_scores, keys)
            grads.append(grad)
        merged = jnp.where(head_mask(BLOCK, 0), grads[0], grads[1]) * scale
        near, far = near_ref[here, :], far_ref[here, :]
        dproj_ref[0, here, :] = turn(merged, cos_ref[here, :], -near, -far).astype(BF)
    dproj_ref[1] = turn(dk_own[...], tables[0], -tables[1], -tables[2]).astype(BF)
    dproj_ref[2] = dv_own[...].astype(BF)


def attend_back(query, upstream, merged, logs, tables, keys, values, dk_in, dv_in):
    rows, width = query.shape
    pairs = width // LANES
    prev = len(keys) - 1
    carried = dk_in is not None
    tile = pl.BlockSpec((rows, LANES), lambda j: (0, j))
    table = pl.BlockSpec((rows, LANES), lambda j: (0, 0))
    of_k = [pl.BlockSpec((k.shape[0], LANES), lambda j: (0, j)) for k in keys]
    of_v = [pl.BlockSpec((v.shape[0], LANES), lambda j: (0, j)) for v in values]
    in_specs = [tile] * 3 + [pl.BlockSpec((1, 8, rows), lambda j: (j, 0, 0))] + [table] * 3
    in_specs += of_k + of_v + (of_k + of_k if carried else [])
    sums = [jax.ShapeDtypeStruct(k.shape, F32) for k in keys[:-1]]
    total = sum(k.shape[0] for k in keys)
    outs = pl.pallas_call(
        functools.partial(attend_back_kernel, prev, carried),
        name="attend_back",
        grid=(pairs,),
        in_specs=in_specs,
        out_specs=[pl.BlockSpec((3, rows, LANES), lambda j: (0, 0, j))] + of_k[:-1] * 2,
        out_shape=[jax.ShapeDtypeStruct((3, rows, width), BF)] + sums * 2,
        scratch_shapes=[pltpu.VMEM((rows, LANES), F32)] * 2,
        compiler_params=pltpu.CompilerParams(vmem_limit_bytes=40 * MIB),
        cost_estimate=pl.CostEstimate(
            flops=40 * rows * total * width, bytes_accessed=20 * total * width, transcendentals=0
        ),
    )(
        query, upstream, merged, logs, *tables, *keys, *values,
        *((list(dk_in) + list(dv_in)) if carried else []),
    )
    return outs[0], list(outs[1 : 1 + prev]), list(outs[1 + prev :])


LINE = 4
STEPS = 2 * LINE
TILE = 512


def remote(src, dst, send, recv, axis, index):
    return pltpu.make_async_remote_copy(
        src_ref=src,
        dst_ref=dst,
        send_sem=send,
        recv_sem=recv,
        device_id={axis: index},
        device_id_type=pl.DeviceIdType.MESH,
    )


def greet(core, rank):
    barrier = pltpu.get_barrier_semaphore()

    def tell(axis, index):
        pl.semaphore_signal(
            barrier, inc=1, device_id={axis: index}, device_id_type=pl.DeviceIdType.MESH
        )

    tell("pipe", 1 - core)

    @pl.when(rank > 0)
    def _():
        tell("tensor", rank - 1)

    @pl.when(rank < LINE - 1)
    def _():
        tell("tensor", rank + 1)

    ends = jnp.where(rank > 0, 1, 0) + jnp.where(rank < LINE - 1, 1, 0)
    pl.semaphore_wait(barrier, 1 + ends)


def fetch_weight(layer, core, own, other, target, sem, arrival):
    @pl.when(core == layer)
    def _():
        pltpu.make_async_copy(own, target, sem).start()

    @pl.when(core != layer)
    def _():
        if arrival is not None:
            arrival.wait_recv()
        pltpu.make_async_copy(other, target, sem).start()


class LineSum:
    def __init__(self, rank, part, first, beside, second, last, result, sems, finish):
        self.rank, self.part, self.result, self.finish = rank, part, result, finish
        self.first, self.beside, self.second, self.last = first, beside, second, last
        self.sems = sems
        self.rows = part.shape[1]
        self.block = self.rows // LINE
        half = 2 * self.block
        self.left = rank < 2
        self.far = pl.multiple_of(jnp.where(self.left, half, 0), half)
        self.near = pl.multiple_of(jnp.where(self.left, 0, half), half)
        self.own = pl.multiple_of(rank * self.block, self.block)
        self.inner = (rank == 1) | (rank == 2)
        self.outer = (rank == 0) | (rank == 3)
        self.inward = jnp.where(self.left, 1, 2)
        self.outward = jnp.where(self.left, 0, 3)
        self.across = jnp.where(self.left, 2, 1)
        self.spare = pl.multiple_of(jnp.where(self.left, self.block, half), self.block)
        self.out_half = pl.multiple_of(jnp.where(self.left, 0, self.block), self.block)
        self.in_half = pl.multiple_of(jnp.where(self.left, self.block, 0), self.block)

    def hop(self, name, chunk, src, dst, to):
        return remote(src, dst, self.sems[name].at[0, chunk], self.sems[name].at[1, chunk], "tensor", to)

    def copies(self, chunk):
        half = 2 * self.block
        hop_first = self.hop(
            "first", chunk, self.part.at[chunk, pl.ds(self.far, half)], self.first.at[chunk], self.inward
        )
        hop_beside = self.hop(
            "beside",
            chunk,
            self.part.at[chunk, pl.ds(self.spare, self.block)],
            self.beside.at[chunk],
            self.inward,
        )
        hop_second = self.hop(
            "second", chunk, self.first.at[chunk], self.second.at[chunk], self.across
        )
        hop_last = self.hop(
            "last",
            chunk,
            self.second.at[chunk, pl.ds(self.out_half, self.block)],
            self.last.at[chunk],
            self.outward,
        )
        return hop_first, hop_beside, hop_second, hop_last

    def result_rows(self, chunk, shard):
        start = pl.multiple_of(chunk * self.rows + shard * self.block, self.block)
        return self.result.at[pl.ds(start, self.block)]

    def move(self, way, chunk, hop):
        step = 1 - 2 * way
        shard = jnp.clip(self.rank - step * hop, 0, LINE - 1)
        rows = self.result_rows(chunk, shard)
        name = "up" if way == 0 else "down"
        to = jnp.clip(self.rank + step, 0, LINE - 1)
        index = chunk * (LINE - 1) + hop
        return remote(rows, rows, self.sems[name].at[0, index], self.sems[name].at[1, index], "tensor", to)

    def stage_a(self, chunk):
        @pl.when(self.outer)
        def _():
            hop_first, hop_beside, _, _ = self.copies(chunk)
            hop_first.start()
            hop_beside.start()

    def stage_b(self, chunk):
        @pl.when(self.inner)
        def _():
            hop_first, _, hop_second, _ = self.copies(chunk)
            hop_first.wait_recv()
            self.first[chunk] = (
                self.first[chunk].astype(F32)
                + self.part[chunk, pl.ds(self.far, 2 * self.block)].astype(F32)
            ).astype(BF)
            hop_second.start()

    def stage_c(self, chunk):
        @pl.when(self.inner)
        def _():
            _, hop_beside, hop_second, hop_last = self.copies(chunk)
            hop_second.wait_recv()
            out_rows = pl.ds(self.out_half, self.block)
            near_out = pl.ds(pl.multiple_of(self.near + self.out_half, self.block), self.block)
            self.second[chunk, out_rows] = (
                self.second[chunk, out_rows].astype(F32) + self.part[chunk, near_out].astype(F32)
            ).astype(BF)
            hop_last.start()
            hop_beside.wait_recv()
            total = (
                self.second[chunk, pl.ds(self.in_half, self.block)].astype(F32)
                + self.beside[chunk].astype(F32)
                + self.part[chunk, pl.ds(self.own, self.block)].astype(F32)
            )
            self.finish(chunk, total, self.result_rows(chunk, self.rank))
            self.move(0, chunk, 0).start()
            self.move(1, chunk, 0).start()

    def stage_d(self, chunk):
        @pl.when(self.outer)
        def _():
            _, _, _, hop_last = self.copies(chunk)
            hop_last.wait_recv()
            total = self.last[chunk].astype(F32) + self.part[
                chunk, pl.ds(self.own, self.block)
            ].astype(F32)
            self.finish(chunk, total, self.result_rows(chunk, self.rank))

        @pl.when(self.rank == 0)
        def _():
            self.move(0, chunk, 0).start()

        @pl.when(self.rank == 3)
        def _():
            self.move(1, chunk, 0).start()

    def stage_e(self, chunk, hop):
        for way in range(2):
            behind = self.rank if way == 0 else LINE - 1 - self.rank

            @pl.when(self.inner & (behind > hop))
            def _():
                self.arrival(way, chunk, hop).wait_recv()
                self.move(way, chunk, hop + 1).start()

    def arrival(self, way, chunk, hop):
        step = 1 - 2 * way
        shard = jnp.clip(self.rank - step * (hop + 1), 0, LINE - 1)
        rows = self.result_rows(chunk, shard)
        name = "up" if way == 0 else "down"
        to = jnp.clip(self.rank + step, 0, LINE - 1)
        index = chunk * (LINE - 1) + hop
        return remote(rows, rows, self.sems[name].at[0, index], self.sems[name].at[1, index], "tensor", to)

    def stage_f(self, chunk):
        @pl.when(self.rank == 0)
        def _():
            for hop in range(LINE - 1):
                self.arrival(1, chunk, hop).wait_recv()

        @pl.when(self.rank == 3)
        def _():
            for hop in range(LINE - 1):
                self.arrival(0, chunk, hop).wait_recv()

    def sent_part(self, chunk):
        @pl.when(self.outer)
        def _():
            hop_first, hop_beside, _, _ = self.copies(chunk)
            hop_first.wait_send()
            hop_beside.wait_send()

    def sent_rest(self, chunk):
        @pl.when(self.inner)
        def _():
            _, _, hop_second, hop_last = self.copies(chunk)
            hop_second.wait_send()
            hop_last.wait_send()

        for way in range(2):
            behind = self.rank if way == 0 else LINE - 1 - self.rank
            ahead = LINE - 1 - behind
            for hop in range(LINE - 1):

                @pl.when((ahead > 0) & (behind >= hop))
                def _():
                    self.move(way, chunk, hop).wait_send()


def line_sum_scratch(rows, cols):
    block = rows // LINE
    return [
        pltpu.VMEM((LINE, 2 * block, cols), BF),
        pltpu.VMEM((LINE, block, cols), BF),
        pltpu.VMEM((LINE, 2 * block, cols), BF),
        pltpu.VMEM((LINE, block, cols), BF),
    ] + [pltpu.SemaphoreType.DMA((2, LINE))] * 4 + [
        pltpu.SemaphoreType.DMA((2, LINE * (LINE - 1)))
    ] * 2


SUM_NAMES = ("first", "beside", "second", "last", "up", "down")


def forward_kernel(*refs):
    at = 0

    def take(count):
        nonlocal at
        at += count
        return refs[at - count : at]

    (inputs_ref,) = take(1)
    own_w = take(4)
    gain_ref, shift_ref, bias3_ref, bias_u_ref, bias_o_ref = take(5)
    cos_ref, near_ref, far_ref = take(3)
    other_w = take(4)
    h_out, h_far, q_out, k_out, v_out, o_out, o_far = take(7)
    act_out, act_far, slope_out, logs_out, x1_out, part_out = take(6)
    vmem_w = take(4)
    x_buf, x_share, h_buf, act_buf, slope_buf, q_buf, o_buf, k_all, v_all, logs_buf = take(10)
    part, x1 = take(2)
    sum_bufs = take(4)
    sum_sems = dict(zip(SUM_NAMES, take(6)))
    w_sems, fetch_sems, x_sems, out_sems, slot4_sems, far_send, far_recv, once_sems = take(8)
    assert at == len(refs)
    core = lax.axis_index("pipe")
    rank = lax.axis_index("tensor")
    rows = x_buf.shape[1]
    width = x_buf.shape[2]
    local = q_buf.shape[2]
    hidden = act_buf.shape[2]
    half_hidden = hidden // 2
    half_local = local // 2
    tile = min(TILE, width)
    scale = HEAD_DIM ** (-0.5)

    weight_moves = [
        remote(own, other, w_sems.at[0, i], w_sems.at[1, i], "pipe", 1 - core)
        for i, (own, other) in enumerate(zip(own_w, other_w))
    ]

    def fetch(layer, i):
        fetch_weight(
            layer, core, own_w[i], other_w[i], vmem_w[i], fetch_sems.at[i], weight_moves[i]
        )

    def fetched(i):
        pltpu.make_async_copy(own_w[i], vmem_w[i], fetch_sems.at[i]).wait()

    def chunk_rows(chunk):
        return pl.ds(pl.multiple_of(chunk * rows, rows), rows)

    def x_copy(chunk):
        slot = lax.rem(chunk, 2)
        return pltpu.make_async_copy(
            inputs_ref.at[core, chunk_rows(chunk)], x_buf.at[slot], x_sems.at[slot]
        )

    def finish(chunk, total, target):
        value = total + x_share[chunk].astype(F32) + bias_o_ref[0:1, :]
        target[...] = value.astype(BF)

    summed = LineSum(rank, part, *sum_bufs, x1, sum_sems, finish)

    def outward(step):
        layer, chunk = lax.div(step, LINE), lax.rem(step, LINE)
        slot = lax.rem(step, 2)
        at_rows = chunk_rows(chunk)
        here = []
        for i, (buf, out) in enumerate(
            ((h_buf, h_out), (q_buf, q_out), (o_buf, o_out), (act_buf, act_out), (slope_buf, slope_out))
        ):
            here.append(
                pltpu.make_async_copy(buf.at[slot], out.at[layer, at_rows], out_sems.at[i, slot])
            )
        here.append(
            pltpu.make_async_copy(
                logs_buf.at[slot], logs_out.at[layer, :, :, at_rows], out_sems.at[5, slot]
            )
        )
        theirs = 1 - core
        act_cols = pl.ds(pl.multiple_of(theirs * half_hidden, half_hidden), half_hidden)
        o_cols = pl.ds(pl.multiple_of(theirs * half_local, half_local), half_local)
        there = [
            remote(
                h_buf.at[slot], h_far.at[layer, at_rows], far_send.at[0, slot], far_recv.at[0], "pipe", theirs
            ),
            remote(
                o_buf.at[slot, :, o_cols],
                o_far.at[layer, at_rows],
                far_send.at[1, slot],
                far_recv.at[1],
                "pipe",
                theirs,
            ),
            remote(
                act_buf.at[slot, :, act_cols],
                act_far.at[layer, at_rows],
                far_send.at[2, slot],
                far_recv.at[2],
                "pipe",
                theirs,
            ),
        ]
        return here, there

    def kv_copies(step):
        layer, chunk = lax.div(step, LINE), lax.rem(step, LINE)
        at_rows = chunk_rows(chunk)
        return [
            pltpu.make_async_copy(k_all.at[at_rows], k_out.at[layer, at_rows], slot4_sems.at[0, chunk]),
            pltpu.make_async_copy(v_all.at[at_rows], v_out.at[layer, at_rows], slot4_sems.at[1, chunk]),
        ]

    def x1_copy(chunk):
        at_rows = chunk_rows(chunk)
        return pltpu.make_async_copy(x1.at[at_rows], x1_out.at[at_rows], once_sems.at[0, chunk])

    def part_copy(chunk):
        at_rows = chunk_rows(chunk)
        return pltpu.make_async_copy(part.at[chunk], part_out.at[at_rows], once_sems.at[1, chunk])

    x_copy(0).start()
    greet(core, rank)
    for move in weight_moves:
        move.start()
    x_copy(1).start()

    keep = lax.broadcasted_iota(jnp.int32, (rows, rows), 1) <= lax.broadcasted_iota(
        jnp.int32, (rows, rows), 0
    )

    def attention(chunk, slot):
        def pair(j, _):
            lanes = pl.ds(pl.multiple_of(j * LANES, LANES), LANES)
            query = q_buf[slot, :, lanes]
            outs = []
            for which in range(LANES // HEAD_DIM):
                mask = head_mask(rows, which)
                mine = jnp.where(mask, query, jnp.zeros_like(query))
                scores = []
                if chunk:
                    scores.append(dot_nt(mine, k_all[0 : chunk * rows, lanes]))
                scores.append(
                    jnp.where(keep, dot_nt(mine, k_all[chunk * rows : (chunk + 1) * rows, lanes]), masked_score)
                )
                top = functools.reduce(
                    jnp.maximum, [jnp.max(item, axis=1, keepdims=True) for item in scores]
                )
                weights = [jnp.exp(item - top) for item in scores]
                total = functools.reduce(
                    jnp.add, [jnp.sum(item, axis=1, keepdims=True) for item in weights]
                )
                values = []
                if chunk:
                    values.append(v_all[0 : chunk * rows, lanes])
                values.append(v_all[chunk * rows : (chunk + 1) * rows, lanes])
                merged = functools.reduce(
                    jnp.add, [dot_nn(w.astype(BF), v) for w, v in zip(weights, values)]
                )
                outs.append(merged / total)
                logs_buf[slot, j, which : which + 1, :] = as_row(top + jnp.log(total))
            o_buf[slot, :, lanes] = jnp.where(head_mask(rows, 0), outs[0], outs[1]).astype(BF)
            return 0

        lax.fori_loop(0, local // LANES, pair, 0)

    def step_body(step, _):
        layer, chunk = lax.div(step, LINE), lax.rem(step, LINE)
        slot = lax.rem(step, 2)
        at_rows = chunk_rows(chunk)
        here, there = outward(step)
        kv = kv_copies(step)
        starting = chunk == 0
        ending = step == LINE - 1

        @pl.when(step >= 2)
        def _():
            old_here, old_there = outward(step - 2)
            for item in old_here:
                item.wait()
            for item in old_there:
                item.wait_send()

        small = rows // 8
        gain, shift = gain_ref[pl.ds(layer, 1), :], shift_ref[pl.ds(layer, 1), :]

        def normalise(load):
            def some(i, _):
                span = pl.ds(pl.multiple_of(i * small, small), small)
                values = load(span).astype(F32)
                centre = values - jnp.mean(values, axis=-1, keepdims=True)
                spread = jnp.mean(centre * centre, axis=-1, keepdims=True)
                h_buf[slot, span, :] = (centre * lax.rsqrt(spread + ln_eps) * gain + shift).astype(BF)
                return 0

            lax.fori_loop(0, 8, some, 0)

        @pl.when(step == 0)
        def _():
            fetch(0, 0)

        @pl.when(layer == 0)
        def _():
            x_copy(chunk).wait()
            x_share[chunk] = x_buf[slot, pl.ds(pl.multiple_of(rank * (rows // LINE), rows // LINE), rows // LINE)]
            normalise(lambda span: x_buf[slot, span, :])

            @pl.when(step + 2 < LINE)
            def _():
                x_copy(chunk + 2).start()

        @pl.when(layer == 1)
        def _():
            summed.stage_f(chunk)
            x1_copy(chunk).start()
            base = chunk * rows
            normalise(lambda span: x1[pl.ds(pl.multiple_of(base + span.start, small), small), :])

        here[0].start()
        there[0].start()

        @pl.when(starting)
        def _():
            fetched(0)

        @pl.when(layer == 1)
        def _():
            for item in kv_copies(step - LINE):
                item.wait()

        tables = (cos_ref[at_rows, :], near_ref[at_rows, :], far_ref[at_rows, :])
        h = h_buf[slot]
        for part3 in range(3):
            value = dot_nn(h, vmem_w[0][part3]) + bias3_ref[pl.ds(layer * 3 + part3, 1), :]
            for j in range(local // LANES):
                lanes = slice(j * LANES, (j + 1) * LANES)
                if part3 == 0:
                    q_buf[slot, :, lanes] = (turn(value[:, lanes], *tables) * scale).astype(BF)
                elif part3 == 1:
                    k_all[at_rows, lanes] = turn(value[:, lanes], *tables).astype(BF)
                else:
                    v_all[at_rows, lanes] = value[:, lanes].astype(BF)
        here[1].start()
        for item in kv:
            item.start()

        @pl.when(ending)
        def _():
            fetch(1, 0)

        @pl.when(step == 0)
        def _():
            fetch(0, 1)

        for index in range(LINE):

            @pl.when(chunk == index)
            def _():
                attention(index, slot)

        here[2].start()
        here[5].start()
        there[1].start()

        @pl.when(step == 0)
        def _():
            fetch(0, 2)
            fetch(0, 3)

        @pl.when((step >= 1) & (step <= LINE))
        def _():
            summed.stage_b(step - 1)

        @pl.when((step >= 2) & (step <= LINE + 1))
        def _():
            summed.stage_d(step - 2)

        @pl.when((step >= 3) & (step <= LINE + 2))
        def _():
            summed.stage_e(step - 3, 1)

        @pl.when(starting)
        def _():
            fetched(1)

        def up(i, _):
            cols = pl.ds(pl.multiple_of(i * tile, tile), tile)
            u = dot_nn(h_buf[slot], vmem_w[1][:, cols]) + bias_u_ref[pl.ds(layer, 1), cols]
            square = u * u
            inner = jnp.tanh(gelu_coef * u * (1.0 + 0.044715 * square))
            act_buf[slot, :, cols] = (0.5 * u * (1.0 + inner)).astype(BF)
            slope_buf[slot, :, cols] = (
                0.5 * (1.0 + inner)
                + (0.5 * gelu_coef) * u * (1.0 - inner * inner) * (1.0 + 3.0 * 0.044715 * square)
            ).astype(BF)
            return 0

        lax.fori_loop(0, hidden // tile, up, 0)
        here[3].start()
        here[4].start()
        there[2].start()

        @pl.when(ending)
        def _():
            fetch(1, 1)

        @pl.when(starting)
        def _():
            fetched(2)
            fetched(3)

        @pl.when(layer == 1)
        def _():
            summed.sent_part(chunk)

        def down(i, _):
            cols = pl.ds(pl.multiple_of(i * tile, tile), tile)
            part[chunk, :, cols] = (
                dot_nn(o_buf[slot], vmem_w[2][:, cols]) + dot_nn(act_buf[slot], vmem_w[3][:, cols])
            ).astype(BF)
            return 0

        lax.fori_loop(0, width // tile, down, 0)

        @pl.when(ending)
        def _():
            fetch(1, 2)
            fetch(1, 3)

        @pl.when(layer == 0)
        def _():
            summed.stage_a(chunk)

        @pl.when(layer == 1)
        def _():
            part_copy(chunk).start()

        @pl.when((step >= 1) & (step <= LINE))
        def _():
            summed.stage_c(step - 1)

        @pl.when((step >= 2) & (step <= LINE + 1))
        def _():
            summed.stage_e(step - 2, 0)

        return 0

    lax.fori_loop(0, STEPS, step_body, 0)

    for step in (STEPS - 2, STEPS - 1):
        old_here, old_there = outward(step)
        for item in old_here:
            item.wait()
        for item in old_there:
            item.wait_send()
    for chunk in range(LINE):
        for item in kv_copies(LINE + chunk):
            item.wait()
        x1_copy(chunk).wait()
        part_copy(chunk).wait()
        summed.sent_rest(chunk)
    for move in weight_moves:
        move.wait_send()
    for i, ref in enumerate((h_far, o_far, act_far)):
        remote(ref, ref, far_send.at[i, 0], far_recv.at[i], "pipe", 1 - core).wait_recv()


def forward_both(inputs, weights, vectors, tables):
    _, length, width = inputs.shape
    w_qkv, w_fc1, w_dense, w_fc2 = weights
    local, hidden = w_dense.shape[0], w_fc1.shape[1]
    rows = length // LINE
    pairs = local // LANES

    def bf(*shape):
        return jax.ShapeDtypeStruct(shape, BF)

    out_shape = [bf(*w.shape) for w in weights] + [
        bf(2, length, width),
        bf(2, length, width),
        bf(2, length, local),
        bf(2, length, local),
        bf(2, length, local),
        bf(2, length, local),
        bf(2, length, local // 2),
        bf(2, length, hidden),
        bf(2, length, hidden // 2),
        bf(2, length, hidden),
        jax.ShapeDtypeStruct((2, pairs, 8, length), F32),
        bf(length, width),
        bf(length, width),
    ]
    whole = pl.BlockSpec(memory_space=pltpu.VMEM)
    away = pl.BlockSpec(memory_space=pl.ANY)
    dma = pltpu.SemaphoreType.DMA
    return pl.pallas_call(
        forward_kernel,
        name="forward_both",
        in_specs=[away] * 5 + [whole] * 8,
        out_specs=[away] * len(out_shape),
        out_shape=out_shape,
        scratch_shapes=[pltpu.VMEM(w.shape, BF) for w in weights]
        + [
            pltpu.VMEM((2, rows, width), BF),
            pltpu.VMEM((LINE, rows // LINE, width), BF),
            pltpu.VMEM((2, rows, width), BF),
            pltpu.VMEM((2, rows, hidden), BF),
            pltpu.VMEM((2, rows, hidden), BF),
            pltpu.VMEM((2, rows, local), BF),
            pltpu.VMEM((2, rows, local), BF),
            pltpu.VMEM((length, local), BF),
            pltpu.VMEM((length, local), BF),
            pltpu.VMEM((2, pairs, 8, rows), F32),
            pltpu.VMEM((LINE, rows, width), BF),
            pltpu.VMEM((length, width), BF),
        ]
        + line_sum_scratch(rows, width)
        + [
            dma((2, 4)),
            dma((4,)),
            dma((2,)),
            dma((6, 2)),
            dma((2, LINE)),
            dma((3, 2)),
            dma((3,)),
            dma((2, LINE)),
        ],
        compiler_params=pltpu.CompilerParams(
            collective_id=0, has_side_effects=True, vmem_limit_bytes=62 * MIB
        ),
        cost_estimate=pl.CostEstimate(
            flops=4 * length * width * (4 * local + 2 * hidden),
            bytes_accessed=200 * MIB,
            transcendentals=0,
        ),
    )(inputs, *weights, *vectors, *tables)


def line_scatter_sum(parts, axis, rank):
    left = rank < 2
    far = lax.dynamic_slice_in_dim(parts, jnp.where(left, 2, 0), 2, 0)
    near = lax.dynamic_slice_in_dim(parts, jnp.where(left, 0, 2), 2, 0)
    first = lax.ppermute(far, axis, [(0, 1), (3, 2)])
    beside = lax.ppermute(
        lax.dynamic_index_in_dim(parts, jnp.where(left, 1, 2), 0, keepdims=False),
        axis,
        [(0, 1), (3, 2)],
    )
    middle = (far.astype(F32) + first.astype(F32)).astype(BF)
    second = lax.ppermute(middle, axis, [(1, 2), (2, 1)])
    outer = jnp.where(left, 0, 1)
    last = lax.ppermute(
        (
            lax.dynamic_index_in_dim(near, outer, 0, keepdims=False).astype(F32)
            + lax.dynamic_index_in_dim(second, outer, 0, keepdims=False).astype(F32)
        ).astype(BF),
        axis,
        [(1, 0), (2, 3)],
    )
    slot = rank % 2
    own = lax.dynamic_index_in_dim(near, slot, 0, keepdims=False).astype(F32)
    mid = lax.dynamic_index_in_dim(second, slot, 0, keepdims=False).astype(F32)
    return own + mid + beside.astype(F32) + last.astype(F32)


def line_gather(block, axis, rank):
    right1 = lax.ppermute(block, axis, [(0, 1), (1, 2), (2, 3)])
    left1 = lax.ppermute(block, axis, [(3, 2), (2, 1), (1, 0)])
    right2 = lax.ppermute(right1, axis, [(1, 2), (2, 3)])
    left2 = lax.ppermute(left1, axis, [(2, 1), (1, 0)])
    right3 = lax.ppermute(right2, axis, [(2, 3)])
    left3 = lax.ppermute(left2, axis, [(1, 0)])
    every = jnp.stack([right3, right2, right1, block, left1, left2, left3])
    return lax.dynamic_slice_in_dim(every, 3 - rank, 4, 0)


def bit_pairs(size, bit):
    return [(index, index ^ bit) for index in range(size)]


def halving_sum(grad, axis, rank, size, order):
    rows = grad.shape[0] // size
    bits = []
    bit = 1
    while bit < size:
        bits.append(bit)
        bit *= 2
    if order:
        bits = bits[::-1]
    held = grad.reshape([2] * len(bits) + [rows, grad.shape[1]])
    names = [1 << (len(bits) - 1 - place) for place in range(len(bits))]
    result = held.astype(F32) if not bits else None
    for step, bit in enumerate(bits):
        place = names.index(bit)
        mine = jnp.where((rank & bit) != 0, 1, 0)
        give = lax.dynamic_index_in_dim(held, 1 - mine, place, keepdims=False)
        kept = lax.dynamic_index_in_dim(held, mine, place, keepdims=False)
        got = lax.ppermute(give, axis, bit_pairs(size, bit))
        result = kept.astype(F32) + got.astype(F32)
        held = result.astype(BF)
        names.pop(place)
    return result


def dp_share(grad, axis, rank, size):
    cut = grad.shape[1] // 2
    return jnp.concatenate(
        [
            halving_sum(grad[:, :cut], axis, rank, size, 0),
            halving_sum(grad[:, cut:], axis, rank, size, 1),
        ],
        axis=1,
    ).astype(BF)


def body(
    inputs, cotangent, ln_gain, ln_bias, w_qkv, b_qkv, w_dense, b_dense, w_fc1, b_fc1, w_fc2, b_fc2
):
    core = lax.axis_index("pipe")
    rank = lax.axis_index("tensor")
    dp_size = lax.axis_size("dp")
    dp_rank = lax.axis_index("dp")
    first = core == 0
    _, length, width = inputs.shape
    lines = lax.axis_size("tensor")
    chunk = CHUNK
    chunks = length // chunk
    local = w_qkv.shape[3]
    hidden = w_fc1.shape[2]
    swap_pairs = [(0, 1), (1, 0)]

    def swap(value):
        return lax.ppermute(value, "pipe", swap_pairs)

    def both(own):
        other = swap(own)
        return (jnp.where(first, own, other), jnp.where(first, other, own))

    small = jnp.concatenate(
        [ln_gain[0], ln_bias[0], b_qkv[0].reshape(-1), b_dense[0], b_fc1[0], b_fc2[0]]
    )
    small_both = jnp.stack(both(small)).astype(F32)

    def cut_small():
        at = 0
        out = []
        for count in (width, width, 3 * local, width, hidden, width):
            out.append(small_both[:, at : at + count])
            at += count
        return out

    gains, shifts, bias3, bias_d, bias_u, bias_2 = cut_small()
    vectors = (gains, shifts, bias3.reshape(6, local), bias_u, bias_d + bias_2)
    tables = rotary_tables(length)
    own_w = (w_qkv[0], w_fc1[0], w_dense[0], w_fc2[0])
    results = forward_both(inputs, own_w, vectors, tables)
    other_w = results[:4]
    h, h_far, query, key, value, merged, merged_far, act, act_far, slope, logs, x1_full, part1 = results[4:]
    weights = [
        (jnp.where(first, a, b), jnp.where(first, b, a)) for a, b in zip(own_w, other_w)
    ]
    params = [(gains[l], shifts[l], None, None, vectors[4][l]) for l in range(2)]

    def rows_of(array, index):
        return array[index * chunk : (index + 1) * chunk]

    def normal(rows):
        values = rows.astype(F32)
        centre = values - jnp.mean(values, axis=-1, keepdims=True)
        spread = jnp.mean(centre * centre, axis=-1, keepdims=True)
        return centre * lax.rsqrt(spread + ln_eps)

    def in_pieces(array):
        step = array.shape[-1] // PIECES
        return [array[..., i * step : (i + 1) * step] for i in range(PIECES)]

    def scatter(part):
        blocks = part.reshape(lines, part.shape[0] // lines, width)
        return jnp.concatenate(
            [line_scatter_sum(piece, "tensor", rank) for piece in in_pieces(blocks)], axis=-1
        )

    def gather(share):
        full = jnp.concatenate(
            [line_gather(piece, "tensor", rank) for piece in in_pieces(share)], axis=-1
        )
        return full.reshape(lines * share.shape[0], width)

    def share_of(rows):
        size = rows.shape[0] // lines
        return lax.dynamic_slice_in_dim(rows, rank * size, size, 0)

    x0 = lax.dynamic_index_in_dim(inputs, core, 0, keepdims=False)
    cot = lax.dynamic_index_in_dim(cotangent, core, 0, keepdims=False)
    cot_other = lax.dynamic_index_in_dim(cotangent, 1 - core, 0, keepdims=False)
    x1 = [rows_of(x1_full, index) for index in range(chunks)]
    act0 = share_of(x1_full)
    act1 = (act0.astype(F32) + scatter(part1) + vectors[4][1]).astype(BF)

    def half_of(array, which):
        size = array.shape[-1] // 2
        return lax.dynamic_slice_in_dim(array, which * size, size, array.ndim - 1)

    def backward_chunk(layer, index, rows, upstream, carry):
        gain, shift, _, _, _ = params[layer]
        proj_w, up_w, dense_w, down_w = (pair[layer] for pair in weights)
        grad_merged = jnp.einsum(
            "ld,ed->le", upstream, dense_w, preferred_element_type=F32
        ).astype(BF)
        grad_act = jnp.einsum("ld,fd->lf", upstream, down_w, preferred_element_type=F32)
        grad_pre = (grad_act * rows_of(slope[layer], index).astype(F32)).astype(BF)
        dk_in, dv_in = carry if carry is not None else (None, None)
        grad_proj, dk_out, dv_out = attend_back(
            rows_of(query[layer], index),
            grad_merged,
            rows_of(merged[layer], index),
            logs[layer, :, :, index * chunk : (index + 1) * chunk],
            [rows_of(table, index) for table in tables],
            [rows_of(key[layer], i) for i in range(index + 1)],
            [rows_of(value[layer], i) for i in range(index + 1)],
            dk_in,
            dv_in,
        )
        grad_h = jnp.einsum(
            "cle,cde->ld", grad_proj, proj_w, preferred_element_type=F32
        ) + jnp.einsum("lf,df->ld", grad_pre, up_w, preferred_element_type=F32)
        gain_term = jnp.sum(grad_h * normal(rows), axis=0)
        shift_term = jnp.sum(grad_h, axis=0)
        return grad_h.astype(BF), grad_proj, grad_pre, gain_term, shift_term, (dk_out, dv_out)

    def norm_back(rows, grad_h, upstream, gain):
        values = rows.astype(F32)
        centre = values - jnp.mean(values, axis=-1, keepdims=True)
        inverse = lax.rsqrt(jnp.mean(centre * centre, axis=-1, keepdims=True) + ln_eps)
        xhat = centre * inverse
        e = grad_h * gain
        back = e - jnp.mean(e, axis=-1, keepdims=True) - xhat * jnp.mean(
            e * xhat, axis=-1, keepdims=True
        )
        return (upstream.astype(F32) + inverse * back).astype(BF)

    def backward(layer, rows_list, upstream_list, after):
        grad_projs, grad_pres = [None] * chunks, [None] * chunks
        gain_total = jnp.zeros((width,), F32)
        shift_total = jnp.zeros((width,), F32)
        carry = None
        for index in reversed(range(chunks)):
            grad_h, grad_projs[index], grad_pres[index], gain_term, shift_term, carry = (
                backward_chunk(layer, index, rows_list[index], upstream_list[index], carry)
            )
            gain_total = gain_total + gain_term
            shift_total = shift_total + shift_term
            after(index, grad_h)
        grad_proj = jnp.concatenate(grad_projs, axis=1)
        grad_pre = jnp.concatenate(grad_pres, axis=0)
        bias_terms = [
            jnp.sum(grad_proj, axis=1, dtype=F32),
            jnp.sum(grad_pre, axis=0, dtype=F32),
        ]
        return grad_proj, grad_pre, gain_total, shift_total, bias_terms

    def pair_dot(left, right):
        return sum(
            jnp.einsum("ld,lf->df", a, b, preferred_element_type=F32) for a, b in zip(left, right)
        ).astype(BF)

    def weight_share(left, right):
        return dp_share(pair_dot(left, right), "dp", dp_rank, dp_size)

    def exchange_half(array):
        return half_of(array, core), swap(half_of(array, 1 - core))

    def down_shares(layer, upstreams):
        act_pair = half_of(act[layer], core), act_far[layer]
        merged_pair = half_of(merged[layer], core), merged_far[layer]
        return weight_share(upstreams, act_pair), weight_share(upstreams, merged_pair)

    def up_shares(layer, grad_proj, grad_pre):
        h_pair = (h[layer], h_far[layer])
        pre_pair = exchange_half(grad_pre)
        proj_own, proj_other = exchange_half(grad_proj)
        side = proj_own.shape[2]

        def flat(three):
            return jnp.concatenate([three[0], three[1], three[2]], axis=1)

        up = weight_share(h_pair, pre_pair)
        proj = weight_share(h_pair, (flat(proj_own), flat(proj_other)))
        return up, proj, side

    down1 = down_shares(1, (cot, cot_other))
    dr1 = [None] * chunks
    dr1_full = [None] * chunks

    def after1(index, grad_h):
        upstream = rows_of(cot, index)
        total = scatter(grad_h)
        dr1[index] = norm_back(share_of(x1[index]), total, share_of(upstream), params[1][0])
        dr1_full[index] = gather(dr1[index])

    grad_proj1, grad_pre1, gain1, shift1, biases1 = backward(
        1, x1, [rows_of(cot, i) for i in range(chunks)], after1
    )
    up1 = up_shares(1, grad_proj1, grad_pre1)
    dy0 = jnp.concatenate(dr1_full, axis=0)
    down0 = down_shares(0, (dy0, swap(dy0)))
    grads_h0 = [None] * chunks

    def after0(index, grad_h):
        grads_h0[index] = grad_h

    grad_proj0, grad_pre0, gain0, shift0, biases0 = backward(
        0, [rows_of(x0, i) for i in range(chunks)], dr1_full, after0
    )
    total0 = scatter(jnp.concatenate(grads_h0, axis=0))
    dr0_share = norm_back(share_of(x0), total0, share_of(dy0), params[0][0])
    dr1_share = share_of(dy0)
    up0 = up_shares(0, grad_proj0, grad_pre0)

    def to_owner(value0, value1):
        from1 = lax.ppermute(value0, "pipe", [(1, 0)])
        from0 = lax.ppermute(value1, "pipe", [(0, 1)])
        return jnp.where(first, value0, value1), jnp.where(first, from1, from0)

    def in_order(own, other, axis):
        return jnp.where(
            first,
            jnp.concatenate([own, other], axis=axis),
            jnp.concatenate([other, own], axis=axis),
        )

    def assembled(value0, value1, axis):
        own, other = to_owner(value0, value1)
        return in_order(own.astype(F32), other.astype(F32), axis)

    def stacked(value0, value1):
        own, other = to_owner(value0, value1)
        return in_order(own[None], other[None], 0)

    acts = stacked(act0, act1)
    grads_in = stacked(dr0_share, dr1_share)
    out_fc2 = assembled(down0[0], down1[0], 1).T
    out_dense = assembled(down0[1], down1[1], 1).T
    out_fc1 = assembled(up0[0], up1[0], 1)
    side = up0[2]
    rows_dp = up0[1].shape[0]

    def split3(value):
        return value.reshape(rows_dp, 3, side)

    out_qkv = jnp.transpose(assembled(split3(up0[1]), split3(up1[1]), 2), (1, 0, 2))

    def vector(layer, gain, shift, biases, upstream):
        out_bias = jnp.sum(upstream, axis=0, dtype=F32)
        return jnp.concatenate(
            [gain, shift, biases[0].reshape(-1), biases[1], out_bias]
        ).reshape(-1, LANES)

    def butterfly(value, axis, size):
        bit = 1
        while bit < size:
            value = value + lax.ppermute(value, axis, bit_pairs(size, bit))
            bit *= 2
        return value

    def small_sums(packed):
        packed = butterfly(butterfly(packed, "pipe", 2), "dp", dp_size)
        cut = 2 * width // LANES
        norm = butterfly(packed[:cut], "tensor", lines)
        return norm.reshape(-1), packed[cut:].reshape(-1)

    norm1, rest1 = small_sums(vector(1, gain1, shift1, biases1, cot))
    norm0, rest0 = small_sums(vector(0, gain0, shift0, biases0, dy0))
    norm = jnp.where(first, norm0, norm1)
    rest = jnp.where(first, rest0, rest1)
    place = rank * dp_size + dp_rank
    norm_size = width // (lines * dp_size)

    def piece(vec, offset, size):
        return lax.dynamic_slice_in_dim(vec, offset, size, 0)

    out_gain = piece(norm, place * norm_size, norm_size)
    out_shift = piece(norm, width + place * norm_size, norm_size)
    bias_size = local // dp_size
    out_bqkv = lax.dynamic_slice_in_dim(
        rest[: 3 * local].reshape(3, local), dp_rank * bias_size, bias_size, 1
    )
    up_size = hidden // dp_size
    out_bfc1 = piece(rest, 3 * local + dp_rank * up_size, up_size)
    out_size = width // dp_size
    out_bout = piece(rest, 3 * local + hidden + dp_rank * out_size, out_size)
    return (
        acts[None],
        grads_in[None],
        out_gain[None],
        out_shift[None],
        out_qkv[None],
        out_bqkv[None],
        out_dense[None],
        out_bout[None],
        out_fc1[None],
        out_bfc1[None],
        out_fc2[None],
        out_bout[None],
    )


def solution(mesh):
    in_specs = (
        P("dp", None, None),
        P("dp", None, None),
        P("pipe", None),
        P("pipe", None),
        P("pipe", None, None, "tensor"),
        P("pipe", None, "tensor"),
        P("pipe", "tensor", None),
        P("pipe", None),
        P("pipe", None, "tensor"),
        P("pipe", "tensor"),
        P("pipe", "tensor", None),
        P("pipe", None),
    )
    out_specs = (
        P("pipe", "dp", "tensor", None),
        P("pipe", "dp", "tensor", None),
        P("pipe", ("tensor", "dp")),
        P("pipe", ("tensor", "dp")),
        P("pipe", None, "dp", "tensor"),
        P("pipe", None, ("tensor", "dp")),
        P("pipe", "tensor", "dp"),
        P("pipe", "dp"),
        P("pipe", "dp", "tensor"),
        P("pipe", ("tensor", "dp")),
        P("pipe", "tensor", "dp"),
        P("pipe", "dp"),
    )
    return jax.shard_map(body, mesh=mesh, in_specs=in_specs, out_specs=out_specs, check_vma=False)
```

```python
import functools

import jax
import jax.numpy as jnp
from jax import lax
from jax.experimental import pallas as pl
from jax.experimental.pallas import tpu as pltpu
from jax.sharding import PartitionSpec as P

HEAD_DIM = 64
ROT = 32
LANES = 128
MIB = 1024 * 1024

ln_eps = 1e-05
rope_base = 10000.0
gelu_coef = 0.7978845608028654
masked_score = -1e30

BF = jnp.bfloat16
F32 = jnp.float32


def rotary_tables(length):
    half_rot = ROT // 2
    inverse = rope_base ** (-(jnp.arange(half_rot, dtype=F32) * 2.0 / ROT))
    angles = jnp.arange(length, dtype=F32)[:, None] * inverse[None, :]
    cosines, sines = jnp.cos(angles), jnp.sin(angles)
    rest = HEAD_DIM - ROT
    blank = jnp.zeros((length, half_rot), F32)
    tail = jnp.zeros((length, rest), F32)
    cos_head = jnp.concatenate([cosines, cosines, jnp.ones((length, rest), F32)], axis=1)
    near_head = jnp.concatenate([-sines, blank, tail], axis=1)
    far_head = jnp.concatenate([blank, sines, tail], axis=1)
    pair = LANES // HEAD_DIM
    return tuple(jnp.tile(part, (1, pair)) for part in (cos_head, near_head, far_head))


def turn(values, cos, near, far):
    half_rot = ROT // 2
    return (
        values * cos
        + pltpu.roll(values, LANES - half_rot, 1) * near
        + pltpu.roll(values, half_rot, 1) * far
    )


def head_mask(rows, which):
    lanes = lax.broadcasted_iota(jnp.int32, (rows, LANES), 1)
    return (lanes // HEAD_DIM) == which


def as_row(column):
    return jnp.transpose(jnp.broadcast_to(column, (column.shape[0], LANES)))[0:1, :]


def dot_nt(left, right):
    return lax.dot_general(left, right, (((1,), (1,)), ((), ())), preferred_element_type=F32)


def dot_nn(left, right):
    return lax.dot_general(left, right, (((1,), (0,)), ((), ())), preferred_element_type=F32)


def dot_tn(left, right):
    return lax.dot_general(left, right, (((0,), (0,)), ((), ())), preferred_element_type=F32)


LINE = 4
STEPS = 2 * LINE
TILE = 512


def remote(src, dst, send, recv, axis, index):
    return pltpu.make_async_remote_copy(
        src_ref=src,
        dst_ref=dst,
        send_sem=send,
        recv_sem=recv,
        device_id={axis: index},
        device_id_type=pl.DeviceIdType.MESH,
    )


def greet(core, rank):
    barrier = pltpu.get_barrier_semaphore()

    def tell(axis, index):
        pl.semaphore_signal(
            barrier, inc=1, device_id={axis: index}, device_id_type=pl.DeviceIdType.MESH
        )

    tell("pipe", 1 - core)

    @pl.when(rank > 0)
    def _():
        tell("tensor", rank - 1)

    @pl.when(rank < LINE - 1)
    def _():
        tell("tensor", rank + 1)

    ends = jnp.where(rank > 0, 1, 0) + jnp.where(rank < LINE - 1, 1, 0)
    pl.semaphore_wait(barrier, 1 + ends)


def fetch_weight(layer, core, own, other, target, sem, arrival):
    @pl.when(core == layer)
    def _():
        pltpu.make_async_copy(own, target, sem).start()

    @pl.when(core != layer)
    def _():
        if arrival is not None:
            arrival.wait_recv()
        pltpu.make_async_copy(other, target, sem).start()


class LineSum:
    def __init__(self, rank, part, first, beside, second, last, result, sems, finish):
        self.rank, self.part, self.result, self.finish = rank, part, result, finish
        self.first, self.beside, self.second, self.last = first, beside, second, last
        self.sems = sems
        self.rows = part.shape[1]
        self.block = self.rows // LINE
        half = 2 * self.block
        self.left = rank < 2
        self.far = pl.multiple_of(jnp.where(self.left, half, 0), half)
        self.near = pl.multiple_of(jnp.where(self.left, 0, half), half)
        self.own = pl.multiple_of(rank * self.block, self.block)
        self.inner = (rank == 1) | (rank == 2)
        self.outer = (rank == 0) | (rank == 3)
        self.inward = jnp.where(self.left, 1, 2)
        self.outward = jnp.where(self.left, 0, 3)
        self.across = jnp.where(self.left, 2, 1)
        self.spare = pl.multiple_of(jnp.where(self.left, self.block, half), self.block)
        self.out_half = pl.multiple_of(jnp.where(self.left, 0, self.block), self.block)
        self.in_half = pl.multiple_of(jnp.where(self.left, self.block, 0), self.block)

    def hop(self, name, chunk, src, dst, to):
        return remote(src, dst, self.sems[name].at[0, chunk], self.sems[name].at[1, chunk], "tensor", to)

    def copies(self, chunk):
        half = 2 * self.block
        hop_first = self.hop(
            "first", chunk, self.part.at[chunk, pl.ds(self.far, half)], self.first.at[chunk], self.inward
        )
        hop_beside = self.hop(
            "beside",
            chunk,
            self.part.at[chunk, pl.ds(self.spare, self.block)],
            self.beside.at[chunk],
            self.inward,
        )
        hop_second = self.hop(
            "second", chunk, self.first.at[chunk], self.second.at[chunk], self.across
        )
        hop_last = self.hop(
            "last",
            chunk,
            self.second.at[chunk, pl.ds(self.out_half, self.block)],
            self.last.at[chunk],
            self.outward,
        )
        return hop_first, hop_beside, hop_second, hop_last

    def result_rows(self, chunk, shard):
        start = pl.multiple_of(chunk * self.rows + shard * self.block, self.block)
        return self.result.at[pl.ds(start, self.block)]

    def move(self, way, chunk, hop):
        step = 1 - 2 * way
        shard = jnp.clip(self.rank - step * hop, 0, LINE - 1)
        rows = self.result_rows(chunk, shard)
        name = "up" if way == 0 else "down"
        to = jnp.clip(self.rank + step, 0, LINE - 1)
        index = chunk * (LINE - 1) + hop
        return remote(rows, rows, self.sems[name].at[0, index], self.sems[name].at[1, index], "tensor", to)

    def stage_a(self, chunk):
        @pl.when(self.outer)
        def _():
            hop_first, hop_beside, _, _ = self.copies(chunk)
            hop_first.start()
            hop_beside.start()

    def stage_b(self, chunk):
        @pl.when(self.inner)
        def _():
            hop_first, _, hop_second, _ = self.copies(chunk)
            hop_first.wait_recv()
            self.first[chunk] = (
                self.first[chunk].astype(F32)
                + self.part[chunk, pl.ds(self.far, 2 * self.block)].astype(F32)
            ).astype(BF)
            hop_second.start()

    def stage_c(self, chunk):
        @pl.when(self.inner)
        def _():
            _, hop_beside, hop_second, hop_last = self.copies(chunk)
            hop_second.wait_recv()
            out_rows = pl.ds(self.out_half, self.block)
            near_out = pl.ds(pl.multiple_of(self.near + self.out_half, self.block), self.block)
            self.second[chunk, out_rows] = (
                self.second[chunk, out_rows].astype(F32) + self.part[chunk, near_out].astype(F32)
            ).astype(BF)
            hop_last.start()
            hop_beside.wait_recv()
            total = (
                self.second[chunk, pl.ds(self.in_half, self.block)].astype(F32)
                + self.beside[chunk].astype(F32)
                + self.part[chunk, pl.ds(self.own, self.block)].astype(F32)
            )
            self.finish(chunk, total, self.result_rows(chunk, self.rank))
            self.move(0, chunk, 0).start()
            self.move(1, chunk, 0).start()

    def stage_d(self, chunk):
        @pl.when(self.outer)
        def _():
            _, _, _, hop_last = self.copies(chunk)
            hop_last.wait_recv()
            total = self.last[chunk].astype(F32) + self.part[
                chunk, pl.ds(self.own, self.block)
            ].astype(F32)
            self.finish(chunk, total, self.result_rows(chunk, self.rank))

        @pl.when(self.rank == 0)
        def _():
            self.move(0, chunk, 0).start()

        @pl.when(self.rank == 3)
        def _():
            self.move(1, chunk, 0).start()

    def stage_e(self, chunk, hop):
        for way in range(2):
            behind = self.rank if way == 0 else LINE - 1 - self.rank

            @pl.when(self.inner & (behind > hop))
            def _():
                self.arrival(way, chunk, hop).wait_recv()
                self.move(way, chunk, hop + 1).start()

    def arrival(self, way, chunk, hop):
        step = 1 - 2 * way
        shard = jnp.clip(self.rank - step * (hop + 1), 0, LINE - 1)
        rows = self.result_rows(chunk, shard)
        name = "up" if way == 0 else "down"
        to = jnp.clip(self.rank + step, 0, LINE - 1)
        index = chunk * (LINE - 1) + hop
        return remote(rows, rows, self.sems[name].at[0, index], self.sems[name].at[1, index], "tensor", to)

    def stage_f(self, chunk):
        @pl.when(self.rank == 0)
        def _():
            for hop in range(LINE - 1):
                self.arrival(1, chunk, hop).wait_recv()

        @pl.when(self.rank == 3)
        def _():
            for hop in range(LINE - 1):
                self.arrival(0, chunk, hop).wait_recv()

    def sent_part(self, chunk):
        @pl.when(self.outer)
        def _():
            hop_first, hop_beside, _, _ = self.copies(chunk)
            hop_first.wait_send()
            hop_beside.wait_send()

    def sent_rest(self, chunk):
        @pl.when(self.inner)
        def _():
            _, _, hop_second, hop_last = self.copies(chunk)
            hop_second.wait_send()
            hop_last.wait_send()

        for way in range(2):
            behind = self.rank if way == 0 else LINE - 1 - self.rank
            ahead = LINE - 1 - behind
            for hop in range(LINE - 1):

                @pl.when((ahead > 0) & (behind >= hop))
                def _():
                    self.move(way, chunk, hop).wait_send()


def line_sum_scratch(rows, cols):
    block = rows // LINE
    return [
        pltpu.VMEM((LINE, 2 * block, cols), BF),
        pltpu.VMEM((LINE, block, cols), BF),
        pltpu.VMEM((LINE, 2 * block, cols), BF),
        pltpu.VMEM((LINE, block, cols), BF),
    ] + [pltpu.SemaphoreType.DMA((2, LINE))] * 4 + [
        pltpu.SemaphoreType.DMA((2, LINE * (LINE - 1)))
    ] * 2


SUM_NAMES = ("first", "beside", "second", "last", "up", "down")


def forward_kernel(*refs):
    at = 0

    def take(count):
        nonlocal at
        at += count
        return refs[at - count : at]

    (inputs_ref,) = take(1)
    own_w = take(4)
    gain_ref, shift_ref, bias3_ref, bias_u_ref, bias_o_ref = take(5)
    cos_ref, near_ref, far_ref = take(3)
    other_w = take(4)
    h_out, h_far, q_out, k_out, v_out, o_out, o_near, o_far = take(8)
    act_near, act_far, slope_out, logs_out, x1_out, part_out = take(6)
    vmem_w = take(4)
    x_buf, x_share, h_buf, act_buf, slope_buf, q_buf, o_buf, k_all, v_all, logs_buf = take(10)
    part, x1 = take(2)
    sum_bufs = take(4)
    sum_sems = dict(zip(SUM_NAMES, take(6)))
    w_sems, fetch_sems, x_sems, out_sems, slot4_sems, far_send, far_recv, once_sems = take(8)
    assert at == len(refs)
    core = lax.axis_index("pipe")
    rank = lax.axis_index("tensor")
    rows = x_buf.shape[1]
    width = x_buf.shape[2]
    local = q_buf.shape[2]
    hidden = act_buf.shape[2]
    half_hidden = hidden // 2
    half_local = local // 2
    tile = min(TILE, width)
    scale = HEAD_DIM ** (-0.5)

    weight_moves = [
        remote(own, other, w_sems.at[0, i], w_sems.at[1, i], "pipe", 1 - core)
        for i, (own, other) in enumerate(zip(own_w, other_w))
    ]

    def fetch(layer, i):
        fetch_weight(
            layer, core, own_w[i], other_w[i], vmem_w[i], fetch_sems.at[i], weight_moves[i]
        )

    def fetched(i):
        pltpu.make_async_copy(own_w[i], vmem_w[i], fetch_sems.at[i]).wait()

    def chunk_rows(chunk):
        return pl.ds(pl.multiple_of(chunk * rows, rows), rows)

    def x_copy(chunk):
        slot = lax.rem(chunk, 2)
        return pltpu.make_async_copy(
            inputs_ref.at[core, chunk_rows(chunk)], x_buf.at[slot], x_sems.at[slot]
        )

    def finish(chunk, total, target):
        value = total + x_share[chunk].astype(F32) + bias_o_ref[0:1, :]
        target[...] = value.astype(BF)

    summed = LineSum(rank, part, *sum_bufs, x1, sum_sems, finish)

    def outward(step):
        layer, chunk = lax.div(step, LINE), lax.rem(step, LINE)
        slot = lax.rem(step, 2)
        at_rows = chunk_rows(chunk)
        theirs = 1 - core

        def half(which, size):
            return pl.ds(pl.multiple_of(which * size, size), size)

        here = [
            pltpu.make_async_copy(src, dst, out_sems.at[i, slot])
            for i, (src, dst) in enumerate(
                (
                    (h_buf.at[slot], h_out.at[layer, at_rows]),
                    (q_buf.at[slot], q_out.at[layer, at_rows]),
                    (o_buf.at[slot], o_out.at[layer, at_rows]),
                    (act_buf.at[slot, :, half(core, half_hidden)], act_near.at[layer, at_rows]),
                    (slope_buf.at[slot], slope_out.at[layer, at_rows]),
                    (logs_buf.at[slot], logs_out.at[layer, :, :, at_rows]),
                    (o_buf.at[slot, :, half(core, half_local)], o_near.at[layer, at_rows]),
                )
            )
        ]
        act_cols, o_cols = half(theirs, half_hidden), half(theirs, half_local)
        there = [
            remote(
                h_buf.at[slot], h_far.at[layer, at_rows], far_send.at[0, slot], far_recv.at[0], "pipe", theirs
            ),
            remote(
                o_buf.at[slot, :, o_cols],
                o_far.at[layer, at_rows],
                far_send.at[1, slot],
                far_recv.at[1],
                "pipe",
                theirs,
            ),
            remote(
                act_buf.at[slot, :, act_cols],
                act_far.at[layer, at_rows],
                far_send.at[2, slot],
                far_recv.at[2],
                "pipe",
                theirs,
            ),
        ]
        return here, there

    def kv_copies(step):
        layer, chunk = lax.div(step, LINE), lax.rem(step, LINE)
        at_rows = chunk_rows(chunk)
        return [
            pltpu.make_async_copy(k_all.at[at_rows], k_out.at[layer, at_rows], slot4_sems.at[0, chunk]),
            pltpu.make_async_copy(v_all.at[at_rows], v_out.at[layer, at_rows], slot4_sems.at[1, chunk]),
        ]

    def x1_copy(chunk):
        at_rows = chunk_rows(chunk)
        return pltpu.make_async_copy(x1.at[at_rows], x1_out.at[at_rows], once_sems.at[0, chunk])

    def part_copy(chunk):
        at_rows = chunk_rows(chunk)
        return pltpu.make_async_copy(part.at[chunk], part_out.at[at_rows], once_sems.at[1, chunk])

    x_copy(0).start()
    greet(core, rank)
    for move in weight_moves:
        move.start()
    x_copy(1).start()

    keep = lax.broadcasted_iota(jnp.int32, (rows, rows), 1) <= lax.broadcasted_iota(
        jnp.int32, (rows, rows), 0
    )

    def attention(chunk, slot):
        def pair(j, _):
            lanes = pl.ds(pl.multiple_of(j * LANES, LANES), LANES)
            query = q_buf[slot, :, lanes]
            outs = []
            for which in range(LANES // HEAD_DIM):
                mask = head_mask(rows, which)
                mine = jnp.where(mask, query, jnp.zeros_like(query))
                scores = []
                if chunk:
                    scores.append(dot_nt(mine, k_all[0 : chunk * rows, lanes]))
                scores.append(
                    jnp.where(keep, dot_nt(mine, k_all[chunk * rows : (chunk + 1) * rows, lanes]), masked_score)
                )
                top = functools.reduce(
                    jnp.maximum, [jnp.max(item, axis=1, keepdims=True) for item in scores]
                )
                weights = [jnp.exp(item - top) for item in scores]
                total = functools.reduce(
                    jnp.add, [jnp.sum(item, axis=1, keepdims=True) for item in weights]
                )
                values = []
                if chunk:
                    values.append(v_all[0 : chunk * rows, lanes])
                values.append(v_all[chunk * rows : (chunk + 1) * rows, lanes])
                merged = functools.reduce(
                    jnp.add, [dot_nn(w.astype(BF), v) for w, v in zip(weights, values)]
                )
                outs.append(merged / total)
                logs_buf[slot, j, which : which + 1, :] = as_row(top + jnp.log(total))
            o_buf[slot, :, lanes] = jnp.where(head_mask(rows, 0), outs[0], outs[1]).astype(BF)
            return 0

        lax.fori_loop(0, local // LANES, pair, 0)

    def step_body(step, _):
        layer, chunk = lax.div(step, LINE), lax.rem(step, LINE)
        slot = lax.rem(step, 2)
        at_rows = chunk_rows(chunk)
        here, there = outward(step)
        kv = kv_copies(step)
        starting = chunk == 0
        ending = step == LINE - 1

        @pl.when(step >= 2)
        def _():
            old_here, old_there = outward(step - 2)
            for item in old_here:
                item.wait()
            for item in old_there:
                item.wait_send()

        small = rows // 8
        gain, shift = gain_ref[pl.ds(layer, 1), :], shift_ref[pl.ds(layer, 1), :]

        def normalise(load):
            def some(i, _):
                span = pl.ds(pl.multiple_of(i * small, small), small)
                values = load(span).astype(F32)
                centre = values - jnp.mean(values, axis=-1, keepdims=True)
                spread = jnp.mean(centre * centre, axis=-1, keepdims=True)
                h_buf[slot, span, :] = (centre * lax.rsqrt(spread + ln_eps) * gain + shift).astype(BF)
                return 0

            lax.fori_loop(0, 8, some, 0)

        @pl.when(step == 0)
        def _():
            fetch(0, 0)

        @pl.when(layer == 0)
        def _():
            x_copy(chunk).wait()
            x_share[chunk] = x_buf[slot, pl.ds(pl.multiple_of(rank * (rows // LINE), rows // LINE), rows // LINE)]
            normalise(lambda span: x_buf[slot, span, :])

            @pl.when(step + 2 < LINE)
            def _():
                x_copy(chunk + 2).start()

        @pl.when(layer == 1)
        def _():
            summed.stage_f(chunk)
            x1_copy(chunk).start()
            base = chunk * rows
            normalise(lambda span: x1[pl.ds(pl.multiple_of(base + span.start, small), small), :])

        here[0].start()
        there[0].start()

        @pl.when(starting)
        def _():
            fetched(0)

        @pl.when(layer == 1)
        def _():
            for item in kv_copies(step - LINE):
                item.wait()

        tables = (cos_ref[at_rows, :], near_ref[at_rows, :], far_ref[at_rows, :])
        h = h_buf[slot]
        for part3 in range(3):
            value = dot_nn(h, vmem_w[0][part3]) + bias3_ref[pl.ds(layer * 3 + part3, 1), :]
            for j in range(local // LANES):
                lanes = slice(j * LANES, (j + 1) * LANES)
                if part3 == 0:
                    q_buf[slot, :, lanes] = (turn(value[:, lanes], *tables) * scale).astype(BF)
                elif part3 == 1:
                    k_all[at_rows, lanes] = turn(value[:, lanes], *tables).astype(BF)
                else:
                    v_all[at_rows, lanes] = value[:, lanes].astype(BF)
        here[1].start()
        for item in kv:
            item.start()

        @pl.when(ending)
        def _():
            fetch(1, 0)

        @pl.when(step == 0)
        def _():
            fetch(0, 1)

        for index in range(LINE):

            @pl.when(chunk == index)
            def _():
                attention(index, slot)

        here[2].start()
        here[5].start()
        here[6].start()
        there[1].start()

        @pl.when(step == 0)
        def _():
            fetch(0, 2)
            fetch(0, 3)

        @pl.when((step >= 1) & (step <= LINE))
        def _():
            summed.stage_b(step - 1)

        @pl.when((step >= 2) & (step <= LINE + 1))
        def _():
            summed.stage_d(step - 2)

        @pl.when((step >= 3) & (step <= LINE + 2))
        def _():
            summed.stage_e(step - 3, 1)

        @pl.when(starting)
        def _():
            fetched(1)

        def up(i, _):
            cols = pl.ds(pl.multiple_of(i * tile, tile), tile)
            u = dot_nn(h_buf[slot], vmem_w[1][:, cols]) + bias_u_ref[pl.ds(layer, 1), cols]
            square = u * u
            inner = jnp.tanh(gelu_coef * u * (1.0 + 0.044715 * square))
            act_buf[slot, :, cols] = (0.5 * u * (1.0 + inner)).astype(BF)
            slope_buf[slot, :, cols] = (
                0.5 * (1.0 + inner)
                + (0.5 * gelu_coef) * u * (1.0 - inner * inner) * (1.0 + 3.0 * 0.044715 * square)
            ).astype(BF)
            return 0

        lax.fori_loop(0, hidden // tile, up, 0)
        here[3].start()
        here[4].start()
        there[2].start()

        @pl.when(ending)
        def _():
            fetch(1, 1)

        @pl.when(starting)
        def _():
            fetched(2)
            fetched(3)

        @pl.when(layer == 1)
        def _():
            summed.sent_part(chunk)

        def down(i, _):
            cols = pl.ds(pl.multiple_of(i * tile, tile), tile)
            part[chunk, :, cols] = (
                dot_nn(o_buf[slot], vmem_w[2][:, cols]) + dot_nn(act_buf[slot], vmem_w[3][:, cols])
            ).astype(BF)
            return 0

        lax.fori_loop(0, width // tile, down, 0)

        @pl.when(ending)
        def _():
            fetch(1, 2)
            fetch(1, 3)

        @pl.when(layer == 0)
        def _():
            summed.stage_a(chunk)

        @pl.when(layer == 1)
        def _():
            part_copy(chunk).start()

        @pl.when((step >= 1) & (step <= LINE))
        def _():
            summed.stage_c(step - 1)

        @pl.when((step >= 2) & (step <= LINE + 1))
        def _():
            summed.stage_e(step - 2, 0)

        return 0

    lax.fori_loop(0, STEPS, step_body, 0)

    for step in (STEPS - 2, STEPS - 1):
        old_here, old_there = outward(step)
        for item in old_here:
            item.wait()
        for item in old_there:
            item.wait_send()
    for chunk in range(LINE):
        for item in kv_copies(LINE + chunk):
            item.wait()
        x1_copy(chunk).wait()
        part_copy(chunk).wait()
        summed.sent_rest(chunk)
    for move in weight_moves:
        move.wait_send()
    for i, ref in enumerate((h_far, o_far, act_far)):
        remote(ref, ref, far_send.at[i, 0], far_recv.at[i], "pipe", 1 - core).wait_recv()


def forward_both(inputs, weights, vectors, tables):
    _, length, width = inputs.shape
    w_qkv, w_fc1, w_dense, w_fc2 = weights
    local, hidden = w_dense.shape[0], w_fc1.shape[1]
    rows = length // LINE
    pairs = local // LANES

    def bf(*shape):
        return jax.ShapeDtypeStruct(shape, BF)

    out_shape = [bf(*w.shape) for w in weights] + [
        bf(2, length, width),
        bf(2, length, width),
        bf(2, length, local),
        bf(2, length, local),
        bf(2, length, local),
        bf(2, length, local),
        bf(2, length, local // 2),
        bf(2, length, local // 2),
        bf(2, length, hidden // 2),
        bf(2, length, hidden // 2),
        bf(2, length, hidden),
        jax.ShapeDtypeStruct((2, pairs, 8, length), F32),
        bf(length, width),
        bf(length, width),
    ]
    whole = pl.BlockSpec(memory_space=pltpu.VMEM)
    away = pl.BlockSpec(memory_space=pl.ANY)
    dma = pltpu.SemaphoreType.DMA
    return pl.pallas_call(
        forward_kernel,
        name="forward_both",
        in_specs=[away] * 5 + [whole] * 8,
        out_specs=[away] * len(out_shape),
        out_shape=out_shape,
        scratch_shapes=[pltpu.VMEM(w.shape, BF) for w in weights]
        + [
            pltpu.VMEM((2, rows, width), BF),
            pltpu.VMEM((LINE, rows // LINE, width), BF),
            pltpu.VMEM((2, rows, width), BF),
            pltpu.VMEM((2, rows, hidden), BF),
            pltpu.VMEM((2, rows, hidden), BF),
            pltpu.VMEM((2, rows, local), BF),
            pltpu.VMEM((2, rows, local), BF),
            pltpu.VMEM((length, local), BF),
            pltpu.VMEM((length, local), BF),
            pltpu.VMEM((2, pairs, 8, rows), F32),
            pltpu.VMEM((LINE, rows, width), BF),
            pltpu.VMEM((length, width), BF),
        ]
        + line_sum_scratch(rows, width)
        + [
            dma((2, 4)),
            dma((4,)),
            dma((2,)),
            dma((7, 2)),
            dma((2, LINE)),
            dma((3, 2)),
            dma((3,)),
            dma((2, LINE)),
        ],
        compiler_params=pltpu.CompilerParams(
            collective_id=0, has_side_effects=True, vmem_limit_bytes=62 * MIB
        ),
        cost_estimate=pl.CostEstimate(
            flops=4 * length * width * (4 * local + 2 * hidden),
            bytes_accessed=200 * MIB,
            transcendentals=0,
        ),
    )(inputs, *weights, *vectors, *tables)


class LineShare:
    def __init__(self, rank, part, from_left, from_right, sems, pieces):
        self.rank, self.part, self.pieces = rank, part, pieces
        self.bufs = (from_left, from_right)
        self.sems = sems
        self.cols = part.shape[2] // pieces

    def span(self, piece):
        return pl.ds(pl.multiple_of(piece * self.cols, self.cols), self.cols)

    def copy(self, way, chunk, piece, own):
        step = 1 - 2 * way
        src = (self.part if own else self.bufs[way]).at[chunk, :, self.span(piece)]
        index = chunk * self.pieces + piece
        to = jnp.clip(self.rank + step, 0, LINE - 1)
        return remote(
            src,
            self.bufs[way].at[chunk, :, self.span(piece)],
            self.sems[way].at[0, index],
            self.sems[way].at[1, index],
            "tensor",
            to,
        )

    def emit(self, chunk, piece):
        @pl.when((self.rank == 0) & (chunk > 0))
        def _():
            self.copy(0, chunk, piece, True).start()

        @pl.when((self.rank == LINE - 1) & (chunk < LINE - 1))
        def _():
            self.copy(1, chunk, piece, True).start()

    def relay(self, chunk, hop):
        for way in range(2):
            at = hop if way == 0 else LINE - 1 - hop
            further = (chunk > at) if way == 0 else (chunk < at)

            @pl.when((self.rank == at) & further)
            def _():
                def one(piece, _):
                    copy = self.copy(way, chunk, piece, False)
                    copy.wait_recv()
                    span = self.span(piece)
                    self.bufs[way][chunk, :, span] = (
                        self.bufs[way][chunk, :, span].astype(F32)
                        + self.part[chunk, :, span].astype(F32)
                    ).astype(BF)
                    copy.start()
                    return 0

                lax.fori_loop(0, self.pieces, one, 0)

    def arrived(self, chunk):
        for way in range(2):
            behind = chunk > 0 if way == 0 else chunk < LINE - 1

            @pl.when(behind)
            def _():
                def one(piece, _):
                    self.copy(way, chunk, piece, False).wait_recv()
                    return 0

                lax.fori_loop(0, self.pieces, one, 0)

    def sent(self, chunk):
        for way in range(2):
            end = 0 if way == 0 else LINE - 1
            for hop in range(LINE - 1):
                at = hop if way == 0 else LINE - 1 - hop
                further = (chunk > at) if way == 0 else (chunk < at)

                @pl.when((self.rank == at) & further)
                def _():
                    def one(piece, _):
                        self.copy(way, chunk, piece, at == end).wait_send()
                        return 0

                    lax.fori_loop(0, self.pieces, one, 0)


class PairDots:
    def __init__(self, core, dp_rank, dp_size, left_buf, right_buf, out_buf, sems, stages, received):
        self.core, self.me, self.dp = core, dp_rank, dp_size
        self.left_buf, self.right_buf, self.out_buf = left_buf, right_buf, out_buf
        self.left_sems, self.right_sems, self.out_sems, self.send_sems, self.recv_sems = sems
        self.stages, self.received = stages, received
        self.tokens = left_buf.shape[1] // 2
        self.keep = left_buf.shape[2]
        self.unit = right_buf.shape[2]
        self.groups = {}

    def add(self, index, layer, kind, left, rights):
        counts = [near.shape[-1] // self.unit for near, _ in rights]
        self.groups[index] = (layer, kind, left, rights, counts, sum(counts))

    def units(self, index):
        return self.groups[index][5] * self.dp

    def tile(self, order):
        return lax.rem(self.me + 1 + order, self.dp)

    def left_copies(self, index, order):
        _, _, (near, far), _, _, _ = self.groups[index]
        slot = lax.rem(order, 2)
        cols = pl.ds(pl.multiple_of(self.tile(order) * self.keep, self.keep), self.keep)
        return [
            pltpu.make_async_copy(
                src.at[:, cols],
                self.left_buf.at[slot, pl.ds(i * self.tokens, self.tokens)],
                self.left_sems.at[i, slot],
            )
            for i, src in enumerate((near, far))
        ]

    def right_copies(self, segment, col, slot):
        cols = pl.ds(pl.multiple_of(col * self.unit, self.unit), self.unit)
        return [
            pltpu.make_async_copy(
                src.at[:, cols],
                self.right_buf.at[slot, pl.ds(i * self.tokens, self.tokens)],
                self.right_sems.at[i, slot],
            )
            for i, src in enumerate(segment)
        ]

    def start_right(self, index, unit):
        _, _, _, rights, counts, total = self.groups[index]
        place, slot = lax.rem(unit, total), lax.rem(unit, 2)
        base = 0
        for segment, count in zip(rights, counts):

            @pl.when((place >= base) & (place < base + count))
            def _():
                for item in self.right_copies(segment, place - base, slot):
                    item.start()

            base += count

    def prime(self, index):
        zero = jnp.int32(0)
        for item in self.left_copies(index, zero):
            item.start()
        self.start_right(index, zero)

    def out_copy(self, index, unit):
        layer, kind, _, _, _, total = self.groups[index]
        order, place, slot = lax.div(unit, total), lax.rem(unit, total), lax.rem(unit, 2)
        span = pl.ds(pl.multiple_of(place * self.unit, self.unit), self.unit)
        stage = self.stages[kind].at[layer, self.tile(order)]
        if kind:
            return pltpu.make_async_copy(
                self.out_buf.at[slot, 0 : self.keep, 0 : self.unit], stage.at[:, span], self.out_sems.at[slot]
            )
        return pltpu.make_async_copy(
            self.out_buf.at[slot, 0 : self.unit, 0 : self.keep], stage.at[span], self.out_sems.at[slot]
        )

    def send(self, index, order, act):
        layer, kind, _, _, _, _ = self.groups[index]
        tile = self.tile(order)
        src = self.stages[kind].at[layer, tile]
        dst = self.received[kind].at[self.core, self.me]
        at_home = (self.core == layer) & (tile == self.me)

        @pl.when(at_home)
        def _():
            copy = pltpu.make_async_copy(src, dst, self.send_sems.at[index, order])
            copy.start() if act == "start" else copy.wait()

        @pl.when(jnp.logical_not(at_home))
        def _():
            copy = pltpu.make_async_remote_copy(
                src_ref=src,
                dst_ref=dst,
                send_sem=self.send_sems.at[index, order],
                recv_sem=self.recv_sems.at[kind, self.core],
                device_id={"pipe": jnp.int32(layer), "dp": tile},
                device_id_type=pl.DeviceIdType.MESH,
            )
            copy.start() if act == "start" else copy.wait_send()

    def run(self, index, start, stop):
        _, kind, _, _, _, total = self.groups[index]
        every = self.units(index)

        def one(unit, _):
            order, place, slot = lax.div(unit, total), lax.rem(unit, total), lax.rem(unit, 2)
            left_slot = lax.rem(order, 2)

            @pl.when(place == 0)
            def _():
                for item in self.left_copies(index, order):
                    item.wait()

                @pl.when(order + 1 < self.dp)
                def _():
                    for item in self.left_copies(index, order + 1):
                        item.start()

            for item in self.right_copies(self.groups[index][3][0], jnp.int32(0), slot):
                item.wait()

            @pl.when(unit + 1 < every)
            def _():
                self.start_right(index, unit + 1)

            @pl.when(place >= 2)
            def _():
                self.out_copy(index, unit - 2).wait()

            left, right = self.left_buf[left_slot], self.right_buf[slot]
            if kind:
                self.out_buf[slot, 0 : self.keep, 0 : self.unit] = dot_tn(left, right).astype(BF)
            else:
                self.out_buf[slot, 0 : self.unit, 0 : self.keep] = dot_tn(right, left).astype(BF)
            self.out_copy(index, unit).start()

            @pl.when(place == total - 1)
            def _():
                if total > 1:
                    self.out_copy(index, unit - 1).wait()
                self.out_copy(index, unit).wait()
                self.send(index, order, "start")

            return 0

        lax.fori_loop(start, stop, one, 0)

    def all_sent(self, index):
        def one(order, _):
            self.send(index, order, "wait")
            return 0

        lax.fori_loop(0, self.dp, one, 0)

    def all_received(self, kind):
        ref = self.received[kind]
        theirs = ref.at[1 - self.core]
        ours = ref.at[self.core, pl.ds(0, self.dp - 1)]
        remote(theirs, theirs, self.send_sems.at[0, 0], self.recv_sems.at[kind, 1 - self.core], "pipe", 1 - self.core).wait_recv()
        if self.dp > 1:
            remote(ours, ours, self.send_sems.at[0, 0], self.recv_sems.at[kind, self.core], "pipe", 1 - self.core).wait_recv()


RING = 3


def backward_kernel(dp_size, *refs):
    at = 0

    def take(count):
        nonlocal at
        at += count
        return refs[at - count : at]

    cot_ref, in_ref, x1_ref, slope_ref, q_ref, k_ref, v_ref, o_ref, logs_ref = take(9)
    own_w = take(4)
    other_w = take(4)
    h_near, h_far, act_near, act_far, o_near, o_far = take(6)
    gain_ref, cos_ref, near_ref, far_ref = take(4)
    dr0_out, dy0_out, dy0_far, du_near, du_far, dp_near, dp_far = take(7)
    stages = take(2)
    received = take(2)
    (sums_ref,) = take(1)
    ring, ring_qkv, dense_w = take(3)
    up_buf, x_buf, slope_buf, q_buf, o_buf, logs_buf = take(6)
    k_all, v_all, dk_all, dv_all = take(4)
    do_buf, dp_buf, du_buf, part = take(4)
    mean_buf, inverse_buf, up_share, x_share = take(4)
    (result,) = take(1)
    sum_bufs = take(4)
    sum_sems = dict(zip(SUM_NAMES, take(6)))
    from_left, from_right, left_sems, right_sems = take(4)
    dot_bufs = take(3)
    dot_sems = take(5)
    ring_sems, qkv_sems, dense_sem, load_sems, kv_sems, out_sems = take(6)
    far_send, far_recv, once_sems, result_send = take(4)
    assert at == len(refs)
    w_qkv, w_fc1, w_dense, w_fc2 = range(4)
    core = lax.axis_index("pipe")
    rank = lax.axis_index("tensor")
    dp_rank = lax.axis_index("dp")
    theirs = 1 - core
    rows, width = up_buf.shape
    block = rows // LINE
    local = q_buf.shape[2]
    hidden = du_buf.shape[1]
    half_hidden, half_local = hidden // 2, local // 2
    tile = ring.shape[1]
    up_tiles, out_tiles = hidden // tile, width // tile
    ring_tiles = up_tiles + out_tiles
    scale = HEAD_DIM ** (-0.5)

    def layer_of(step):
        return 1 - lax.div(step, LINE)

    def chunk_of(step):
        return LINE - 1 - lax.rem(step, LINE)

    def chunk_rows(chunk):
        return pl.ds(pl.multiple_of(chunk * rows, rows), rows)

    def weight_copy(layer, views, target, sem, act):
        if act == "wait":
            pltpu.make_async_copy(views[0], target, sem).wait()
            return

        @pl.when(core == layer)
        def _():
            pltpu.make_async_copy(views[0], target, sem).start()

        @pl.when(core != layer)
        def _():
            pltpu.make_async_copy(views[1], target, sem).start()

    def ring_copy(index, act):
        step, place = lax.div(index, ring_tiles), lax.rem(index, ring_tiles)
        slot = lax.rem(index, RING)
        target, sem = ring.at[slot], ring_sems.at[slot]
        layer = layer_of(step)
        if act == "wait":
            weight_copy(layer, [own_w[w_fc2].at[0:tile]], target, sem, act)
            return

        @pl.when(place < up_tiles)
        def _():
            span = pl.ds(pl.multiple_of(place * tile, tile), tile)
            weight_copy(layer, [own_w[w_fc2].at[span], other_w[w_fc2].at[span]], target, sem, act)

        @pl.when(place >= up_tiles)
        def _():
            span = pl.ds(pl.multiple_of((place - up_tiles) * tile, tile), tile)
            weight_copy(layer, [own_w[w_fc1].at[span], other_w[w_fc1].at[span]], target, sem, act)

    def qkv_copy(index, act):
        step, place = lax.div(index, out_tiles), lax.rem(index, out_tiles)
        slot = lax.rem(index, 2)
        span = pl.ds(pl.multiple_of(place * tile, tile), tile)
        views = [w[w_qkv].at[:, span, :] for w in (own_w, other_w)]
        weight_copy(layer_of(step), views, ring_qkv.at[slot], qkv_sems.at[slot], act)

    def dense_copy(layer, act):
        weight_copy(layer, [own_w[w_dense], other_w[w_dense]], dense_w, dense_sem.at[0], act)

    def kv_copies(layer):
        return [
            pltpu.make_async_copy(k_ref.at[layer], k_all, kv_sems.at[0]),
            pltpu.make_async_copy(v_ref.at[layer], v_all, kv_sems.at[1]),
        ]

    def early_loads(step):
        layer, slot = layer_of(step), lax.rem(step, 2)
        at_rows = chunk_rows(chunk_of(step))
        return [
            pltpu.make_async_copy(q_ref.at[layer, at_rows], q_buf.at[slot], load_sems.at[0, slot]),
            pltpu.make_async_copy(o_ref.at[layer, at_rows], o_buf.at[slot], load_sems.at[1, slot]),
            pltpu.make_async_copy(
                logs_ref.at[layer, :, :, at_rows], logs_buf.at[slot], load_sems.at[2, slot]
            ),
        ]

    def slope_load(step):
        return pltpu.make_async_copy(
            slope_ref.at[layer_of(step), chunk_rows(chunk_of(step))], slope_buf, load_sems.at[3, 0]
        )

    def x_load(src):
        return pltpu.make_async_copy(src, x_buf, load_sems.at[4, 0])

    def up_load(src):
        return pltpu.make_async_copy(src, up_buf, load_sems.at[5, 0])

    def norm_back(layer, rows_x, rows_up, total):
        values = rows_x.astype(F32)
        centre = values - jnp.mean(values, axis=-1, keepdims=True)
        inverse = lax.rsqrt(jnp.mean(centre * centre, axis=-1, keepdims=True) + ln_eps)
        xhat = centre * inverse
        e = total * gain_ref[layer : layer + 1, :]
        back = e - jnp.mean(e, axis=-1, keepdims=True) - xhat * jnp.mean(
            e * xhat, axis=-1, keepdims=True
        )
        return (rows_up.astype(F32) + inverse * back).astype(BF)

    def finish(chunk, total, target):
        target[...] = norm_back(1, x_share[chunk], up_share[chunk], total)

    summed = LineSum(rank, part, *sum_bufs, result, sum_sems, finish)
    shared = LineShare(rank, part, from_left, from_right, (left_sems, right_sems), out_tiles)
    dots = PairDots(core, dp_rank, dp_size, *dot_bufs, dot_sems, stages, received)
    dots.add(0, 1, 0, (cot_ref.at[core], cot_ref.at[theirs]), [(act_near.at[1], act_far.at[1]), (o_near.at[1], o_far.at[1])])
    dots.add(2, 0, 0, (dy0_out, dy0_far), [(act_near.at[0], act_far.at[0]), (o_near.at[0], o_far.at[0])])
    for index, layer in ((1, 1), (3, 0)):
        dots.add(
            index,
            layer,
            1,
            (h_near.at[layer], h_far.at[layer]),
            [(du_near.at[layer], du_far.at[layer])]
            + [(dp_near.at[layer, c], dp_far.at[layer, c]) for c in range(3)],
        )

    def half(which, size):
        return pl.ds(pl.multiple_of(which * size, size), size)

    def dp_copies(step):
        layer, at_rows = layer_of(step), chunk_rows(chunk_of(step))
        return [
            pltpu.make_async_copy(
                dp_buf.at[:, :, half(core, half_local)], dp_near.at[layer, :, at_rows], out_sems.at[0]
            ),
            remote(
                dp_buf.at[:, :, half(theirs, half_local)],
                dp_far.at[layer, :, at_rows],
                far_send.at[0],
                far_recv.at[0, layer],
                "pipe",
                theirs,
            ),
        ]

    def du_copies(step):
        layer, at_rows = layer_of(step), chunk_rows(chunk_of(step))
        return [
            pltpu.make_async_copy(
                du_buf.at[:, half(core, half_hidden)], du_near.at[layer, at_rows], out_sems.at[1]
            ),
            remote(
                du_buf.at[:, half(theirs, half_hidden)],
                du_far.at[layer, at_rows],
                far_send.at[1],
                far_recv.at[1, layer],
                "pipe",
                theirs,
            ),
        ]

    def result_copies(chunk):
        at_rows = chunk_rows(chunk)
        return [
            pltpu.make_async_copy(result.at[at_rows], dy0_out.at[at_rows], once_sems.at[chunk]),
            remote(
                result.at[at_rows],
                dy0_far.at[at_rows],
                result_send.at[chunk],
                far_recv.at[2, 0],
                "pipe",
                theirs,
            ),
        ]

    def start_all(copies):
        for item in copies:
            item.start()

    def left_all(copies):
        copies[0].wait()
        copies[1].wait_send()

    def far_arrived(i, layer, ref):
        remote(ref, ref, far_send.at[0], far_recv.at[i, layer], "pipe", theirs).wait_recv()

    dense_copy(1, "start")
    up_load(cot_ref.at[core, (LINE - 1) * rows : LINE * rows]).start()
    start_all(early_loads(jnp.int32(0)))
    start_all(kv_copies(1))
    for i in range(RING - 1):
        ring_copy(jnp.int32(i), "start")
    qkv_copy(jnp.int32(0), "start")
    dots.prime(0)

    barrier = pltpu.get_barrier_semaphore()

    def tell(where):
        pl.semaphore_signal(barrier, inc=1, device_id=where, device_id_type=pl.DeviceIdType.MESH)

    def tell_peer(other, _):
        tell({"pipe": theirs, "dp": other})

        @pl.when(other != dp_rank)
        def _():
            tell({"dp": other})

        return 0

    lax.fori_loop(0, dp_size, tell_peer, 0)

    @pl.when(rank > 0)
    def _():
        tell({"tensor": rank - 1})

    @pl.when(rank < LINE - 1)
    def _():
        tell({"tensor": rank + 1})

    ends = jnp.where(rank > 0, 1, 0) + jnp.where(rank < LINE - 1, 1, 0)
    pl.semaphore_wait(barrier, 2 * dp_size - 1 + ends)

    sums_ref[...] = jnp.zeros_like(sums_ref)

    keep = lax.broadcasted_iota(jnp.int32, (rows, rows), 0) <= lax.broadcasted_iota(
        jnp.int32, (rows, rows), 1
    )

    def attention(chunk, slot):
        here = slice(chunk * rows, (chunk + 1) * rows)
        spans = ([(slice(0, chunk * rows), False)] if chunk else []) + [(here, True)]
        tables = (cos_ref[here, :], -near_ref[here, :], -far_ref[here, :])

        def pair(j, _):
            lanes = pl.ds(pl.multiple_of(j * LANES, LANES), LANES)
            query, upstream = q_buf[slot, :, lanes], do_buf[:, lanes]
            product = upstream.astype(F32) * o_buf[slot, :, lanes].astype(F32)
            grads = []
            key_terms = [None] * len(spans)
            value_terms = [None] * len(spans)
            for which in range(LANES // HEAD_DIM):
                mask = head_mask(rows, which)
                mine = jnp.where(mask, query, jnp.zeros_like(query))
                mine_up = jnp.where(mask, upstream, jnp.zeros_like(upstream))
                logs = logs_buf[slot, j, which : which + 1, :]
                centre = as_row(jnp.sum(jnp.where(mask, product, 0.0), axis=1, keepdims=True))
                grad = None
                for i, (span, diagonal) in enumerate(spans):
                    keys = k_all[span, lanes]
                    probs = jnp.exp(dot_nt(keys, mine) - logs)
                    if diagonal:
                        probs = jnp.where(keep, probs, 0.0)
                    grad_probs = dot_nt(v_all[span, lanes], mine_up)
                    grad_scores = (probs * (grad_probs - centre)).astype(BF)
                    value_term = dot_nn(probs.astype(BF), mine_up)
                    key_term = dot_nn(grad_scores, mine)
                    term = dot_tn(grad_scores, keys)
                    grad = term if grad is None else grad + term
                    if which == 0:
                        key_terms[i], value_terms[i] = key_term, value_term
                    else:
                        dk_all[span, lanes] += key_terms[i] + key_term
                        dv_all[span, lanes] += value_terms[i] + value_term
                grads.append(grad)
            merged = jnp.where(head_mask(rows, 0), grads[0], grads[1]) * scale
            dp_buf[0, :, lanes] = turn(merged, *tables).astype(BF)
            dp_buf[1, :, lanes] = turn(dk_all[here, lanes], *tables).astype(BF)
            dp_buf[2, :, lanes] = dv_all[here, lanes].astype(BF)
            return 0

        lax.fori_loop(0, local // LANES, pair, 0)

    each_first = dots.units(0) // LINE
    each_second = dots.units(1) // LINE

    def step_body(step, _):
        layer, chunk, slot = layer_of(step), chunk_of(step), lax.rem(step, 2)
        lead = layer == 1
        starting = lax.rem(step, LINE) == 0
        at_rows = chunk_rows(chunk)

        @pl.when(step == LINE)
        def _():
            left_all(dp_copies(step - 1))
            left_all(du_copies(step - 1))
            far_arrived(0, 1, dp_far.at[1])
            far_arrived(1, 1, du_far.at[1])
            dots.prime(1)

        @pl.when(step >= LINE)
        def _():
            at_unit = (step - LINE) * each_second
            dots.run(1, at_unit, at_unit + each_second)
            summed.stage_f(chunk)
            start_all(result_copies(chunk))
            up_buf[...] = result[at_rows, :]
            x_load(in_ref.at[core, at_rows]).start()

        @pl.when(lead)
        def _():
            up_load(cot_ref.at[core, at_rows]).wait()
            x_load(x1_ref.at[at_rows]).start()

        slope_load(step).start()

        @pl.when(step + 1 < STEPS)
        def _():
            start_all(early_loads(step + 1))

        @pl.when(starting)
        def _():
            dense_copy(layer, "wait")
            dk_all[...] = jnp.zeros_like(dk_all)
            dv_all[...] = jnp.zeros_like(dv_all)

        do_buf[...] = dot_nt(up_buf[...], dense_w[...]).astype(BF)

        @pl.when(step == LINE - 1)
        def _():
            dense_copy(jnp.int32(0), "start")

        sums_ref[layer, 3:4, :] += jnp.sum(up_buf[...].astype(F32), axis=0, keepdims=True)

        @pl.when(lead)
        def _():
            up_share[chunk] = up_buf[pl.ds(pl.multiple_of(rank * block, block), block), :]

        for item in early_loads(step):
            item.wait()

        @pl.when(starting)
        def _():
            for item in kv_copies(layer):
                item.wait()

        @pl.when((step >= 1) & (step != LINE))
        def _():
            left_all(dp_copies(step - 1))

        for index in range(LINE):

            @pl.when(chunk == index)
            def _():
                attention(index, slot)

        start_all(dp_copies(step))

        @pl.when(step == LINE - 1)
        def _():
            start_all(kv_copies(jnp.int32(0)))

        for i in range(3):
            sums_ref[layer, 4 + i : 5 + i, 0:local] += jnp.sum(
                dp_buf[i].astype(F32), axis=0, keepdims=True
            )

        @pl.when((step >= 1) & (step <= LINE))
        def _():
            summed.stage_b(chunk_of(step - 1))

        @pl.when((step >= 2) & (step <= LINE + 1))
        def _():
            summed.stage_d(chunk_of(step - 2))

        @pl.when((step >= 3) & (step <= LINE + 2))
        def _():
            summed.stage_e(chunk_of(step - 3), 1)

        @pl.when(step > LINE)
        def _():
            shared.relay(chunk_of(step - 1), 1)

        @pl.when(lead)
        def _():
            at_unit = step * each_first
            dots.run(0, at_unit, at_unit + each_first)

        slope_load(step).wait()

        @pl.when((step >= 1) & (step != LINE))
        def _():
            left_all(du_copies(step - 1))

        def hidden_part(i, _):
            cols = pl.ds(pl.multiple_of(i * tile, tile), tile)
            index = step * ring_tiles + i
            ring_copy(index, "wait")
            ring_copy(index + RING - 1, "start")
            weight = ring.at[lax.rem(index, RING)]
            value = dot_nt(up_buf[...], weight[...]) * slope_buf[:, cols].astype(F32)
            value = value.astype(BF)
            du_buf[:, cols] = value
            sums_ref[layer, 2:3, cols] += jnp.sum(value.astype(F32), axis=0, keepdims=True)
            return 0

        lax.fori_loop(0, up_tiles, hidden_part, 0)
        start_all(du_copies(step))

        @pl.when(step + 1 < LINE)
        def _():
            up_load(cot_ref.at[core, chunk_rows(chunk - 1)]).start()

        x_load(x1_ref.at[at_rows]).wait()
        small = rows // 8

        def statistics(i, _):
            span = pl.ds(pl.multiple_of(i * small, small), small)
            values = x_buf[span, :].astype(F32)
            mean = jnp.mean(values, axis=-1, keepdims=True)
            centre = values - mean
            mean_buf[span, :] = mean
            inverse_buf[span, :] = lax.rsqrt(
                jnp.mean(centre * centre, axis=-1, keepdims=True) + ln_eps
            )
            return 0

        lax.fori_loop(0, 8, statistics, 0)

        @pl.when(lead)
        def _():
            x_share[chunk] = x_buf[pl.ds(pl.multiple_of(rank * block, block), block), :]

        @pl.when(jnp.logical_not(lead))
        def _():
            summed.sent_part(chunk)

        def normed_part(i, _):
            cols = pl.ds(pl.multiple_of(i * tile, tile), tile)
            index = step * ring_tiles + up_tiles + i
            ring_copy(index, "wait")

            @pl.when(index + RING - 1 < STEPS * ring_tiles)
            def _():
                ring_copy(index + RING - 1, "start")

            qkv_index = step * out_tiles + i
            qkv_copy(qkv_index, "wait")

            @pl.when(qkv_index + 1 < STEPS * out_tiles)
            def _():
                qkv_copy(qkv_index + 1, "start")

            value = dot_nt(du_buf[...], ring[lax.rem(index, RING)])
            for c in range(3):
                value = value + dot_nt(dp_buf[c], ring_qkv[lax.rem(qkv_index, 2), c])
            xhat = (x_buf[:, cols].astype(F32) - mean_buf[...]) * inverse_buf[...]
            sums_ref[layer, 0:1, cols] += jnp.sum(value * xhat, axis=0, keepdims=True)
            sums_ref[layer, 1:2, cols] += jnp.sum(value, axis=0, keepdims=True)
            part[chunk, :, cols] = value.astype(BF)

            @pl.when(jnp.logical_not(lead))
            def _():
                shared.emit(chunk, i)

            return 0

        lax.fori_loop(0, out_tiles, normed_part, 0)

        @pl.when(lead)
        def _():
            summed.stage_a(chunk)

        @pl.when((step >= 1) & (step <= LINE))
        def _():
            summed.stage_c(chunk_of(step - 1))

        @pl.when((step >= 2) & (step <= LINE + 1))
        def _():
            summed.stage_e(chunk_of(step - 2), 0)

        @pl.when(step > LINE)
        def _():
            shared.relay(chunk_of(step - 1), 2)

        return 0

    lax.fori_loop(0, STEPS, step_body, 0)

    mine = chunk_rows(rank)
    reload = [up_load(result.at[mine]), x_load(in_ref.at[core, mine])]
    start_all(reload)
    for chunk in range(LINE):
        left_all(result_copies(chunk))
    far_arrived(2, 0, dy0_far)
    dots.prime(2)
    some = dots.units(2) // 2
    dots.run(2, 0, some)
    shared.relay(0, 1)
    dots.run(2, some, dots.units(2))
    last_step = jnp.int32(STEPS - 1)
    left_all(dp_copies(last_step))
    left_all(du_copies(last_step))
    far_arrived(0, 0, dp_far.at[0])
    far_arrived(1, 0, du_far.at[0])
    dots.prime(3)
    shared.relay(0, 2)
    dots.run(3, 0, dots.units(3))
    shared.arrived(rank)
    for item in reload:
        item.wait()
    small = rows // 8

    def last(i, _):
        span = pl.ds(pl.multiple_of(i * small, small), small)
        left = jnp.where(rank > 0, from_left[rank, span, :], jnp.zeros((small, width), BF))
        right = jnp.where(rank < LINE - 1, from_right[rank, span, :], jnp.zeros((small, width), BF))
        total = part[rank, span, :].astype(F32) + left.astype(F32) + right.astype(F32)
        up_buf[span, :] = norm_back(0, x_buf[span, :], up_buf[span, :], total)
        return 0

    lax.fori_loop(0, 8, last, 0)
    out_copy = pltpu.make_async_copy(up_buf, dr0_out, load_sems.at[5, 0])
    out_copy.start()
    out_copy.wait()
    for chunk in range(LINE):
        summed.sent_rest(chunk)
        shared.sent(chunk)
    for index in range(4):
        dots.all_sent(index)
    for kind in range(2):
        dots.all_received(kind)


def backward_both(dp_size, cotangent, inputs, x1, saved, own_w, other_w, sides, gains, tables):
    slope, query, key, value, merged, logs = saved
    _, length, width = inputs.shape
    w_qkv, w_fc1, w_dense, w_fc2 = own_w
    local, hidden = w_dense.shape[0], w_fc1.shape[1]
    rows = length // LINE
    block = rows // LINE
    pairs = local // LANES
    tile = min(TILE, width)
    out_tiles = width // tile
    keep = width // dp_size
    unit = local // 2
    down, up = hidden // 2 + local // 2, hidden // 2 + 3 * (local // 2)

    def bf(*shape):
        return jax.ShapeDtypeStruct(shape, BF)

    def room(*shape):
        return pltpu.VMEM(shape, BF)

    whole = pl.BlockSpec(memory_space=pltpu.VMEM)
    away = pl.BlockSpec(memory_space=pl.ANY)
    dma = pltpu.SemaphoreType.DMA
    outs = [
        bf(rows, width),
        bf(length, width),
        bf(length, width),
        bf(2, length, hidden // 2),
        bf(2, length, hidden // 2),
        bf(2, 3, length, local // 2),
        bf(2, 3, length, local // 2),
        bf(2, dp_size, down, keep),
        bf(2, dp_size, keep, up),
        bf(2, dp_size, down, keep),
        bf(2, dp_size, keep, up),
    ]
    most = max(keep, unit)
    return pl.pallas_call(
        functools.partial(backward_kernel, dp_size),
        name="backward_both",
        in_specs=[away] * 23 + [whole] * 4,
        out_specs=[away] * len(outs) + [whole],
        out_shape=outs + [jax.ShapeDtypeStruct((2, 8, max(width, hidden)), F32)],
        scratch_shapes=[
            room(RING, tile, width),
            room(2, 3, tile, local),
            room(local, width),
            room(rows, width),
            room(rows, width),
            room(rows, hidden),
            room(2, rows, local),
            room(2, rows, local),
            pltpu.VMEM((2, pairs, 8, rows), F32),
            room(length, local),
            room(length, local),
            pltpu.VMEM((length, local), F32),
            pltpu.VMEM((length, local), F32),
            room(rows, local),
            room(3, rows, local),
            room(rows, hidden),
            room(LINE, rows, width),
            pltpu.VMEM((rows, 1), F32),
            pltpu.VMEM((rows, 1), F32),
            room(LINE, block, width),
            room(LINE, block, width),
            room(length, width),
        ]
        + line_sum_scratch(rows, width)
        + [room(LINE, rows, width)] * 2
        + [dma((2, LINE * out_tiles))] * 2
        + [
            room(2, 2 * length, keep),
            room(2, 2 * length, unit),
            room(2, most, most),
            dma((2, 2)),
            dma((2, 2)),
            dma((2,)),
            dma((4, dp_size)),
            dma((2, 2)),
        ]
        + [
            dma((RING,)),
            dma((2,)),
            dma((1,)),
            dma((6, 2)),
            dma((2,)),
            dma((2,)),
            dma((2,)),
            dma((3, 2)),
            dma((LINE,)),
            dma((LINE,)),
        ],
        compiler_params=pltpu.CompilerParams(
            collective_id=1, has_side_effects=True, vmem_limit_bytes=63 * MIB
        ),
        cost_estimate=pl.CostEstimate(
            flops=16 * length * width * (4 * local + 2 * hidden),
            bytes_accessed=400 * MIB,
            transcendentals=0,
        ),
    )(
        cotangent, inputs, x1, slope, query, key, value, merged, logs, *own_w, *other_w, *sides, gains, *tables
    )


def bit_pairs(size, bit):
    return [(index, index ^ bit) for index in range(size)]


def body(
    inputs, cotangent, ln_gain, ln_bias, w_qkv, b_qkv, w_dense, b_dense, w_fc1, b_fc1, w_fc2, b_fc2
):
    core = lax.axis_index("pipe")
    rank = lax.axis_index("tensor")
    dp_size = lax.axis_size("dp")
    dp_rank = lax.axis_index("dp")
    first = core == 0
    _, length, width = inputs.shape
    lines = lax.axis_size("tensor")
    local = w_qkv.shape[3]
    hidden = w_fc1.shape[2]

    def both(own):
        other = lax.ppermute(own, "pipe", [(0, 1), (1, 0)])
        return (jnp.where(first, own, other), jnp.where(first, other, own))

    small = jnp.concatenate(
        [ln_gain[0], ln_bias[0], b_qkv[0].reshape(-1), b_dense[0], b_fc1[0], b_fc2[0]]
    )
    small_both = jnp.stack(both(small)).astype(F32)
    vectors = []
    at = 0
    for count in (width, width, 3 * local, width, hidden, width):
        vectors.append(small_both[:, at : at + count])
        at += count
    gains, shifts, bias3, bias_d, bias_u, bias_2 = vectors
    bias_o = bias_d + bias_2
    tables = rotary_tables(length)
    own_w = (w_qkv[0], w_fc1[0], w_dense[0], w_fc2[0])

    results = forward_both(
        inputs, own_w, (gains, shifts, bias3.reshape(6, local), bias_u, bias_o), tables
    )
    other_w = results[:4]
    h, h_far, query, key, value, merged, merged_near, merged_far = results[4:12]
    act_near, act_far, slope, logs, x1, part1 = results[12:]
    saved = (slope, query, key, value, merged, logs)

    def share_of(rows):
        size = rows.shape[0] // lines
        return lax.dynamic_slice_in_dim(rows, rank * size, size, 0)

    act0 = share_of(x1)
    summed1 = lax.psum_scatter(part1, "tensor", scatter_dimension=0, tiled=True)
    act1 = (act0.astype(F32) + summed1.astype(F32) + bias_o[1]).astype(BF)
    sides = (h, h_far, act_near, act_far, merged_near, merged_far)
    grads = backward_both(
        dp_size, cotangent, inputs, x1, saved, own_w, other_w, sides, gains, tables
    )
    dr0_share, dy0 = grads[:2]
    down, up, sums = grads[9:]
    dr1_share = share_of(dy0)

    def to_owner(value0, value1):
        from1 = lax.ppermute(value0, "pipe", [(1, 0)])
        from0 = lax.ppermute(value1, "pipe", [(0, 1)])
        return jnp.where(first, value0, value1), jnp.where(first, from1, from0)

    def in_order(own, other, axis):
        return jnp.where(
            first,
            jnp.concatenate([own, other], axis=axis),
            jnp.concatenate([other, own], axis=axis),
        )

    def stacked(value0, value1):
        own, other = to_owner(value0, value1)
        return in_order(own[None], other[None], 0)

    acts = stacked(act0, act1)
    grads_in = stacked(dr0_share, dr1_share)
    down = jnp.sum(down.astype(F32), axis=1)
    up = jnp.sum(up.astype(F32), axis=1)
    side, cut = local // 2, hidden // 2
    rows_kept = up.shape[1]
    out_fc2 = down[:, :cut].reshape(hidden, rows_kept)
    out_dense = down[:, cut:].reshape(local, rows_kept)
    out_fc1 = jnp.concatenate([up[0, :, :cut], up[1, :, :cut]], axis=1)
    out_qkv = jnp.stack(
        [
            jnp.concatenate(
                [up[part, :, cut + c * side : cut + (c + 1) * side] for part in range(2)], axis=1
            )
            for c in range(3)
        ]
    )

    def butterfly(value, axis, size):
        bit = 1
        while bit < size:
            value = value + lax.ppermute(value, axis, bit_pairs(size, bit))
            bit *= 2
        return value

    def small_sums(sums):
        packed = butterfly(butterfly(sums, "pipe", 2), "dp", dp_size)
        return butterfly(packed[:2], "tensor", lines), packed[2:]

    norm1, rest1 = small_sums(sums[1])
    norm0, rest0 = small_sums(sums[0])
    norm = jnp.where(first, norm0, norm1)
    rest = jnp.where(first, rest0, rest1)
    place = rank * dp_size + dp_rank

    def piece(rows, count, index, parts):
        size = count // parts
        return lax.dynamic_slice_in_dim(rows[:, :count], index * size, size, 1)

    out_norm = piece(norm, width, place, lines * dp_size)
    out_bfc1 = piece(rest[0:1], hidden, dp_rank, dp_size)
    out_bout = piece(rest[1:2], width, dp_rank, dp_size)
    out_bqkv = piece(rest[2:5], local, dp_rank, dp_size)
    return (
        acts[None],
        grads_in[None],
        out_norm[0:1],
        out_norm[1:2],
        out_qkv[None],
        out_bqkv[None],
        out_dense[None],
        out_bout,
        out_fc1[None],
        out_bfc1,
        out_fc2[None],
        out_bout,
    )


def solution(mesh):
    in_specs = (
        P("dp", None, None),
        P("dp", None, None),
        P("pipe", None),
        P("pipe", None),
        P("pipe", None, None, "tensor"),
        P("pipe", None, "tensor"),
        P("pipe", "tensor", None),
        P("pipe", None),
        P("pipe", None, "tensor"),
        P("pipe", "tensor"),
        P("pipe", "tensor", None),
        P("pipe", None),
    )
    out_specs = (
        P("pipe", "dp", "tensor", None),
        P("pipe", "dp", "tensor", None),
        P("pipe", ("tensor", "dp")),
        P("pipe", ("tensor", "dp")),
        P("pipe", None, "dp", "tensor"),
        P("pipe", None, ("tensor", "dp")),
        P("pipe", "tensor", "dp"),
        P("pipe", "dp"),
        P("pipe", "dp", "tensor"),
        P("pipe", ("tensor", "dp")),
        P("pipe", "tensor", "dp"),
        P("pipe", "dp"),
    )
    return jax.shard_map(body, mesh=mesh, in_specs=in_specs, out_specs=out_specs, check_vma=False)
```

```python
import functools

import jax
import jax.numpy as jnp
from jax import lax
from jax.experimental import pallas as pl
from jax.experimental.pallas import tpu as pltpu
from jax.sharding import PartitionSpec as P

HEAD_DIM = 64
ROT = 32
LANES = 128
MIB = 1024 * 1024

ln_eps = 1e-05
rope_base = 10000.0
gelu_coef = 0.7978845608028654
masked_score = -1e30

BF = jnp.bfloat16
F32 = jnp.float32


def rotary_tables(length):
    half_rot = ROT // 2
    inverse = rope_base ** (-(jnp.arange(half_rot, dtype=F32) * 2.0 / ROT))
    angles = jnp.arange(length, dtype=F32)[:, None] * inverse[None, :]
    cosines, sines = jnp.cos(angles), jnp.sin(angles)
    rest = HEAD_DIM - ROT
    blank = jnp.zeros((length, half_rot), F32)
    tail = jnp.zeros((length, rest), F32)
    cos_head = jnp.concatenate([cosines, cosines, jnp.ones((length, rest), F32)], axis=1)
    near_head = jnp.concatenate([-sines, blank, tail], axis=1)
    far_head = jnp.concatenate([blank, sines, tail], axis=1)
    pair = LANES // HEAD_DIM
    return tuple(jnp.tile(part, (1, pair)) for part in (cos_head, near_head, far_head))


def turn(values, cos, near, far):
    half_rot = ROT // 2
    return (
        values * cos
        + pltpu.roll(values, LANES - half_rot, 1) * near
        + pltpu.roll(values, half_rot, 1) * far
    )


def head_mask(rows, which):
    lanes = lax.broadcasted_iota(jnp.int32, (rows, LANES), 1)
    return (lanes // HEAD_DIM) == which


def as_row(column):
    return jnp.transpose(jnp.broadcast_to(column, (column.shape[0], LANES)))[0:1, :]


def dot_nt(left, right):
    return lax.dot_general(left, right, (((1,), (1,)), ((), ())), preferred_element_type=F32)


def dot_nn(left, right):
    return lax.dot_general(left, right, (((1,), (0,)), ((), ())), preferred_element_type=F32)


def dot_tn(left, right):
    return lax.dot_general(left, right, (((0,), (0,)), ((), ())), preferred_element_type=F32)


LINE = 4
STEPS = 2 * LINE
TILE = 512


def remote(src, dst, send, recv, axis, index):
    return pltpu.make_async_remote_copy(
        src_ref=src,
        dst_ref=dst,
        send_sem=send,
        recv_sem=recv,
        device_id={axis: index},
        device_id_type=pl.DeviceIdType.MESH,
    )


def greet(core, rank):
    barrier = pltpu.get_barrier_semaphore()

    def tell(axis, index):
        pl.semaphore_signal(
            barrier, inc=1, device_id={axis: index}, device_id_type=pl.DeviceIdType.MESH
        )

    tell("pipe", 1 - core)

    @pl.when(rank > 0)
    def _():
        tell("tensor", rank - 1)

    @pl.when(rank < LINE - 1)
    def _():
        tell("tensor", rank + 1)

    ends = jnp.where(rank > 0, 1, 0) + jnp.where(rank < LINE - 1, 1, 0)
    pl.semaphore_wait(barrier, 1 + ends)


def fetch_weight(layer, core, own, other, target, sem, arrival):
    @pl.when(core == layer)
    def _():
        pltpu.make_async_copy(own, target, sem).start()

    @pl.when(core != layer)
    def _():
        if arrival is not None:
            arrival.wait_recv()
        pltpu.make_async_copy(other, target, sem).start()


class LineSum:
    def __init__(self, rank, part, first, beside, second, last, result, sems, finish):
        self.rank, self.part, self.result, self.finish = rank, part, result, finish
        self.first, self.beside, self.second, self.last = first, beside, second, last
        self.sems = sems
        self.rows = part.shape[1]
        self.block = self.rows // LINE
        half = 2 * self.block
        self.left = rank < 2
        self.far = pl.multiple_of(jnp.where(self.left, half, 0), half)
        self.near = pl.multiple_of(jnp.where(self.left, 0, half), half)
        self.own = pl.multiple_of(rank * self.block, self.block)
        self.inner = (rank == 1) | (rank == 2)
        self.outer = (rank == 0) | (rank == 3)
        self.inward = jnp.where(self.left, 1, 2)
        self.outward = jnp.where(self.left, 0, 3)
        self.across = jnp.where(self.left, 2, 1)
        self.spare = pl.multiple_of(jnp.where(self.left, self.block, half), self.block)
        self.out_half = pl.multiple_of(jnp.where(self.left, 0, self.block), self.block)
        self.in_half = pl.multiple_of(jnp.where(self.left, self.block, 0), self.block)

    def hop(self, name, chunk, src, dst, to):
        return remote(src, dst, self.sems[name].at[0, chunk], self.sems[name].at[1, chunk], "tensor", to)

    def copies(self, chunk):
        half = 2 * self.block
        hop_first = self.hop(
            "first", chunk, self.part.at[chunk, pl.ds(self.far, half)], self.first.at[chunk], self.inward
        )
        hop_beside = self.hop(
            "beside",
            chunk,
            self.part.at[chunk, pl.ds(self.spare, self.block)],
            self.beside.at[chunk],
            self.inward,
        )
        hop_second = self.hop(
            "second", chunk, self.first.at[chunk], self.second.at[chunk], self.across
        )
        hop_last = self.hop(
            "last",
            chunk,
            self.second.at[chunk, pl.ds(self.out_half, self.block)],
            self.last.at[chunk],
            self.outward,
        )
        return hop_first, hop_beside, hop_second, hop_last

    def result_rows(self, chunk, shard):
        start = pl.multiple_of(chunk * self.rows + shard * self.block, self.block)
        return self.result.at[pl.ds(start, self.block)]

    def move(self, way, chunk, hop):
        step = 1 - 2 * way
        shard = jnp.clip(self.rank - step * hop, 0, LINE - 1)
        rows = self.result_rows(chunk, shard)
        name = "up" if way == 0 else "down"
        to = jnp.clip(self.rank + step, 0, LINE - 1)
        index = chunk * (LINE - 1) + hop
        return remote(rows, rows, self.sems[name].at[0, index], self.sems[name].at[1, index], "tensor", to)

    def stage_a(self, chunk):
        @pl.when(self.outer)
        def _():
            hop_first, hop_beside, _, _ = self.copies(chunk)
            hop_first.start()
            hop_beside.start()

    def stage_b(self, chunk):
        @pl.when(self.inner)
        def _():
            hop_first, _, hop_second, _ = self.copies(chunk)
            hop_first.wait_recv()
            self.first[chunk] = (
                self.first[chunk].astype(F32)
                + self.part[chunk, pl.ds(self.far, 2 * self.block)].astype(F32)
            ).astype(BF)
            hop_second.start()

    def stage_c(self, chunk):
        @pl.when(self.inner)
        def _():
            _, hop_beside, hop_second, hop_last = self.copies(chunk)
            hop_second.wait_recv()
            out_rows = pl.ds(self.out_half, self.block)
            near_out = pl.ds(pl.multiple_of(self.near + self.out_half, self.block), self.block)
            self.second[chunk, out_rows] = (
                self.second[chunk, out_rows].astype(F32) + self.part[chunk, near_out].astype(F32)
            ).astype(BF)
            hop_last.start()
            hop_beside.wait_recv()
            total = (
                self.second[chunk, pl.ds(self.in_half, self.block)].astype(F32)
                + self.beside[chunk].astype(F32)
                + self.part[chunk, pl.ds(self.own, self.block)].astype(F32)
            )
            self.finish(chunk, total, self.result_rows(chunk, self.rank))
            self.move(0, chunk, 0).start()
            self.move(1, chunk, 0).start()

    def stage_d(self, chunk):
        @pl.when(self.outer)
        def _():
            _, _, _, hop_last = self.copies(chunk)
            hop_last.wait_recv()
            total = self.last[chunk].astype(F32) + self.part[
                chunk, pl.ds(self.own, self.block)
            ].astype(F32)
            self.finish(chunk, total, self.result_rows(chunk, self.rank))

        @pl.when(self.rank == 0)
        def _():
            self.move(0, chunk, 0).start()

        @pl.when(self.rank == 3)
        def _():
            self.move(1, chunk, 0).start()

    def stage_e(self, chunk, hop):
        for way in range(2):
            behind = self.rank if way == 0 else LINE - 1 - self.rank

            @pl.when(self.inner & (behind > hop))
            def _():
                self.arrival(way, chunk, hop).wait_recv()
                self.move(way, chunk, hop + 1).start()

    def arrival(self, way, chunk, hop):
        step = 1 - 2 * way
        shard = jnp.clip(self.rank - step * (hop + 1), 0, LINE - 1)
        rows = self.result_rows(chunk, shard)
        name = "up" if way == 0 else "down"
        to = jnp.clip(self.rank + step, 0, LINE - 1)
        index = chunk * (LINE - 1) + hop
        return remote(rows, rows, self.sems[name].at[0, index], self.sems[name].at[1, index], "tensor", to)

    def stage_f(self, chunk):
        @pl.when(self.rank == 0)
        def _():
            for hop in range(LINE - 1):
                self.arrival(1, chunk, hop).wait_recv()

        @pl.when(self.rank == 3)
        def _():
            for hop in range(LINE - 1):
                self.arrival(0, chunk, hop).wait_recv()

    def sent_part(self, chunk):
        @pl.when(self.outer)
        def _():
            hop_first, hop_beside, _, _ = self.copies(chunk)
            hop_first.wait_send()
            hop_beside.wait_send()

    def sent_rest(self, chunk):
        @pl.when(self.inner)
        def _():
            _, _, hop_second, hop_last = self.copies(chunk)
            hop_second.wait_send()
            hop_last.wait_send()

        for way in range(2):
            behind = self.rank if way == 0 else LINE - 1 - self.rank
            ahead = LINE - 1 - behind
            for hop in range(LINE - 1):

                @pl.when((ahead > 0) & (behind >= hop))
                def _():
                    self.move(way, chunk, hop).wait_send()


def line_sum_scratch(rows, cols):
    block = rows // LINE
    return [
        pltpu.VMEM((LINE, 2 * block, cols), BF),
        pltpu.VMEM((LINE, block, cols), BF),
        pltpu.VMEM((LINE, 2 * block, cols), BF),
        pltpu.VMEM((LINE, block, cols), BF),
    ] + [pltpu.SemaphoreType.DMA((2, LINE))] * 4 + [
        pltpu.SemaphoreType.DMA((2, LINE * (LINE - 1)))
    ] * 2


SUM_NAMES = ("first", "beside", "second", "last", "up", "down")


class LineShare:
    def __init__(self, rank, part, room, sems, pieces):
        self.rank, self.part, self.room, self.pieces = rank, part, room, pieces
        self.sems = sems
        self.cols = part.shape[2] // pieces

    def span(self, piece):
        return pl.ds(pl.multiple_of(piece * self.cols, self.cols), self.cols)

    def slot(self, way, chunk, device):
        return chunk if way == 0 else jnp.where(device == chunk, LINE, chunk)

    def copy(self, way, chunk, piece, own):
        to = jnp.clip(self.rank + 1 - 2 * way, 0, LINE - 1)
        span = self.span(piece)
        here = self.part.at[chunk, :, span] if own else self.room.at[self.slot(way, chunk, self.rank), :, span]
        index = chunk * self.pieces + piece
        return remote(
            here,
            self.room.at[self.slot(way, chunk, to), :, span],
            self.sems[way].at[0, index],
            self.sems[way].at[1, index],
            "tensor",
            to,
        )

    def emit(self, chunk, piece):
        @pl.when((self.rank == 0) & (chunk > 0))
        def _():
            self.copy(0, chunk, piece, True).start()

        @pl.when((self.rank == LINE - 1) & (chunk < LINE - 1))
        def _():
            self.copy(1, chunk, piece, True).start()

    def relay(self, chunk, hop):
        for way in range(2):
            at = hop if way == 0 else LINE - 1 - hop
            further = (chunk > at) if way == 0 else (chunk < at)

            @pl.when((self.rank == at) & further)
            def _():
                def one(piece, _):
                    copy = self.copy(way, chunk, piece, False)
                    copy.wait_recv()
                    span = self.span(piece)
                    slot = self.slot(way, chunk, self.rank)
                    self.room[slot, :, span] = (
                        self.room[slot, :, span].astype(F32) + self.part[chunk, :, span].astype(F32)
                    ).astype(BF)
                    copy.start()
                    return 0

                lax.fori_loop(0, self.pieces, one, 0)

    def arrived(self):
        for way in range(2):
            behind = self.rank > 0 if way == 0 else self.rank < LINE - 1

            @pl.when(behind)
            def _():
                def one(piece, _):
                    self.copy(way, self.rank, piece, False).wait_recv()
                    return 0

                lax.fori_loop(0, self.pieces, one, 0)

    def total(self, span):
        blank = jnp.zeros((span.size, self.part.shape[2]), BF)
        left = jnp.where(self.rank > 0, self.room[self.rank, span, :], blank)
        right = jnp.where(self.rank < LINE - 1, self.room[LINE, span, :], blank)
        return self.part[self.rank, span, :].astype(F32) + left.astype(F32) + right.astype(F32)

    def sent(self, chunk):
        for way in range(2):
            end = 0 if way == 0 else LINE - 1
            for hop in range(LINE - 1):
                at = hop if way == 0 else LINE - 1 - hop
                further = (chunk > at) if way == 0 else (chunk < at)

                @pl.when((self.rank == at) & further)
                def _():
                    def one(piece, _):
                        self.copy(way, chunk, piece, at == end).wait_send()
                        return 0

                    lax.fori_loop(0, self.pieces, one, 0)


def deliver(core, layer, mine, target, sems, act):
    @pl.when(core == layer)
    def _():
        copy = pltpu.make_async_copy(mine, target.at[core], sems.at[layer])
        copy.start() if act == "start" else copy.wait()

    @pl.when(core != layer)
    def _():
        copy = remote(mine, target.at[core], sems.at[layer], sems.at[2], "pipe", 1 - core)
        copy.start() if act == "start" else copy.wait_send()


def delivered(core, target, sems):
    ref = target.at[1 - core]
    remote(ref, ref, sems.at[0], sems.at[2], "pipe", 1 - core).wait_recv()


def forward_kernel(*refs):
    at = 0

    def take(count):
        nonlocal at
        at += count
        return refs[at - count : at]

    (inputs_ref,) = take(1)
    own_w = take(4)
    gain_ref, shift_ref, bias3_ref, bias_u_ref, bias_o_ref = take(5)
    cos_ref, near_ref, far_ref = take(3)
    other_w = take(4)
    h_out, h_far, q_out, k_out, v_out, o_out, o_near, o_far = take(8)
    act_near, act_far, slope_out, logs_out, x1_out, part_out = take(6)
    vmem_w = take(4)
    x_buf, x_share, h_buf, act_buf, slope_buf, q_buf, o_buf, k_all, v_all, logs_buf = take(10)
    part, x1 = take(2)
    sum_bufs = take(4)
    sum_sems = dict(zip(SUM_NAMES, take(6)))
    w_sems, fetch_sems, x_sems, out_sems, slot4_sems, far_send, far_recv, once_sems = take(8)
    assert at == len(refs)
    core = lax.axis_index("pipe")
    rank = lax.axis_index("tensor")
    theirs = 1 - core
    rows = x_buf.shape[1]
    width = x_buf.shape[2]
    local = q_buf.shape[2]
    hidden = act_buf.shape[2]
    half_hidden = hidden // 2
    half_local = local // 2
    tile = min(TILE, width)
    scale = HEAD_DIM ** (-0.5)

    weight_moves = [
        remote(own, other, w_sems.at[0, i], w_sems.at[1, i], "pipe", 1 - core)
        for i, (own, other) in enumerate(zip(own_w, other_w))
    ]

    def fetch(layer, i):
        fetch_weight(
            layer, core, own_w[i], other_w[i], vmem_w[i], fetch_sems.at[i], weight_moves[i]
        )

    def fetched(i):
        pltpu.make_async_copy(own_w[i], vmem_w[i], fetch_sems.at[i]).wait()

    def chunk_rows(chunk):
        return pl.ds(pl.multiple_of(chunk * rows, rows), rows)

    def x_copy(chunk):
        slot = lax.rem(chunk, 2)
        return pltpu.make_async_copy(
            inputs_ref.at[core, chunk_rows(chunk)], x_buf.at[slot], x_sems.at[slot]
        )

    def finish(chunk, total, target):
        value = total + x_share[chunk].astype(F32) + bias_o_ref[0:1, :]
        target[...] = value.astype(BF)

    summed = LineSum(rank, part, *sum_bufs, x1, sum_sems, finish)

    def half(which, size):
        return pl.ds(pl.multiple_of(which * size, size), size)

    def placed(step):
        layer, chunk = lax.div(step, LINE), lax.rem(step, LINE)
        return layer, chunk_rows(chunk), lax.rem(step, 2), chunk

    def local_copy(name, src, dst, slot):
        return pltpu.make_async_copy(src, dst, out_sems.at[name, slot])

    def far_copy(name, src, dst, slot):
        return remote(src, dst, far_send.at[name, slot], far_recv.at[name], "pipe", theirs)

    def h_copies(step):
        layer, at_rows, _, slot = placed(step)
        return [
            local_copy(0, h_buf.at[slot], h_out.at[layer, at_rows], slot),
            far_copy(0, h_buf.at[slot], h_far.at[layer, at_rows], slot),
        ]

    def q_copies(step):
        layer, at_rows, slot, _ = placed(step)
        return [local_copy(1, q_buf.at[slot], q_out.at[layer, at_rows], slot)]

    def logs_copies(step):
        layer, at_rows, slot, _ = placed(step)
        return [local_copy(2, logs_buf.at[slot], logs_out.at[layer, :, :, at_rows], slot)]

    def o_copies(step):
        layer, at_rows, _, slot = placed(step)
        return [
            local_copy(3, o_buf.at[slot], o_out.at[layer, at_rows], slot),
            far_copy(1, o_buf.at[slot, :, half(theirs, half_local)], o_far.at[layer, at_rows], slot),
            local_copy(4, o_buf.at[slot, :, half(core, half_local)], o_near.at[layer, at_rows], slot),
        ]

    def act_copies(step):
        layer, at_rows, slot, _ = placed(step)
        return [
            local_copy(5, act_buf.at[slot, :, half(core, half_hidden)], act_near.at[layer, at_rows], slot),
            far_copy(2, act_buf.at[slot, :, half(theirs, half_hidden)], act_far.at[layer, at_rows], slot),
            local_copy(6, slope_buf.at[slot], slope_out.at[layer, at_rows], slot),
        ]

    def start_all(copies):
        for item in copies:
            item.start()

    def left_all(copies):
        for i, item in enumerate(copies):
            if i == 1:
                item.wait_send()
            else:
                item.wait()

    def kv_copies(step):
        layer, chunk = lax.div(step, LINE), lax.rem(step, LINE)
        at_rows = chunk_rows(chunk)
        return [
            pltpu.make_async_copy(k_all.at[at_rows], k_out.at[layer, at_rows], slot4_sems.at[0, chunk]),
            pltpu.make_async_copy(v_all.at[at_rows], v_out.at[layer, at_rows], slot4_sems.at[1, chunk]),
        ]

    def x1_copy(chunk):
        at_rows = chunk_rows(chunk)
        return pltpu.make_async_copy(x1.at[at_rows], x1_out.at[at_rows], once_sems.at[0, chunk])

    def part_copy(chunk):
        at_rows = chunk_rows(chunk)
        return pltpu.make_async_copy(part.at[chunk], part_out.at[at_rows], once_sems.at[1, chunk])

    x_copy(0).start()
    greet(core, rank)
    for move in weight_moves:
        move.start()
    x_copy(1).start()

    keep = lax.broadcasted_iota(jnp.int32, (rows, rows), 1) <= lax.broadcasted_iota(
        jnp.int32, (rows, rows), 0
    )

    def attention(chunk, slot):
        def pair(j, _):
            lanes = pl.ds(pl.multiple_of(j * LANES, LANES), LANES)
            query = q_buf[slot, :, lanes]
            outs = []
            for which in range(LANES // HEAD_DIM):
                mask = head_mask(rows, which)
                mine = jnp.where(mask, query, jnp.zeros_like(query))
                scores = []
                if chunk:
                    scores.append(dot_nt(mine, k_all[0 : chunk * rows, lanes]))
                scores.append(
                    jnp.where(keep, dot_nt(mine, k_all[chunk * rows : (chunk + 1) * rows, lanes]), masked_score)
                )
                top = functools.reduce(
                    jnp.maximum, [jnp.max(item, axis=1, keepdims=True) for item in scores]
                )
                weights = [jnp.exp(item - top) for item in scores]
                total = functools.reduce(
                    jnp.add, [jnp.sum(item, axis=1, keepdims=True) for item in weights]
                )
                values = []
                if chunk:
                    values.append(v_all[0 : chunk * rows, lanes])
                values.append(v_all[chunk * rows : (chunk + 1) * rows, lanes])
                merged = functools.reduce(
                    jnp.add, [dot_nn(w.astype(BF), v) for w, v in zip(weights, values)]
                )
                outs.append(merged / total)
                logs_buf[slot, j, which : which + 1, :] = as_row(top + jnp.log(total))
            o_buf[chunk, :, lanes] = jnp.where(head_mask(rows, 0), outs[0], outs[1]).astype(BF)
            return 0

        lax.fori_loop(0, local // LANES, pair, 0)

    def go_on(step):
        @pl.when((step >= 1) & (step <= LINE))
        def _():
            summed.stage_b(step - 1)

        @pl.when((step >= 2) & (step <= LINE + 1))
        def _():
            summed.stage_d(step - 2)

        @pl.when((step >= 3) & (step <= LINE + 2))
        def _():
            summed.stage_e(step - 3, 1)

    def attention_part(step, _):
        layer, chunk = lax.div(step, LINE), lax.rem(step, LINE)
        slot = lax.rem(step, 2)
        at_rows = chunk_rows(chunk)

        @pl.when(step >= 2)
        def _():
            left_all(q_copies(step - 2))
            left_all(logs_copies(step - 2))

        @pl.when(step >= LINE)
        def _():
            left_all(h_copies(step - LINE))
            left_all(o_copies(step - LINE))

        small = rows // 8
        gain, shift = gain_ref[pl.ds(layer, 1), :], shift_ref[pl.ds(layer, 1), :]

        def normalise(load):
            def some(i, _):
                span = pl.ds(pl.multiple_of(i * small, small), small)
                values = load(span).astype(F32)
                centre = values - jnp.mean(values, axis=-1, keepdims=True)
                spread = jnp.mean(centre * centre, axis=-1, keepdims=True)
                h_buf[chunk, span, :] = (centre * lax.rsqrt(spread + ln_eps) * gain + shift).astype(BF)
                return 0

            lax.fori_loop(0, 8, some, 0)

        @pl.when(layer == 0)
        def _():
            x_copy(chunk).wait()
            x_share[chunk] = x_buf[slot, pl.ds(pl.multiple_of(rank * (rows // LINE), rows // LINE), rows // LINE)]
            normalise(lambda span: x_buf[slot, span, :])

            @pl.when(step + 2 < LINE)
            def _():
                x_copy(chunk + 2).start()

        @pl.when(step == 0)
        def _():
            fetch(0, 0)

        @pl.when(layer == 1)
        def _():
            summed.stage_f(chunk)
            x1_copy(chunk).start()
            base = chunk * rows
            normalise(lambda span: x1[pl.ds(pl.multiple_of(base + span.start, small), small), :])

        start_all(h_copies(step))

        @pl.when(chunk == 0)
        def _():
            fetched(0)

        @pl.when(layer == 1)
        def _():
            for item in kv_copies(step - LINE):
                item.wait()

        tables = (cos_ref[at_rows, :], near_ref[at_rows, :], far_ref[at_rows, :])
        h = h_buf[chunk]
        for part3 in range(3):
            value = dot_nn(h, vmem_w[0][part3]) + bias3_ref[pl.ds(layer * 3 + part3, 1), :]
            for j in range(local // LANES):
                lanes = slice(j * LANES, (j + 1) * LANES)
                if part3 == 0:
                    q_buf[slot, :, lanes] = (turn(value[:, lanes], *tables) * scale).astype(BF)
                elif part3 == 1:
                    k_all[at_rows, lanes] = turn(value[:, lanes], *tables).astype(BF)
                else:
                    v_all[at_rows, lanes] = value[:, lanes].astype(BF)
        start_all(q_copies(step))
        start_all(kv_copies(step))

        @pl.when(step == LINE - 1)
        def _():
            fetch(1, 0)

        @pl.when(layer == 1)
        def _():
            go_on(step)

        for index in range(LINE):

            @pl.when(chunk == index)
            def _():
                attention(index, slot)

        start_all(o_copies(step))
        start_all(logs_copies(step))

        @pl.when(step == jnp.where(core == 0, 0, LINE - 2))
        def _():
            fetch(0, 1)

        @pl.when(step == jnp.where(core == 0, 0, LINE - 1))
        def _():
            fetch(0, 2)

        return 0

    def hidden_part(step, _):
        layer, chunk = lax.div(step, LINE), lax.rem(step, LINE)
        slot = lax.rem(step, 2)

        @pl.when(step >= 2)
        def _():
            left_all(act_copies(step - 2))

        @pl.when(chunk == 0)
        def _():
            fetched(1)

        def up(i, _):
            cols = pl.ds(pl.multiple_of(i * tile, tile), tile)
            u = dot_nn(h_buf[chunk], vmem_w[1][:, cols]) + bias_u_ref[pl.ds(layer, 1), cols]
            square = u * u
            inner = jnp.tanh(u * (gelu_coef + (gelu_coef * 0.044715) * square))
            plus = 0.5 + 0.5 * inner
            act = u * plus
            act_buf[slot, :, cols] = act.astype(BF)
            slope_buf[slot, :, cols] = (
                plus + act * (1.0 - inner) * (gelu_coef + (3.0 * 0.044715 * gelu_coef) * square)
            ).astype(BF)
            return 0

        lax.fori_loop(0, hidden // tile, up, 0)
        start_all(act_copies(step))

        @pl.when(step == 0)
        def _():
            fetch(0, 3)

        @pl.when(step == LINE - 1)
        def _():
            fetch(1, 1)

        @pl.when(layer == 0)
        def _():
            go_on(step)

        @pl.when(chunk == 0)
        def _():
            fetched(2)
            fetched(3)

        @pl.when(layer == 1)
        def _():
            summed.sent_part(chunk)

        def down(i, _):
            cols = pl.ds(pl.multiple_of(i * tile, tile), tile)
            part[chunk, :, cols] = (
                dot_nn(o_buf[chunk], vmem_w[2][:, cols]) + dot_nn(act_buf[slot], vmem_w[3][:, cols])
            ).astype(BF)
            return 0

        lax.fori_loop(0, width // tile, down, 0)

        @pl.when(step == LINE - 1)
        def _():
            fetch(1, 2)
            fetch(1, 3)

        @pl.when(layer == 0)
        def _():
            summed.stage_a(chunk)

        @pl.when(layer == 1)
        def _():
            part_copy(chunk).start()

        @pl.when((step >= 1) & (step <= LINE))
        def _():
            summed.stage_c(step - 1)

        @pl.when((step >= 2) & (step <= LINE + 1))
        def _():
            summed.stage_e(step - 2, 0)

        return 0

    def whole_step(step, _):
        attention_part(step, 0)
        hidden_part(step, 0)
        return 0

    def first_layer(turn_, _):
        kind = jnp.where(core == 0, lax.rem(turn_, 2), lax.div(turn_, LINE))
        step = jnp.where(core == 0, lax.div(turn_, 2), lax.rem(turn_, LINE))

        @pl.when(kind == 0)
        def _():
            attention_part(step, 0)

        @pl.when(kind == 1)
        def _():
            hidden_part(step, 0)

        return 0

    lax.fori_loop(0, 2 * LINE, first_layer, 0)
    lax.fori_loop(LINE, STEPS, whole_step, 0)

    for step in range(STEPS - 2, STEPS):
        left_all(q_copies(step))
        left_all(logs_copies(step))
        left_all(act_copies(step))
    for step in range(LINE, STEPS):
        left_all(h_copies(step))
        left_all(o_copies(step))
        for item in kv_copies(step):
            item.wait()
    for chunk in range(LINE):
        x1_copy(chunk).wait()
        part_copy(chunk).wait()
        summed.sent_rest(chunk)
    for move in weight_moves:
        move.wait_send()
    for i, ref in enumerate((h_far, o_far, act_far)):
        remote(ref, ref, far_send.at[i, 0], far_recv.at[i], "pipe", theirs).wait_recv()


def forward_both(inputs, weights, vectors, tables):
    _, length, width = inputs.shape
    w_qkv, w_fc1, w_dense, w_fc2 = weights
    local, hidden = w_dense.shape[0], w_fc1.shape[1]
    rows = length // LINE
    pairs = local // LANES

    def bf(*shape):
        return jax.ShapeDtypeStruct(shape, BF)

    out_shape = [bf(*w.shape) for w in weights] + [
        bf(2, length, width),
        bf(2, length, width),
        bf(2, length, local),
        bf(2, length, local),
        bf(2, length, local),
        bf(2, length, local),
        bf(2, length, local // 2),
        bf(2, length, local // 2),
        bf(2, length, hidden // 2),
        bf(2, length, hidden // 2),
        bf(2, length, hidden),
        jax.ShapeDtypeStruct((2, pairs, 8, length), F32),
        bf(length, width),
        bf(length, width),
    ]
    whole = pl.BlockSpec(memory_space=pltpu.VMEM)
    away = pl.BlockSpec(memory_space=pl.ANY)
    dma = pltpu.SemaphoreType.DMA
    return pl.pallas_call(
        forward_kernel,
        name="forward_both",
        in_specs=[away] * 5 + [whole] * 8,
        out_specs=[away] * len(out_shape),
        out_shape=out_shape,
        scratch_shapes=[pltpu.VMEM(w.shape, BF) for w in weights]
        + [
            pltpu.VMEM((2, rows, width), BF),
            pltpu.VMEM((LINE, rows // LINE, width), BF),
            pltpu.VMEM((LINE, rows, width), BF),
            pltpu.VMEM((2, rows, hidden), BF),
            pltpu.VMEM((2, rows, hidden), BF),
            pltpu.VMEM((2, rows, local), BF),
            pltpu.VMEM((LINE, rows, local), BF),
            pltpu.VMEM((length, local), BF),
            pltpu.VMEM((length, local), BF),
            pltpu.VMEM((2, pairs, 8, rows), F32),
            pltpu.VMEM((LINE, rows, width), BF),
            pltpu.VMEM((length, width), BF),
        ]
        + line_sum_scratch(rows, width)
        + [
            dma((2, 4)),
            dma((4,)),
            dma((2,)),
            dma((7, LINE)),
            dma((2, LINE)),
            dma((3, LINE)),
            dma((3,)),
            dma((2, LINE)),
        ],
        compiler_params=pltpu.CompilerParams(
            collective_id=0, has_side_effects=True, vmem_limit_bytes=63 * MIB
        ),
        cost_estimate=pl.CostEstimate(
            flops=4 * length * width * (4 * local + 2 * hidden),
            bytes_accessed=200 * MIB,
            transcendentals=0,
        ),
    )(inputs, *weights, *vectors, *tables)


class PairDots:
    def __init__(self, core, dp_rank, dp_size, left_buf, right_buf, out_buf, sems, stages, received):
        self.core, self.me, self.dp = core, dp_rank, dp_size
        self.left_buf, self.right_buf, self.out_buf = left_buf, right_buf, out_buf
        self.left_sems, self.right_sems, self.out_sems, self.send_sems, self.recv_sems = sems
        self.stages, self.received = stages, received
        self.tokens = left_buf.shape[1] // 2
        self.keep = left_buf.shape[2]
        self.groups = {}

    def add(self, index, layer, kind, left, rights):
        total = sum(near.shape[-1] for near, _ in rights)
        widths = []
        while sum(widths) < total:
            widths.append(min(TILE, total - sum(widths)))
        self.groups[index] = (layer, kind, left, rights, widths)

    def tile(self, order):
        return lax.rem(self.me + 1 + order, self.dp)

    def left_copies(self, index, order):
        near, far = self.groups[index][2]
        slot = lax.rem(order, 2)
        cols = pl.ds(pl.multiple_of(self.tile(order) * self.keep, self.keep), self.keep)
        return [
            pltpu.make_async_copy(
                src.at[:, cols],
                self.left_buf.at[slot, i * self.tokens : (i + 1) * self.tokens],
                self.left_sems.at[i, slot],
            )
            for i, src in enumerate((near, far))
        ]

    def right_copies(self, index):
        copies = []
        base = 0
        for pair in self.groups[index][3]:
            width = pair[0].shape[-1]
            for i, src in enumerate(pair):
                target = self.right_buf.at[i * self.tokens : (i + 1) * self.tokens, base : base + width]
                copies.append(pltpu.make_async_copy(src, target, self.right_sems.at[len(copies)]))
            base += width
        return copies

    def prime(self, index):
        for item in self.left_copies(index, jnp.int32(0)) + self.right_copies(index):
            item.start()

    def out_copy(self, index, order, piece):
        layer, kind, _, _, widths = self.groups[index]
        base, width, slot = sum(widths[:piece]), widths[piece], piece % 2
        stage = self.stages[kind].at[layer, self.tile(order)]
        if kind:
            return pltpu.make_async_copy(
                self.out_buf.at[slot, 0 : self.keep, 0:width],
                stage.at[:, base : base + width],
                self.out_sems.at[slot],
            )
        return pltpu.make_async_copy(
            self.out_buf.at[slot, 0:width, 0 : self.keep],
            stage.at[base : base + width],
            self.out_sems.at[slot],
        )

    def send(self, index, order, act):
        layer, kind = self.groups[index][:2]
        tile = self.tile(order)
        src = self.stages[kind].at[layer, tile]
        dst = self.received[kind].at[self.core, self.me]
        at_home = (self.core == layer) & (tile == self.me)

        @pl.when(at_home)
        def _():
            copy = pltpu.make_async_copy(src, dst, self.send_sems.at[index, order])
            copy.start() if act == "start" else copy.wait()

        @pl.when(jnp.logical_not(at_home))
        def _():
            copy = pltpu.make_async_remote_copy(
                src_ref=src,
                dst_ref=dst,
                send_sem=self.send_sems.at[index, order],
                recv_sem=self.recv_sems.at[kind, self.core],
                device_id={"pipe": jnp.int32(layer), "dp": tile},
                device_id_type=pl.DeviceIdType.MESH,
            )
            copy.start() if act == "start" else copy.wait_send()

    def run(self, index, start, stop):
        _, kind, _, _, widths = self.groups[index]

        def one(order, _):
            slot = lax.rem(order, 2)
            for item in self.left_copies(index, order):
                item.wait()

            @pl.when(order == 0)
            def _():
                for item in self.right_copies(index):
                    item.wait()

            @pl.when(order + 1 < self.dp)
            def _():
                for item in self.left_copies(index, order + 1):
                    item.start()

            base = 0
            for piece, width in enumerate(widths):
                if piece >= 2:
                    self.out_copy(index, order, piece - 2).wait()
                left, right = self.left_buf[slot], self.right_buf[:, base : base + width]
                if kind:
                    self.out_buf[piece % 2, 0 : self.keep, 0:width] = dot_tn(left, right).astype(BF)
                else:
                    self.out_buf[piece % 2, 0:width, 0 : self.keep] = dot_tn(right, left).astype(BF)
                self.out_copy(index, order, piece).start()
                base += width
            for piece in range(max(0, len(widths) - 2), len(widths)):
                self.out_copy(index, order, piece).wait()
            self.send(index, order, "start")
            return 0

        lax.fori_loop(start, stop, one, 0)

    def all_sent(self, index):
        def one(order, _):
            self.send(index, order, "wait")
            return 0

        lax.fori_loop(0, self.dp, one, 0)

    def all_received(self, kind):
        ref = self.received[kind]
        theirs = ref.at[1 - self.core]
        ours = ref.at[self.core, pl.ds(0, self.dp - 1)]
        remote(theirs, theirs, self.send_sems.at[0, 0], self.recv_sems.at[kind, 1 - self.core], "pipe", 1 - self.core).wait_recv()
        if self.dp > 1:
            remote(ours, ours, self.send_sems.at[0, 0], self.recv_sems.at[kind, self.core], "pipe", 1 - self.core).wait_recv()


class SmallSums:
    def __init__(self, core, rank, dp_rank, dp_size, sums, from_peers, from_line, final, sems):
        self.core, self.rank, self.me, self.dp = core, rank, dp_rank, dp_size
        self.sums, self.from_peers, self.from_line, self.final = sums, from_peers, from_line, final
        self.peer_send, self.peer_recv, self.line_send, self.line_recv = sems

    def to_peer(self, layer, other, act):
        src = self.sums.at[layer]
        dst = self.from_peers.at[self.core, self.me]
        sem = self.peer_send.at[layer, other]
        at_home = (self.core == layer) & (other == self.me)

        @pl.when(at_home)
        def _():
            copy = pltpu.make_async_copy(src, dst, sem)
            copy.start() if act == "start" else copy.wait()

        @pl.when(jnp.logical_not(at_home))
        def _():
            copy = pltpu.make_async_remote_copy(
                src_ref=src,
                dst_ref=dst,
                send_sem=sem,
                recv_sem=self.peer_recv.at[self.core],
                device_id={"pipe": jnp.int32(layer), "dp": other},
                device_id_type=pl.DeviceIdType.MESH,
            )
            copy.start() if act == "start" else copy.wait_send()

    def peers(self, act):
        for layer in range(2):

            def one(other, _):
                self.to_peer(layer, other, act)
                return 0

            lax.fori_loop(0, self.dp, one, 0)

    def line_copy(self, other):
        return remote(
            self.from_line.at[LINE],
            self.from_line.at[self.rank],
            self.line_send.at[other],
            self.line_recv.at[self.rank],
            "tensor",
            other,
        )

    def pass_on(self):
        self.peers("wait")
        theirs = self.from_peers.at[1 - self.core]
        remote(theirs, theirs, self.peer_send.at[0, 0], self.peer_recv.at[1 - self.core], "pipe", 1 - self.core).wait_recv()
        if self.dp > 1:
            ours = self.from_peers.at[self.core, pl.ds(0, self.dp - 1)]
            remote(ours, ours, self.peer_send.at[0, 0], self.peer_recv.at[self.core], "pipe", 1 - self.core).wait_recv()
        total = self.from_peers[0, 0] + self.from_peers[1, 0]
        for i in range(1, self.dp):
            total = total + (self.from_peers[0, i] + self.from_peers[1, i])
        self.from_line[LINE] = total
        for other in range(LINE):

            @pl.when(self.rank != other)
            def _():
                self.line_copy(other).start()

    def finish(self):
        own = self.from_line[LINE]
        self.final[2:8, :] = own[2:8, :]
        self.final[0:2, :] = own[0:2, :]
        for other in range(LINE):

            @pl.when(self.rank != other)
            def _():
                self.line_copy(other).wait_send()
                block = self.from_line.at[other]
                remote(
                    block, block, self.line_send.at[other], self.line_recv.at[other], "tensor", other
                ).wait_recv()
                self.final[0:2, :] += self.from_line[other, 0:2, :]


RING = 3


def backward_kernel(dp_size, *refs):
    at = 0

    def take(count):
        nonlocal at
        at += count
        return refs[at - count : at]

    cot_ref, in_ref, x1_ref, part1_ref = take(4)
    slope_ref, q_ref, k_ref, v_ref, o_ref, logs_ref = take(6)
    own_w = take(4)
    other_w = take(4)
    h_near, h_far, act_near, act_far, o_near, o_far = take(6)
    gain_ref, bias_o_ref, cos_ref, near_ref, far_ref = take(5)
    acts_out, grads_out, dy0_out, dy0_far, du_near, du_far, dp_near, dp_far = take(8)
    stages = take(2)
    received = take(2)
    (final_ref,) = take(1)
    ring, ring_qkv, dense_w = take(3)
    up_buf, x_buf, slope_buf, q_buf, o_buf, logs_buf = take(6)
    k_all, v_all, dk_all, dv_all = take(4)
    do_buf, dp_buf, du_buf, part = take(4)
    mean_buf, inverse_buf, up_share, x_share = take(4)
    (result,) = take(1)
    sum_bufs = take(4)
    sum_sems = dict(zip(SUM_NAMES, take(6)))
    share_room, left_sems, right_sems, left1_sems, right1_sems, free_sem = take(6)
    dot_bufs = take(3)
    dot_sems = take(5)
    ring_sems, qkv_sems, dense_sem, load_sems, kv_sems, out_sems = take(6)
    far_send, far_recv, once_sems, result_send, grads_sems, acts_sems = take(6)
    sums_ref, from_peers, from_line = take(3)
    small_sems = take(4)
    assert at == len(refs)
    w_qkv, w_fc1, w_dense, w_fc2 = range(4)
    core = lax.axis_index("pipe")
    rank = lax.axis_index("tensor")
    dp_rank = lax.axis_index("dp")
    theirs = 1 - core
    rows, width = up_buf.shape
    block = rows // LINE
    local = q_buf.shape[2]
    hidden = du_buf.shape[1]
    half_hidden, half_local = hidden // 2, local // 2
    tile = ring.shape[1]
    up_tiles, out_tiles = hidden // tile, width // tile
    ring_tiles = up_tiles + out_tiles
    scale = HEAD_DIM ** (-0.5)

    def layer_of(step):
        return 1 - lax.div(step, LINE)

    def chunk_of(step):
        return LINE - 1 - lax.rem(step, LINE)

    def chunk_rows(chunk):
        return pl.ds(pl.multiple_of(chunk * rows, rows), rows)

    def weight_copy(layer, views, target, sem, act):
        if act == "wait":
            pltpu.make_async_copy(views[0], target, sem).wait()
            return

        @pl.when(core == layer)
        def _():
            pltpu.make_async_copy(views[0], target, sem).start()

        @pl.when(core != layer)
        def _():
            pltpu.make_async_copy(views[1], target, sem).start()

    def ring_copy(index, act):
        step, place = lax.div(index, ring_tiles), lax.rem(index, ring_tiles)
        slot = lax.rem(index, RING)
        target, sem = ring.at[slot], ring_sems.at[slot]
        layer = layer_of(step)
        if act == "wait":
            weight_copy(layer, [own_w[w_fc2].at[0:tile]], target, sem, act)
            return

        @pl.when(place < up_tiles)
        def _():
            span = pl.ds(pl.multiple_of(place * tile, tile), tile)
            weight_copy(layer, [own_w[w_fc2].at[span], other_w[w_fc2].at[span]], target, sem, act)

        @pl.when(place >= up_tiles)
        def _():
            span = pl.ds(pl.multiple_of((place - up_tiles) * tile, tile), tile)
            weight_copy(layer, [own_w[w_fc1].at[span], other_w[w_fc1].at[span]], target, sem, act)

    def qkv_copy(index, act):
        step, place = lax.div(index, out_tiles), lax.rem(index, out_tiles)
        slot = lax.rem(index, 2)
        span = pl.ds(pl.multiple_of(place * tile, tile), tile)
        views = [w[w_qkv].at[:, span, :] for w in (own_w, other_w)]
        weight_copy(layer_of(step), views, ring_qkv.at[slot], qkv_sems.at[slot], act)

    def dense_copy(layer, act):
        weight_copy(layer, [own_w[w_dense], other_w[w_dense]], dense_w, dense_sem.at[0], act)

    def kv_copies(layer):
        return [
            pltpu.make_async_copy(k_ref.at[layer], k_all, kv_sems.at[0]),
            pltpu.make_async_copy(v_ref.at[layer], v_all, kv_sems.at[1]),
        ]

    def early_loads(step):
        layer, slot = layer_of(step), 0
        at_rows = chunk_rows(chunk_of(step))
        return [
            pltpu.make_async_copy(q_ref.at[layer, at_rows], q_buf.at[slot], load_sems.at[0, slot]),
            pltpu.make_async_copy(o_ref.at[layer, at_rows], o_buf.at[slot], load_sems.at[1, slot]),
            pltpu.make_async_copy(
                logs_ref.at[layer, :, :, at_rows], logs_buf.at[slot], load_sems.at[2, slot]
            ),
        ]

    def slope_load(step):
        return pltpu.make_async_copy(
            slope_ref.at[layer_of(step), chunk_rows(chunk_of(step))], slope_buf, load_sems.at[3, 0]
        )

    def x_load(src):
        return pltpu.make_async_copy(src, x_buf, load_sems.at[4, 0])

    def up_load(src):
        return pltpu.make_async_copy(src, up_buf, load_sems.at[5, 0])

    def norm_back(layer, rows_x, rows_up, total):
        values = rows_x.astype(F32)
        centre = values - jnp.mean(values, axis=-1, keepdims=True)
        inverse = lax.rsqrt(jnp.mean(centre * centre, axis=-1, keepdims=True) + ln_eps)
        xhat = centre * inverse
        e = total * gain_ref[layer : layer + 1, :]
        back = e - jnp.mean(e, axis=-1, keepdims=True) - xhat * jnp.mean(
            e * xhat, axis=-1, keepdims=True
        )
        return (rows_up.astype(F32) + inverse * back).astype(BF)

    def finish(chunk, total, target):
        target[...] = norm_back(1, x_share[chunk], up_share[chunk], total)

    summed = LineSum(rank, part, *sum_bufs, result, sum_sems, finish)
    shared = LineShare(rank, part, share_room, (left_sems, right_sems), out_tiles)
    dots = PairDots(core, dp_rank, dp_size, *dot_bufs, dot_sems, stages, received)
    shared1 = LineShare(rank, part, share_room, (left1_sems, right1_sems), out_tiles)
    smalls = SmallSums(
        core, rank, dp_rank, dp_size, sums_ref, from_peers, from_line, final_ref, small_sems
    )
    dots.add(0, 1, 0, (cot_ref.at[core], cot_ref.at[theirs]), [(act_near.at[1], act_far.at[1]), (o_near.at[1], o_far.at[1])])
    dots.add(2, 0, 0, (dy0_out, dy0_far), [(act_near.at[0], act_far.at[0]), (o_near.at[0], o_far.at[0])])
    for index, layer in ((1, 1), (3, 0)):
        dots.add(
            index,
            layer,
            1,
            (h_near.at[layer], h_far.at[layer]),
            [(du_near.at[layer], du_far.at[layer])]
            + [(dp_near.at[layer, c], dp_far.at[layer, c]) for c in range(3)],
        )

    def half(which, size):
        return pl.ds(pl.multiple_of(which * size, size), size)

    def dp_copies(step):
        layer, at_rows = layer_of(step), chunk_rows(chunk_of(step))
        return [
            pltpu.make_async_copy(
                dp_buf.at[:, :, half(core, half_local)], dp_near.at[layer, :, at_rows], out_sems.at[0]
            ),
            remote(
                dp_buf.at[:, :, half(theirs, half_local)],
                dp_far.at[layer, :, at_rows],
                far_send.at[0],
                far_recv.at[0, layer],
                "pipe",
                theirs,
            ),
        ]

    def du_copies(step):
        layer, at_rows = layer_of(step), chunk_rows(chunk_of(step))
        return [
            pltpu.make_async_copy(
                du_buf.at[:, half(core, half_hidden)], du_near.at[layer, at_rows], out_sems.at[1]
            ),
            remote(
                du_buf.at[:, half(theirs, half_hidden)],
                du_far.at[layer, at_rows],
                far_send.at[1],
                far_recv.at[1, layer],
                "pipe",
                theirs,
            ),
        ]

    def result_copies(chunk):
        at_rows = chunk_rows(chunk)
        return [
            pltpu.make_async_copy(result.at[at_rows], dy0_out.at[at_rows], once_sems.at[chunk]),
            remote(
                result.at[at_rows],
                dy0_far.at[at_rows],
                result_send.at[chunk],
                far_recv.at[2, 0],
                "pipe",
                theirs,
            ),
        ]

    def start_all(copies):
        for item in copies:
            item.start()

    def left_all(copies):
        copies[0].wait()
        copies[1].wait_send()

    def far_arrived(i, layer, ref):
        remote(ref, ref, far_send.at[0], far_recv.at[i, layer], "pipe", theirs).wait_recv()

    dense_copy(1, "start")
    up_load(cot_ref.at[core, (LINE - 1) * rows : LINE * rows]).start()
    start_all(early_loads(jnp.int32(0)))
    start_all(kv_copies(1))
    for i in range(RING - 1):
        ring_copy(jnp.int32(i), "start")
    qkv_copy(jnp.int32(0), "start")
    dots.prime(0)

    barrier = pltpu.get_barrier_semaphore()

    def tell(where):
        pl.semaphore_signal(barrier, inc=1, device_id=where, device_id_type=pl.DeviceIdType.MESH)

    def tell_peer(other, _):
        tell({"pipe": theirs, "dp": other})

        @pl.when(other != dp_rank)
        def _():
            tell({"dp": other})

        return 0

    lax.fori_loop(0, dp_size, tell_peer, 0)

    for other in range(LINE):

        @pl.when(rank != other)
        def _():
            tell({"tensor": jnp.int32(other)})

    pl.semaphore_wait(barrier, 2 * dp_size - 1 + LINE - 1)

    sums_ref[...] = jnp.zeros_like(sums_ref)

    keep = lax.broadcasted_iota(jnp.int32, (rows, rows), 0) <= lax.broadcasted_iota(
        jnp.int32, (rows, rows), 1
    )

    def attention(chunk, slot):
        here = slice(chunk * rows, (chunk + 1) * rows)
        spans = ([(slice(0, chunk * rows), False)] if chunk else []) + [(here, True)]
        tables = (cos_ref[here, :], -near_ref[here, :], -far_ref[here, :])

        def pair(j, _):
            lanes = pl.ds(pl.multiple_of(j * LANES, LANES), LANES)
            query, upstream = q_buf[slot, :, lanes], do_buf[:, lanes]
            product = upstream.astype(F32) * o_buf[slot, :, lanes].astype(F32)
            grads = []
            key_terms = [None] * len(spans)
            value_terms = [None] * len(spans)
            for which in range(LANES // HEAD_DIM):
                mask = head_mask(rows, which)
                mine = jnp.where(mask, query, jnp.zeros_like(query))
                mine_up = jnp.where(mask, upstream, jnp.zeros_like(upstream))
                logs = logs_buf[slot, j, which : which + 1, :]
                centre = as_row(jnp.sum(jnp.where(mask, product, 0.0), axis=1, keepdims=True))
                grad = None
                for i, (span, diagonal) in enumerate(spans):
                    keys = k_all[span, lanes]
                    probs = jnp.exp(dot_nt(keys, mine) - logs)
                    if diagonal:
                        probs = jnp.where(keep, probs, 0.0)
                    grad_probs = dot_nt(v_all[span, lanes], mine_up)
                    grad_scores = (probs * (grad_probs - centre)).astype(BF)
                    value_term = dot_nn(probs.astype(BF), mine_up)
                    key_term = dot_nn(grad_scores, mine)
                    term = dot_tn(grad_scores, keys)
                    grad = term if grad is None else grad + term
                    if which == 0:
                        key_terms[i], value_terms[i] = key_term, value_term
                    else:
                        dk_all[span, lanes] += key_terms[i] + key_term
                        dv_all[span, lanes] += value_terms[i] + value_term
                grads.append(grad)
            merged = jnp.where(head_mask(rows, 0), grads[0], grads[1]) * scale
            dp_buf[0, :, lanes] = turn(merged, *tables).astype(BF)
            dp_buf[1, :, lanes] = turn(dk_all[here, lanes], *tables).astype(BF)
            dp_buf[2, :, lanes] = dv_all[here, lanes].astype(BF)
            return 0

        lax.fori_loop(0, local // LANES, pair, 0)


    def step_body(step, _):
        layer, chunk, slot = layer_of(step), chunk_of(step), 0
        lead = layer == 1
        starting = lax.rem(step, LINE) == 0
        at_rows = chunk_rows(chunk)

        @pl.when(step == LINE)
        def _():
            left_all(dp_copies(step - 1))
            left_all(du_copies(step - 1))
            far_arrived(0, 1, dp_far.at[1])
            far_arrived(1, 1, du_far.at[1])
            dots.prime(1)

        @pl.when(step >= LINE)
        def _():
            summed.stage_f(chunk)
            start_all(result_copies(chunk))
            up_buf[...] = result[at_rows, :]
            x_load(in_ref.at[core, at_rows]).start()

        @pl.when(lead)
        def _():
            up_load(cot_ref.at[core, at_rows]).wait()
            x_load(x1_ref.at[at_rows]).start()

        slope_load(step).start()

        @pl.when(starting)
        def _():
            dense_copy(layer, "wait")
            dk_all[...] = jnp.zeros_like(dk_all)
            dv_all[...] = jnp.zeros_like(dv_all)

        slope_load(step).wait()

        @pl.when((step >= 1) & (step != LINE))
        def _():
            left_all(du_copies(step - 1))

        def hidden_part(i, _):
            cols = pl.ds(pl.multiple_of(i * tile, tile), tile)
            index = step * ring_tiles + i
            ring_copy(index, "wait")
            ring_copy(index + RING - 1, "start")
            weight = ring.at[lax.rem(index, RING)]
            value = dot_nt(up_buf[...], weight[...]) * slope_buf[:, cols].astype(F32)
            value = value.astype(BF)
            du_buf[:, cols] = value
            sums_ref[layer, 2:3, cols] += jnp.sum(value.astype(F32), axis=0, keepdims=True)
            return 0

        lax.fori_loop(0, up_tiles, hidden_part, 0)
        start_all(du_copies(step))

        @pl.when(step == STEPS - 1)
        def _():
            for c in range(LINE):
                left_all(result_copies(c))
            far_arrived(2, 0, dy0_far)
            dots.prime(2)

        do_buf[...] = dot_nt(up_buf[...], dense_w[...]).astype(BF)

        @pl.when(step == LINE - 1)
        def _():
            dense_copy(jnp.int32(0), "start")

        sums_ref[layer, 3:4, :] += jnp.sum(up_buf[...].astype(F32), axis=0, keepdims=True)

        @pl.when(lead)
        def _():
            up_share[chunk] = up_buf[pl.ds(pl.multiple_of(rank * block, block), block), :]

        @pl.when(step + 1 < LINE)
        def _():
            up_load(cot_ref.at[core, chunk_rows(chunk - 1)]).start()

        for item in early_loads(step):
            item.wait()

        @pl.when(starting)
        def _():
            for item in kv_copies(layer):
                item.wait()

        @pl.when((step >= 1) & (step != LINE))
        def _():
            left_all(dp_copies(step - 1))

        for index in range(LINE):

            @pl.when(chunk == index)
            def _():
                attention(index, slot)

        start_all(dp_copies(step))

        @pl.when(step + 1 < STEPS)
        def _():
            start_all(early_loads(step + 1))

        @pl.when(step == LINE - 1)
        def _():
            start_all(kv_copies(jnp.int32(0)))

        for i in range(3):
            sums_ref[layer, 4 + i : 5 + i, 0:local] += jnp.sum(
                dp_buf[i].astype(F32), axis=0, keepdims=True
            )

        @pl.when((step >= 1) & (step <= LINE))
        def _():
            summed.stage_b(chunk_of(step - 1))

        @pl.when((step >= 2) & (step <= LINE + 1))
        def _():
            summed.stage_d(chunk_of(step - 2))

        @pl.when((step >= 3) & (step <= LINE + 2))
        def _():
            summed.stage_e(chunk_of(step - 3), 1)

        @pl.when(step > LINE)
        def _():
            shared.relay(chunk_of(step - 1), 1)

        @pl.when(lead)
        def _():
            dots.run(0, lax.div(step * dp_size, LINE), lax.div((step + 1) * dp_size, LINE))

        @pl.when((step >= LINE) & (step < STEPS - 1))
        def _():
            begin = jnp.where(step == LINE, 0, lax.div((step - LINE + 1) * dp_size, LINE))
            dots.run(1, begin, lax.div((step - LINE + 2) * dp_size, LINE))

        @pl.when(step == STEPS - 1)
        def _():
            dots.run(2, 0, dp_size)
            left_all(dp_copies(step))
            left_all(du_copies(step))
            far_arrived(0, 0, dp_far.at[0])
            far_arrived(1, 0, du_far.at[0])
            dots.prime(3)

        x_load(x1_ref.at[at_rows]).wait()
        small = rows // 8

        def statistics(i, _):
            span = pl.ds(pl.multiple_of(i * small, small), small)
            values = x_buf[span, :].astype(F32)
            mean = jnp.mean(values, axis=-1, keepdims=True)
            centre = values - mean
            mean_buf[span, :] = mean
            inverse_buf[span, :] = lax.rsqrt(
                jnp.mean(centre * centre, axis=-1, keepdims=True) + ln_eps
            )
            return 0

        lax.fori_loop(0, 8, statistics, 0)

        @pl.when(lead)
        def _():
            x_share[chunk] = x_buf[pl.ds(pl.multiple_of(rank * block, block), block), :]

        @pl.when(jnp.logical_not(lead))
        def _():
            summed.sent_part(chunk)

        def normed_part(i, _):
            cols = pl.ds(pl.multiple_of(i * tile, tile), tile)
            index = step * ring_tiles + up_tiles + i
            ring_copy(index, "wait")

            @pl.when(index + RING - 1 < STEPS * ring_tiles)
            def _():
                ring_copy(index + RING - 1, "start")

            qkv_index = step * out_tiles + i
            qkv_copy(qkv_index, "wait")

            @pl.when(qkv_index + 1 < STEPS * out_tiles)
            def _():
                qkv_copy(qkv_index + 1, "start")

            value = dot_nt(du_buf[...], ring[lax.rem(index, RING)])
            for c in range(3):
                value = value + dot_nt(dp_buf[c], ring_qkv[lax.rem(qkv_index, 2), c])
            xhat = (x_buf[:, cols].astype(F32) - mean_buf[...]) * inverse_buf[...]
            sums_ref[layer, 0:1, cols] += jnp.sum(value * xhat, axis=0, keepdims=True)
            sums_ref[layer, 1:2, cols] += jnp.sum(value, axis=0, keepdims=True)
            part[chunk, :, cols] = value.astype(BF)

            @pl.when(jnp.logical_not(lead))
            def _():
                shared.emit(chunk, i)

            return 0

        lax.fori_loop(0, out_tiles, normed_part, 0)

        @pl.when(lead)
        def _():
            summed.stage_a(chunk)

        @pl.when((step >= 1) & (step <= LINE))
        def _():
            summed.stage_c(chunk_of(step - 1))

        @pl.when((step >= 2) & (step <= LINE + 1))
        def _():
            summed.stage_e(chunk_of(step - 2), 0)

        @pl.when(step > LINE)
        def _():
            shared.relay(chunk_of(step - 1), 2)

        return 0

    lax.fori_loop(0, STEPS, step_body, 0)

    smalls.peers("start")
    mine = chunk_rows(rank)
    deliver(core, 1, result.at[mine], grads_out, grads_sems, "start")
    deliver(core, 0, x1_ref.at[mine], acts_out, acts_sems, "start")
    reload = [up_load(result.at[mine]), x_load(in_ref.at[core, mine])]
    start_all(reload)
    some = dp_size // 2
    dots.run(3, 0, some)
    shared.relay(0, 1)
    dots.run(3, some, dp_size)
    shared.relay(0, 2)
    smalls.pass_on()
    shared.arrived()
    for item in reload:
        item.wait()
    small = rows // 8

    def last(i, _):
        span = pl.ds(pl.multiple_of(i * small, small), small)
        up_buf[span, :] = norm_back(0, x_buf[span, :], up_buf[span, :], shared.total(span))
        return 0

    lax.fori_loop(0, 8, last, 0)
    deliver(core, 0, up_buf, grads_out, grads_sems, "start")
    for chunk in range(LINE):
        shared.sent(chunk)

    x1_mine = x_load(x1_ref.at[mine])
    x1_mine.start()
    part_loads = [
        pltpu.make_async_copy(
            part1_ref.at[c * rows : (c + 1) * rows], part.at[c], once_sems.at[c]
        )
        for c in range(LINE)
    ]
    start_all(part_loads)
    for offset in (-1, 1):
        other = rank + offset

        @pl.when((other >= 0) & (other < LINE))
        def _():
            pl.semaphore_signal(
                free_sem, inc=1, device_id={"tensor": other}, device_id_type=pl.DeviceIdType.MESH
            )

    for item in part_loads:
        item.wait()
    pl.semaphore_wait(
        free_sem, jnp.where(rank > 0, 1, 0) + jnp.where(rank < LINE - 1, 1, 0)
    )
    for chunk in (3, 0, 2, 1):

        def emit(piece, _):
            shared1.emit(chunk, piece)
            return 0

        lax.fori_loop(0, out_tiles, emit, 0)
    smalls.finish()
    for hop in (1, 2):
        for chunk in (3, 0, 2, 1):
            shared1.relay(chunk, hop)
    shared1.arrived()
    x1_mine.wait()
    deliver(core, 0, up_buf, grads_out, grads_sems, "wait")

    def last_rows(i, _):
        span = pl.ds(pl.multiple_of(i * small, small), small)
        value = x_buf[span, :].astype(F32) + shared1.total(span) + bias_o_ref[1:2, :]
        up_buf[span, :] = value.astype(BF)
        return 0

    lax.fori_loop(0, 8, last_rows, 0)
    deliver(core, 1, up_buf, acts_out, acts_sems, "start")
    deliver(core, 1, result.at[mine], grads_out, grads_sems, "wait")
    deliver(core, 0, x1_ref.at[mine], acts_out, acts_sems, "wait")
    deliver(core, 1, up_buf, acts_out, acts_sems, "wait")
    delivered(core, grads_out, grads_sems)
    delivered(core, acts_out, acts_sems)
    for chunk in range(LINE):
        summed.sent_rest(chunk)
        shared1.sent(chunk)
    for index in range(4):
        dots.all_sent(index)
    for kind in range(2):
        dots.all_received(kind)


def backward_both(
    dp_size, cotangent, inputs, x1, part1, saved, own_w, other_w, sides, gains, bias_o, tables
):
    slope, query, key, value, merged, logs = saved
    _, length, width = inputs.shape
    w_qkv, w_fc1, w_dense, w_fc2 = own_w
    local, hidden = w_dense.shape[0], w_fc1.shape[1]
    rows = length // LINE
    block = rows // LINE
    pairs = local // LANES
    tile = min(TILE, width)
    out_tiles = width // tile
    keep = width // dp_size
    down, up = hidden // 2 + local // 2, hidden // 2 + 3 * (local // 2)

    def bf(*shape):
        return jax.ShapeDtypeStruct(shape, BF)

    def room(*shape):
        return pltpu.VMEM(shape, BF)

    whole = pl.BlockSpec(memory_space=pltpu.VMEM)
    away = pl.BlockSpec(memory_space=pl.ANY)
    dma = pltpu.SemaphoreType.DMA
    outs = [
        bf(2, rows, width),
        bf(2, rows, width),
        bf(length, width),
        bf(length, width),
        bf(2, length, hidden // 2),
        bf(2, length, hidden // 2),
        bf(2, 3, length, local // 2),
        bf(2, 3, length, local // 2),
        bf(2, dp_size, down, keep),
        bf(2, dp_size, keep, up),
        bf(2, dp_size, down, keep),
        bf(2, dp_size, keep, up),
    ]
    most = max(width, hidden)
    return pl.pallas_call(
        functools.partial(backward_kernel, dp_size),
        name="backward_both",
        in_specs=[away] * 24 + [whole] * 5,
        out_specs=[away] * len(outs) + [whole],
        out_shape=outs + [jax.ShapeDtypeStruct((8, most), F32)],
        scratch_shapes=[
            room(RING, tile, width),
            room(2, 3, tile, local),
            room(local, width),
            room(rows, width),
            room(rows, width),
            room(rows, hidden),
            room(1, rows, local),
            room(1, rows, local),
            pltpu.VMEM((1, pairs, 8, rows), F32),
            room(length, local),
            room(length, local),
            pltpu.VMEM((length, local), F32),
            pltpu.VMEM((length, local), F32),
            room(rows, local),
            room(3, rows, local),
            room(rows, hidden),
            room(LINE, rows, width),
            pltpu.VMEM((rows, 1), F32),
            pltpu.VMEM((rows, 1), F32),
            room(LINE, block, width),
            room(LINE, block, width),
            room(length, width),
        ]
        + line_sum_scratch(rows, width)
        + [room(LINE + 1, rows, width)]
        + [dma((2, LINE * out_tiles))] * 4
        + [pltpu.SemaphoreType.REGULAR]
        + [
            room(2, 2 * length, keep),
            room(2 * length, max(down, up)),
            room(2, max(keep, TILE), max(keep, TILE)),
            dma((2, 2)),
            dma((8,)),
            dma((2,)),
            dma((4, dp_size)),
            dma((2, 2)),
        ]
        + [
            dma((RING,)),
            dma((2,)),
            dma((1,)),
            dma((6, 2)),
            dma((2,)),
            dma((2,)),
            dma((2,)),
            dma((3, 2)),
            dma((LINE,)),
            dma((LINE,)),
            dma((3,)),
            dma((3,)),
            pltpu.VMEM((2, 8, most), F32),
            pltpu.VMEM((2, dp_size, 8, most), F32),
            pltpu.VMEM((LINE + 1, 8, most), F32),
            dma((2, dp_size)),
            dma((2,)),
            dma((LINE,)),
            dma((LINE,)),
        ],
        compiler_params=pltpu.CompilerParams(
            collective_id=1, has_side_effects=True, vmem_limit_bytes=63 * MIB
        ),
        cost_estimate=pl.CostEstimate(
            flops=16 * length * width * (4 * local + 2 * hidden),
            bytes_accessed=400 * MIB,
            transcendentals=0,
        ),
    )(
        cotangent, inputs, x1, part1, slope, query, key, value, merged, logs, *own_w, *other_w, *sides, gains, bias_o, *tables
    )


def down_kernel(got_ref, wide_ref, narrow_ref):
    total = jnp.sum(got_ref[0].astype(F32), axis=0)
    last = pl.num_programs(1) - 1

    @pl.when(pl.program_id(1) < last)
    def _():
        wide_ref[...] = total

    @pl.when(pl.program_id(1) == last)
    def _():
        narrow_ref[...] = total


def down_total(got, hidden, local):
    _, peers, _, keep = got.shape
    side = local // 2
    blocks = hidden // 2 // side
    return pl.pallas_call(
        down_kernel,
        name="down_total",
        grid=(2, blocks + 1),
        in_specs=[pl.BlockSpec((1, peers, side, keep), lambda part, i: (part, 0, i, 0))],
        out_specs=[
            pl.BlockSpec((side, keep), lambda part, i: (part * blocks + jnp.minimum(i, blocks - 1), 0)),
            pl.BlockSpec((side, keep), lambda part, i: (part, 0)),
        ],
        out_shape=[
            jax.ShapeDtypeStruct((hidden, keep), F32),
            jax.ShapeDtypeStruct((local, keep), F32),
        ],
    )(got)


def up_kernel(got_ref, wide_ref, three_ref):
    total = jnp.sum(got_ref[0].astype(F32), axis=0)
    cut, side = wide_ref.shape[1], three_ref.shape[2]
    wide_ref[...] = total[:, :cut]
    for c in range(3):
        three_ref[c] = total[:, cut + c * side : cut + (c + 1) * side]


def up_total(got, hidden, local):
    _, peers, keep, cols = got.shape
    some = min(64, keep)
    return pl.pallas_call(
        up_kernel,
        name="up_total",
        grid=(2, keep // some),
        in_specs=[pl.BlockSpec((1, peers, some, cols), lambda part, i: (part, 0, i, 0))],
        out_specs=[
            pl.BlockSpec((some, hidden // 2), lambda part, i: (i, part)),
            pl.BlockSpec((3, some, local // 2), lambda part, i: (0, i, part)),
        ],
        out_shape=[
            jax.ShapeDtypeStruct((keep, hidden), F32),
            jax.ShapeDtypeStruct((3, keep, local), F32),
        ],
    )(got)


def body(
    inputs, cotangent, ln_gain, ln_bias, w_qkv, b_qkv, w_dense, b_dense, w_fc1, b_fc1, w_fc2, b_fc2
):
    core = lax.axis_index("pipe")
    rank = lax.axis_index("tensor")
    dp_size = lax.axis_size("dp")
    dp_rank = lax.axis_index("dp")
    first = core == 0
    _, length, width = inputs.shape
    lines = lax.axis_size("tensor")
    local = w_qkv.shape[3]
    hidden = w_fc1.shape[2]

    def both(own):
        other = lax.ppermute(own, "pipe", [(0, 1), (1, 0)])
        return (jnp.where(first, own, other), jnp.where(first, other, own))

    small = jnp.concatenate(
        [ln_gain[0], ln_bias[0], b_qkv[0].reshape(-1), b_dense[0], b_fc1[0], b_fc2[0]]
    )
    small_both = jnp.stack(both(small)).astype(F32)
    vectors = []
    at = 0
    for count in (width, width, 3 * local, width, hidden, width):
        vectors.append(small_both[:, at : at + count])
        at += count
    gains, shifts, bias3, bias_d, bias_u, bias_2 = vectors
    bias_o = bias_d + bias_2
    tables = rotary_tables(length)
    own_w = (w_qkv[0], w_fc1[0], w_dense[0], w_fc2[0])

    results = forward_both(
        inputs, own_w, (gains, shifts, bias3.reshape(6, local), bias_u, bias_o), tables
    )
    other_w = results[:4]
    h, h_far, query, key, value, merged, merged_near, merged_far = results[4:12]
    act_near, act_far, slope, logs, x1, part1 = results[12:]
    saved = (slope, query, key, value, merged, logs)

    sides = (h, h_far, act_near, act_far, merged_near, merged_far)
    grads = backward_both(
        dp_size, cotangent, inputs, x1, part1, saved, own_w, other_w, sides, gains, bias_o, tables
    )
    acts, grads_in = grads[:2]
    down, up, sums = grads[10:]
    out_fc2, out_dense = down_total(down, hidden, local)
    out_fc1, out_qkv = up_total(up, hidden, local)
    place = rank * dp_size + dp_rank

    def piece(rows, count, index, parts):
        size = count // parts
        return lax.dynamic_slice_in_dim(rows[:, :count], index * size, size, 1)

    out_norm = piece(sums[0:2], width, place, lines * dp_size)
    out_bfc1 = piece(sums[2:3], hidden, dp_rank, dp_size)
    out_bout = piece(sums[3:4], width, dp_rank, dp_size)
    out_bqkv = piece(sums[4:7], local, dp_rank, dp_size)
    return (
        acts[None],
        grads_in[None],
        out_norm[0:1],
        out_norm[1:2],
        out_qkv[None],
        out_bqkv[None],
        out_dense[None],
        out_bout,
        out_fc1[None],
        out_bfc1,
        out_fc2[None],
        out_bout,
    )


def solution(mesh):
    in_specs = (
        P("dp", None, None),
        P("dp", None, None),
        P("pipe", None),
        P("pipe", None),
        P("pipe", None, None, "tensor"),
        P("pipe", None, "tensor"),
        P("pipe", "tensor", None),
        P("pipe", None),
        P("pipe", None, "tensor"),
        P("pipe", "tensor"),
        P("pipe", "tensor", None),
        P("pipe", None),
    )
    out_specs = (
        P("pipe", "dp", "tensor", None),
        P("pipe", "dp", "tensor", None),
        P("pipe", ("tensor", "dp")),
        P("pipe", ("tensor", "dp")),
        P("pipe", None, "dp", "tensor"),
        P("pipe", None, ("tensor", "dp")),
        P("pipe", "tensor", "dp"),
        P("pipe", "dp"),
        P("pipe", "dp", "tensor"),
        P("pipe", ("tensor", "dp")),
        P("pipe", "tensor", "dp"),
        P("pipe", "dp"),
    )
    return jax.shard_map(body, mesh=mesh, in_specs=in_specs, out_specs=out_specs, check_vma=False)
```

```python
import functools

import jax
import jax.numpy as jnp
from jax import lax
from jax.experimental import pallas as pl
from jax.experimental.pallas import tpu as pltpu
from jax.sharding import PartitionSpec as P

HEAD_DIM = 64
ROT = 32
LANES = 128
MIB = 1024 * 1024

ln_eps = 1e-05
rope_base = 10000.0
gelu_coef = 0.7978845608028654
masked_score = -1e30

BF = jnp.bfloat16
F32 = jnp.float32


def rotary_tables(length):
    half_rot = ROT // 2
    place = jnp.arange(LANES, dtype=jnp.int32) % HEAD_DIM
    inverse = rope_base ** (-((place % half_rot).astype(F32) * 2.0 / ROT))
    angles = jnp.arange(length, dtype=F32)[:, None] * inverse[None, :]
    cosines, sines = jnp.cos(angles), jnp.sin(angles)
    place = place[None, :]
    return (
        jnp.where(place < ROT, cosines, 1.0),
        jnp.where(place < half_rot, -sines, 0.0),
        jnp.where((place >= half_rot) & (place < ROT), sines, 0.0),
    )


def turn(values, cos, near, far):
    half_rot = ROT // 2
    return (
        values * cos
        + pltpu.roll(values, LANES - half_rot, 1) * near
        + pltpu.roll(values, half_rot, 1) * far
    )


def head_mask(rows, which):
    lanes = lax.broadcasted_iota(jnp.int32, (rows, LANES), 1)
    return (lanes // HEAD_DIM) == which


def as_row(column):
    return jnp.transpose(jnp.broadcast_to(column, (column.shape[0], LANES)))[0:1, :]


def dot_nt(left, right):
    return lax.dot_general(left, right, (((1,), (1,)), ((), ())), preferred_element_type=F32)


def dot_nn(left, right):
    return lax.dot_general(left, right, (((1,), (0,)), ((), ())), preferred_element_type=F32)


def dot_tn(left, right):
    return lax.dot_general(left, right, (((0,), (0,)), ((), ())), preferred_element_type=F32)


LINE = 4
STEPS = 2 * LINE
TILE = 512
SUM_PIECES = 2


def remote(src, dst, send, recv, axis, index):
    return pltpu.make_async_remote_copy(
        src_ref=src,
        dst_ref=dst,
        send_sem=send,
        recv_sem=recv,
        device_id={axis: index},
        device_id_type=pl.DeviceIdType.MESH,
    )


def greet(core, rank):
    barrier = pltpu.get_barrier_semaphore()

    def tell(axis, index):
        pl.semaphore_signal(
            barrier, inc=1, device_id={axis: index}, device_id_type=pl.DeviceIdType.MESH
        )

    tell("pipe", 1 - core)

    @pl.when(rank > 0)
    def _():
        tell("tensor", rank - 1)

    @pl.when(rank < LINE - 1)
    def _():
        tell("tensor", rank + 1)

    ends = jnp.where(rank > 0, 1, 0) + jnp.where(rank < LINE - 1, 1, 0)
    pl.semaphore_wait(barrier, 1 + ends)


def fetch_weight(layer, core, own, other, target, sem, arrival):
    @pl.when(core == layer)
    def _():
        pltpu.make_async_copy(own, target, sem).start()

    @pl.when(core != layer)
    def _():
        if arrival is not None:
            arrival.wait_recv()
        pltpu.make_async_copy(other, target, sem).start()


class LineSum:
    def __init__(self, rank, part, first, beside, second, last, result, sems, finish):
        self.rank, self.part, self.result, self.finish = rank, part, result, finish
        self.first, self.beside, self.second, self.last = first, beside, second, last
        self.sems = sems
        self.rows = part.shape[1]
        self.block = self.rows // LINE
        self.cols = part.shape[2] // SUM_PIECES
        half = 2 * self.block
        self.left = rank < 2
        self.far = pl.multiple_of(jnp.where(self.left, half, 0), half)
        self.near = pl.multiple_of(jnp.where(self.left, 0, half), half)
        self.own = pl.multiple_of(rank * self.block, self.block)
        self.inner = (rank == 1) | (rank == 2)
        self.outer = (rank == 0) | (rank == 3)
        self.inward = jnp.where(self.left, 1, 2)
        self.outward = jnp.where(self.left, 0, 3)
        self.across = jnp.where(self.left, 2, 1)
        self.spare = pl.multiple_of(jnp.where(self.left, self.block, half), self.block)
        self.out_half = pl.multiple_of(jnp.where(self.left, 0, self.block), self.block)
        self.in_half = pl.multiple_of(jnp.where(self.left, self.block, 0), self.block)

    def copies(self, chunk, piece):
        half = 2 * self.block
        cols = slice(piece * self.cols, (piece + 1) * self.cols)
        index = chunk * SUM_PIECES + piece

        def hop(name, src, dst, to):
            sems = self.sems[name]
            return remote(
                src.at[chunk, src_rows, cols], dst, sems.at[0, index], sems.at[1, index], "tensor", to
            )

        src_rows = pl.ds(self.far, half)
        hop_first = hop("first", self.part, self.first.at[chunk, :, cols], self.inward)
        src_rows = pl.ds(self.spare, self.block)
        hop_beside = hop("beside", self.part, self.beside.at[chunk, :, cols], self.inward)
        src_rows = pl.ds(0, half)
        hop_second = hop("second", self.first, self.second.at[chunk, :, cols], self.across)
        src_rows = pl.ds(self.out_half, self.block)
        hop_last = hop("last", self.second, self.last.at[chunk, :, cols], self.outward)
        return hop_first, hop_beside, hop_second, hop_last

    def result_rows(self, chunk, shard):
        start = pl.multiple_of(chunk * self.rows + shard * self.block, self.block)
        return self.result.at[pl.ds(start, self.block)]

    def move(self, way, chunk, hop):
        step = 1 - 2 * way
        shard = jnp.clip(self.rank - step * hop, 0, LINE - 1)
        rows = self.result_rows(chunk, shard)
        name = "up" if way == 0 else "down"
        to = jnp.clip(self.rank + step, 0, LINE - 1)
        index = chunk * (LINE - 1) + hop
        return remote(rows, rows, self.sems[name].at[0, index], self.sems[name].at[1, index], "tensor", to)

    def stage_a(self, chunk):
        @pl.when(self.outer)
        def _():
            for piece in range(SUM_PIECES):
                self.copies(chunk, piece)[0].start()

    def stage_b(self, chunk):
        @pl.when(self.outer)
        def _():
            for piece in range(SUM_PIECES):
                self.copies(chunk, piece)[1].start()

        @pl.when(self.inner)
        def _():
            for piece in range(SUM_PIECES):
                hop_first, _, hop_second, _ = self.copies(chunk, piece)
                cols = slice(piece * self.cols, (piece + 1) * self.cols)
                hop_first.wait_recv()
                self.first[chunk, :, cols] = (
                    self.first[chunk, :, cols].astype(F32)
                    + self.part[chunk, pl.ds(self.far, 2 * self.block), cols].astype(F32)
                ).astype(BF)
                hop_second.start()

    def stage_c(self, chunk):
        @pl.when(self.inner)
        def _():
            out_rows = pl.ds(self.out_half, self.block)
            near_out = pl.ds(pl.multiple_of(self.near + self.out_half, self.block), self.block)
            for piece in range(SUM_PIECES):
                _, _, hop_second, hop_last = self.copies(chunk, piece)
                cols = slice(piece * self.cols, (piece + 1) * self.cols)
                hop_second.wait_recv()
                self.second[chunk, out_rows, cols] = (
                    self.second[chunk, out_rows, cols].astype(F32)
                    + self.part[chunk, near_out, cols].astype(F32)
                ).astype(BF)
                hop_last.start()
            for piece in range(SUM_PIECES):
                self.copies(chunk, piece)[1].wait_recv()
            total = (
                self.second[chunk, pl.ds(self.in_half, self.block)].astype(F32)
                + self.beside[chunk].astype(F32)
                + self.part[chunk, pl.ds(self.own, self.block)].astype(F32)
            )
            self.finish(chunk, total, self.result_rows(chunk, self.rank))
            self.move(0, chunk, 0).start()
            self.move(1, chunk, 0).start()

    def stage_d(self, chunk):
        @pl.when(self.outer)
        def _():
            for piece in range(SUM_PIECES):
                self.copies(chunk, piece)[3].wait_recv()
            total = self.last[chunk].astype(F32) + self.part[
                chunk, pl.ds(self.own, self.block)
            ].astype(F32)
            self.finish(chunk, total, self.result_rows(chunk, self.rank))

        @pl.when(self.rank == 0)
        def _():
            self.move(0, chunk, 0).start()

        @pl.when(self.rank == 3)
        def _():
            self.move(1, chunk, 0).start()

    def stage_e(self, chunk, hop):
        for way in range(2):
            behind = self.rank if way == 0 else LINE - 1 - self.rank

            @pl.when(self.inner & (behind > hop))
            def _():
                self.arrival(way, chunk, hop).wait_recv()
                self.move(way, chunk, hop + 1).start()

    def arrival(self, way, chunk, hop):
        step = 1 - 2 * way
        shard = jnp.clip(self.rank - step * (hop + 1), 0, LINE - 1)
        rows = self.result_rows(chunk, shard)
        name = "up" if way == 0 else "down"
        to = jnp.clip(self.rank + step, 0, LINE - 1)
        index = chunk * (LINE - 1) + hop
        return remote(rows, rows, self.sems[name].at[0, index], self.sems[name].at[1, index], "tensor", to)

    def stage_f(self, chunk):
        @pl.when(self.rank == 0)
        def _():
            for hop in range(LINE - 1):
                self.arrival(1, chunk, hop).wait_recv()

        @pl.when(self.rank == 3)
        def _():
            for hop in range(LINE - 1):
                self.arrival(0, chunk, hop).wait_recv()

    def sent_part(self, chunk):
        @pl.when(self.outer)
        def _():
            for piece in range(SUM_PIECES):
                hop_first, hop_beside, _, _ = self.copies(chunk, piece)
                hop_first.wait_send()
                hop_beside.wait_send()

    def sent_rest(self, chunk):
        @pl.when(self.inner)
        def _():
            for piece in range(SUM_PIECES):
                _, _, hop_second, hop_last = self.copies(chunk, piece)
                hop_second.wait_send()
                hop_last.wait_send()

        for way in range(2):
            behind = self.rank if way == 0 else LINE - 1 - self.rank
            ahead = LINE - 1 - behind
            for hop in range(LINE - 1):

                @pl.when((ahead > 0) & (behind >= hop))
                def _():
                    self.move(way, chunk, hop).wait_send()


def line_sum_scratch(rows, cols):
    block = rows // LINE
    return [
        pltpu.VMEM((LINE, 2 * block, cols), BF),
        pltpu.VMEM((LINE, block, cols), BF),
        pltpu.VMEM((LINE, 2 * block, cols), BF),
        pltpu.VMEM((LINE, block, cols), BF),
    ] + [pltpu.SemaphoreType.DMA((2, LINE * SUM_PIECES))] * 4 + [
        pltpu.SemaphoreType.DMA((2, LINE * (LINE - 1)))
    ] * 2


SUM_NAMES = ("first", "beside", "second", "last", "up", "down")


class LineShare:
    def __init__(self, rank, part, room, sems, pieces):
        self.rank, self.part, self.room, self.pieces = rank, part, room, pieces
        self.sems = sems
        self.cols = part.shape[2] // pieces

    def span(self, piece):
        return pl.ds(pl.multiple_of(piece * self.cols, self.cols), self.cols)

    def slot(self, way, chunk, device):
        return chunk if way == 0 else jnp.where(device == chunk, LINE, chunk)

    def copy(self, way, chunk, piece, own):
        to = jnp.clip(self.rank + 1 - 2 * way, 0, LINE - 1)
        span = self.span(piece)
        here = self.part.at[chunk, :, span] if own else self.room.at[self.slot(way, chunk, self.rank), :, span]
        index = chunk * self.pieces + piece
        return remote(
            here,
            self.room.at[self.slot(way, chunk, to), :, span],
            self.sems[way].at[0, index],
            self.sems[way].at[1, index],
            "tensor",
            to,
        )

    def emit(self, chunk, piece):
        @pl.when((self.rank == 0) & (chunk > 0))
        def _():
            self.copy(0, chunk, piece, True).start()

        @pl.when((self.rank == LINE - 1) & (chunk < LINE - 1))
        def _():
            self.copy(1, chunk, piece, True).start()

    def relay(self, chunk, hop):
        for way in range(2):
            at = hop if way == 0 else LINE - 1 - hop
            further = (chunk > at) if way == 0 else (chunk < at)

            @pl.when((self.rank == at) & further)
            def _():
                def one(piece, _):
                    copy = self.copy(way, chunk, piece, False)
                    copy.wait_recv()
                    span = self.span(piece)
                    slot = self.slot(way, chunk, self.rank)
                    self.room[slot, :, span] = (
                        self.room[slot, :, span].astype(F32) + self.part[chunk, :, span].astype(F32)
                    ).astype(BF)
                    copy.start()
                    return 0

                lax.fori_loop(0, self.pieces, one, 0)

    def arrived(self):
        for way in range(2):
            behind = self.rank > 0 if way == 0 else self.rank < LINE - 1

            @pl.when(behind)
            def _():
                def one(piece, _):
                    self.copy(way, self.rank, piece, False).wait_recv()
                    return 0

                lax.fori_loop(0, self.pieces, one, 0)

    def total(self, span):
        blank = jnp.zeros((span.size, self.part.shape[2]), BF)
        left = jnp.where(self.rank > 0, self.room[self.rank, span, :], blank)
        right = jnp.where(self.rank < LINE - 1, self.room[LINE, span, :], blank)
        return self.part[self.rank, span, :].astype(F32) + left.astype(F32) + right.astype(F32)

    def sent(self, chunk):
        for way in range(2):
            end = 0 if way == 0 else LINE - 1
            for hop in range(LINE - 1):
                at = hop if way == 0 else LINE - 1 - hop
                further = (chunk > at) if way == 0 else (chunk < at)

                @pl.when((self.rank == at) & further)
                def _():
                    def one(piece, _):
                        self.copy(way, chunk, piece, at == end).wait_send()
                        return 0

                    lax.fori_loop(0, self.pieces, one, 0)


def deliver(core, layer, mine, target, sems, act):
    @pl.when(core == layer)
    def _():
        copy = pltpu.make_async_copy(mine, target.at[core], sems.at[layer])
        copy.start() if act == "start" else copy.wait()

    @pl.when(core != layer)
    def _():
        copy = remote(mine, target.at[core], sems.at[layer], sems.at[2], "pipe", 1 - core)
        copy.start() if act == "start" else copy.wait_send()


def delivered(core, target, sems):
    ref = target.at[1 - core]
    remote(ref, ref, sems.at[0], sems.at[2], "pipe", 1 - core).wait_recv()


def forward_kernel(*refs):
    at = 0

    def take(count):
        nonlocal at
        at += count
        return refs[at - count : at]

    (inputs_ref,) = take(1)
    own_w = take(4)
    given = take(6)
    cos_ref, near_ref, far_ref = take(3)
    other_w = take(4)
    h_out, h_far, q_out, k_out, v_out, o_out, o_near, o_far = take(8)
    act_near, act_far, slope_out, logs_out, x1_out, part_out = take(6)
    (small_out,) = take(1)
    vmem_w = take(4)
    x_buf, x_share, h_buf, act_buf, slope_buf, q_buf, o_buf, k_all, v_all, logs_buf = take(10)
    part, x1 = take(2)
    sum_bufs = take(4)
    sum_sems = dict(zip(SUM_NAMES, take(6)))
    w_sems, fetch_sems, x_sems, out_sems, slot4_sems, far_send, far_recv, once_sems = take(8)
    small, small_sems = take(2)
    assert at == len(refs)
    core = lax.axis_index("pipe")
    rank = lax.axis_index("tensor")
    theirs = 1 - core
    rows = x_buf.shape[1]
    width = x_buf.shape[2]
    local = q_buf.shape[2]
    hidden = act_buf.shape[2]
    half_hidden = hidden // 2
    half_local = local // 2
    tile = min(TILE, width)
    scale = HEAD_DIM ** (-0.5)

    weight_moves = [
        remote(own, other, w_sems.at[0, i], w_sems.at[1, i], "pipe", 1 - core)
        for i, (own, other) in enumerate(zip(own_w, other_w))
    ]

    def fetch(layer, i):
        fetch_weight(
            layer, core, own_w[i], other_w[i], vmem_w[i], fetch_sems.at[i], weight_moves[i]
        )

    def fetched(i):
        pltpu.make_async_copy(own_w[i], vmem_w[i], fetch_sems.at[i]).wait()

    def chunk_rows(chunk):
        return pl.ds(pl.multiple_of(chunk * rows, rows), rows)

    def x_copy(chunk):
        slot = lax.rem(chunk, 2)
        return pltpu.make_async_copy(
            inputs_ref.at[core, chunk_rows(chunk)], x_buf.at[slot], x_sems.at[slot]
        )

    def finish(chunk, total, target):
        value = total + x_share[chunk].astype(F32) + small[0, 3:4, 0:width]
        target[...] = value.astype(BF)

    summed = LineSum(rank, part, *sum_bufs, x1, sum_sems, finish)

    def half(which, size):
        return pl.ds(pl.multiple_of(which * size, size), size)

    def placed(step):
        layer, chunk = lax.div(step, LINE), lax.rem(step, LINE)
        return layer, chunk_rows(chunk), lax.rem(step, 2), chunk

    def local_copy(name, src, dst, slot):
        return pltpu.make_async_copy(src, dst, out_sems.at[name, slot])

    def far_copy(name, src, dst, slot):
        return remote(src, dst, far_send.at[name, slot], far_recv.at[name], "pipe", theirs)

    def h_copies(step):
        layer, at_rows, _, slot = placed(step)
        return [
            local_copy(0, h_buf.at[slot], h_out.at[layer, at_rows], slot),
            far_copy(0, h_buf.at[slot], h_far.at[layer, at_rows], slot),
        ]

    def q_copies(step):
        layer, at_rows, slot, _ = placed(step)
        return [local_copy(1, q_buf.at[slot], q_out.at[layer, at_rows], slot)]

    def logs_copies(step):
        layer, at_rows, slot, _ = placed(step)
        return [local_copy(2, logs_buf.at[slot], logs_out.at[layer, :, :, at_rows], slot)]

    def o_copies(step):
        layer, at_rows, _, slot = placed(step)
        return [
            local_copy(3, o_buf.at[slot], o_out.at[layer, at_rows], slot),
            far_copy(1, o_buf.at[slot, :, half(theirs, half_local)], o_far.at[layer, at_rows], slot),
            local_copy(4, o_buf.at[slot, :, half(core, half_local)], o_near.at[layer, at_rows], slot),
        ]

    def act_copies(step):
        layer, at_rows, slot, _ = placed(step)
        return [
            local_copy(5, act_buf.at[slot, :, half(core, half_hidden)], act_near.at[layer, at_rows], slot),
            far_copy(2, act_buf.at[slot, :, half(theirs, half_hidden)], act_far.at[layer, at_rows], slot),
            local_copy(6, slope_buf.at[slot], slope_out.at[layer, at_rows], slot),
        ]

    def start_all(copies):
        for item in copies:
            item.start()

    def left_all(copies):
        for i, item in enumerate(copies):
            if i == 1:
                item.wait_send()
            else:
                item.wait()

    def kv_copies(step):
        layer, chunk = lax.div(step, LINE), lax.rem(step, LINE)
        at_rows = chunk_rows(chunk)
        return [
            pltpu.make_async_copy(k_all.at[at_rows], k_out.at[layer, at_rows], slot4_sems.at[0, chunk]),
            pltpu.make_async_copy(v_all.at[at_rows], v_out.at[layer, at_rows], slot4_sems.at[1, chunk]),
        ]

    def x1_copy(chunk):
        at_rows = chunk_rows(chunk)
        return pltpu.make_async_copy(x1.at[at_rows], x1_out.at[at_rows], once_sems.at[0, chunk])

    def part_copy(chunk):
        at_rows = chunk_rows(chunk)
        return pltpu.make_async_copy(part.at[chunk], part_out.at[at_rows], once_sems.at[1, chunk])

    gain_in, shift_in, bias3_in, bias_d_in, bias_u_in, bias_2_in = given
    x_copy(0).start()
    small[core, 0:1, 0:width] = gain_in[...].astype(F32)
    small[core, 1:2, 0:width] = shift_in[...].astype(F32)
    small[core, 2:3, 0:hidden] = bias_u_in[...].astype(F32)
    small[core, 3:4, 0:width] = bias_d_in[...].astype(F32) + bias_2_in[...].astype(F32)
    for c in range(3):
        small[core, 4 + c : 5 + c, 0:local] = bias3_in[0, c : c + 1, :].astype(F32)
    greet(core, rank)
    small_move = remote(
        small.at[core], small.at[core], small_sems.at[0], small_sems.at[1], "pipe", 1 - core
    )
    small_move.start()
    for move in weight_moves:
        move.start()
    x_copy(1).start()

    keep = lax.broadcasted_iota(jnp.int32, (rows, rows), 1) <= lax.broadcasted_iota(
        jnp.int32, (rows, rows), 0
    )

    def attention(chunk, slot):
        def pair(j, _):
            lanes = pl.ds(pl.multiple_of(j * LANES, LANES), LANES)
            query = q_buf[slot, :, lanes]
            outs = []
            for which in range(LANES // HEAD_DIM):
                mask = head_mask(rows, which)
                mine = jnp.where(mask, query, jnp.zeros_like(query))
                scores = []
                if chunk:
                    scores.append(dot_nt(mine, k_all[0 : chunk * rows, lanes]))
                scores.append(
                    jnp.where(keep, dot_nt(mine, k_all[chunk * rows : (chunk + 1) * rows, lanes]), masked_score)
                )
                top = functools.reduce(
                    jnp.maximum, [jnp.max(item, axis=1, keepdims=True) for item in scores]
                )
                weights = [jnp.exp(item - top) for item in scores]
                total = functools.reduce(
                    jnp.add, [jnp.sum(item, axis=1, keepdims=True) for item in weights]
                )
                values = []
                if chunk:
                    values.append(v_all[0 : chunk * rows, lanes])
                values.append(v_all[chunk * rows : (chunk + 1) * rows, lanes])
                merged = functools.reduce(
                    jnp.add, [dot_nn(w.astype(BF), v) for w, v in zip(weights, values)]
                )
                outs.append(merged / total)
                logs_buf[slot, j, which : which + 1, :] = as_row(top + jnp.log(total))
            o_buf[chunk, :, lanes] = jnp.where(head_mask(rows, 0), outs[0], outs[1]).astype(BF)
            return 0

        lax.fori_loop(0, local // LANES, pair, 0)

    def go_on(step):
        @pl.when((step >= 1) & (step <= LINE))
        def _():
            summed.stage_b(step - 1)

        @pl.when((step >= 2) & (step <= LINE + 1))
        def _():
            summed.stage_d(step - 2)

        @pl.when((step >= 3) & (step <= LINE + 2))
        def _():
            summed.stage_e(step - 3, 1)

    def attention_part(step, _):
        layer, chunk = lax.div(step, LINE), lax.rem(step, LINE)
        slot = lax.rem(step, 2)
        at_rows = chunk_rows(chunk)

        @pl.when(step >= 2)
        def _():
            left_all(q_copies(step - 2))
            left_all(logs_copies(step - 2))

        @pl.when(step >= LINE)
        def _():
            left_all(h_copies(step - LINE))
            left_all(o_copies(step - LINE))

        some_rows = rows // 8
        gain, shift = small[layer, 0:1, 0:width], small[layer, 1:2, 0:width]

        def normalise(load):
            def some(i, _):
                span = pl.ds(pl.multiple_of(i * some_rows, some_rows), some_rows)
                values = load(span).astype(F32)
                centre = values - jnp.mean(values, axis=-1, keepdims=True)
                spread = jnp.mean(centre * centre, axis=-1, keepdims=True)
                h_buf[chunk, span, :] = (centre * lax.rsqrt(spread + ln_eps) * gain + shift).astype(BF)
                return 0

            lax.fori_loop(0, 8, some, 0)

        @pl.when(layer == 0)
        def _():
            x_copy(chunk).wait()
            x_share[chunk] = x_buf[slot, pl.ds(pl.multiple_of(rank * (rows // LINE), rows // LINE), rows // LINE)]
            normalise(lambda span: x_buf[slot, span, :])

            @pl.when(step + 2 < LINE)
            def _():
                x_copy(chunk + 2).start()

        @pl.when(step == 0)
        def _():
            fetch(0, 0)

        @pl.when(layer == 1)
        def _():
            summed.stage_f(chunk)
            x1_copy(chunk).start()
            base = chunk * rows
            normalise(lambda span: x1[pl.ds(pl.multiple_of(base + span.start, some_rows), some_rows), :])

        start_all(h_copies(step))

        @pl.when(chunk == 0)
        def _():
            fetched(0)

        @pl.when(layer == 1)
        def _():
            for item in kv_copies(step - LINE):
                item.wait()

        tables = (cos_ref[at_rows, :], near_ref[at_rows, :], far_ref[at_rows, :])
        h = h_buf[chunk]
        for part3 in range(3):
            value = dot_nn(h, vmem_w[0][part3]) + small[layer, 4 + part3 : 5 + part3, 0:local]
            for j in range(local // LANES):
                lanes = slice(j * LANES, (j + 1) * LANES)
                if part3 == 0:
                    q_buf[slot, :, lanes] = (turn(value[:, lanes], *tables) * scale).astype(BF)
                elif part3 == 1:
                    k_all[at_rows, lanes] = turn(value[:, lanes], *tables).astype(BF)
                else:
                    v_all[at_rows, lanes] = value[:, lanes].astype(BF)
        start_all(q_copies(step))
        start_all(kv_copies(step))

        @pl.when(step == LINE - 1)
        def _():
            fetch(1, 0)

        @pl.when(layer == 1)
        def _():
            go_on(step)

        for index in range(LINE):

            @pl.when(chunk == index)
            def _():
                attention(index, slot)

        start_all(o_copies(step))
        start_all(logs_copies(step))

        @pl.when(step == jnp.where(core == 0, 0, LINE - 2))
        def _():
            fetch(0, 1)

        @pl.when(step == jnp.where(core == 0, 0, LINE - 1))
        def _():
            fetch(0, 2)

        return 0

    def hidden_part(step, _):
        layer, chunk = lax.div(step, LINE), lax.rem(step, LINE)
        slot = lax.rem(step, 2)

        @pl.when(step >= 2)
        def _():
            left_all(act_copies(step - 2))

        @pl.when(chunk == 0)
        def _():
            fetched(1)

        def up(i, _):
            cols = pl.ds(pl.multiple_of(i * tile, tile), tile)
            u = dot_nn(h_buf[chunk], vmem_w[1][:, cols]) + small[layer, 2:3, cols]
            square = u * u
            inner = jnp.tanh(u * (gelu_coef + (gelu_coef * 0.044715) * square))
            plus = 0.5 + 0.5 * inner
            act = u * plus
            act_buf[slot, :, cols] = act.astype(BF)
            slope_buf[slot, :, cols] = (
                plus + act * (1.0 - inner) * (gelu_coef + (3.0 * 0.044715 * gelu_coef) * square)
            ).astype(BF)
            return 0

        lax.fori_loop(0, hidden // tile, up, 0, unroll=True)
        start_all(act_copies(step))

        @pl.when(step == 0)
        def _():
            fetch(0, 3)

        @pl.when(step == LINE - 1)
        def _():
            fetch(1, 1)

        @pl.when(layer == 0)
        def _():
            go_on(step)

        @pl.when(chunk == 0)
        def _():
            fetched(2)
            fetched(3)

        @pl.when(layer == 1)
        def _():
            summed.sent_part(chunk)

        def down(i, _):
            cols = pl.ds(pl.multiple_of(i * tile, tile), tile)
            part[chunk, :, cols] = (
                dot_nn(o_buf[chunk], vmem_w[2][:, cols]) + dot_nn(act_buf[slot], vmem_w[3][:, cols])
            ).astype(BF)
            return 0

        lax.fori_loop(0, width // tile, down, 0, unroll=True)

        @pl.when(step == LINE - 1)
        def _():
            fetch(1, 2)
            fetch(1, 3)

        @pl.when(layer == 0)
        def _():
            summed.stage_a(chunk)

        @pl.when(layer == 1)
        def _():
            part_copy(chunk).start()

        @pl.when((step >= 1) & (step <= LINE))
        def _():
            summed.stage_c(step - 1)

        @pl.when((step >= 2) & (step <= LINE + 1))
        def _():
            summed.stage_e(step - 2, 0)

        return 0

    def whole_step(step, _):
        attention_part(step, 0)
        hidden_part(step, 0)
        return 0

    def first_layer(turn_, _):
        kind = jnp.where(core == 0, lax.rem(turn_, 2), lax.div(turn_, LINE))
        step = jnp.where(core == 0, lax.div(turn_, 2), lax.rem(turn_, LINE))

        @pl.when(kind == 0)
        def _():
            attention_part(step, 0)

        @pl.when(kind == 1)
        def _():
            hidden_part(step, 0)

        return 0

    remote(
        small.at[1 - core], small.at[1 - core], small_sems.at[0], small_sems.at[1], "pipe", 1 - core
    ).wait_recv()
    small_out[...] = small[...]
    lax.fori_loop(0, 2 * LINE, first_layer, 0)
    lax.fori_loop(LINE, STEPS, whole_step, 0)

    for step in range(STEPS - 2, STEPS):
        left_all(q_copies(step))
        left_all(logs_copies(step))
        left_all(act_copies(step))
    for step in range(LINE, STEPS):
        left_all(h_copies(step))
        left_all(o_copies(step))
        for item in kv_copies(step):
            item.wait()
    for chunk in range(LINE):
        x1_copy(chunk).wait()
        part_copy(chunk).wait()
        summed.sent_rest(chunk)
    for move in weight_moves:
        move.wait_send()
    small_move.wait_send()
    for i, ref in enumerate((h_far, o_far, act_far)):
        remote(ref, ref, far_send.at[i, 0], far_recv.at[i], "pipe", theirs).wait_recv()


def forward_both(inputs, weights, vectors, tables):
    _, length, width = inputs.shape
    w_qkv, w_fc1, w_dense, w_fc2 = weights
    local, hidden = w_dense.shape[0], w_fc1.shape[1]
    rows = length // LINE
    pairs = local // LANES

    def bf(*shape):
        return jax.ShapeDtypeStruct(shape, BF)

    out_shape = [bf(*w.shape) for w in weights] + [
        bf(2, length, width),
        bf(2, length, width),
        bf(2, length, local),
        bf(2, length, local),
        bf(2, length, local),
        bf(2, length, local),
        bf(2, length, local // 2),
        bf(2, length, local // 2),
        bf(2, length, hidden // 2),
        bf(2, length, hidden // 2),
        bf(2, length, hidden),
        jax.ShapeDtypeStruct((2, pairs, 8, length), F32),
        bf(length, width),
        bf(length, width),
        jax.ShapeDtypeStruct((2, 8, max(width, hidden)), F32),
    ]
    whole = pl.BlockSpec(memory_space=pltpu.VMEM)
    away = pl.BlockSpec(memory_space=pl.ANY)
    dma = pltpu.SemaphoreType.DMA
    return pl.pallas_call(
        forward_kernel,
        name="forward_both",
        in_specs=[away] * 5 + [whole] * 9,
        out_specs=[away] * (len(out_shape) - 1) + [whole],
        out_shape=out_shape,
        scratch_shapes=[pltpu.VMEM(w.shape, BF) for w in weights]
        + [
            pltpu.VMEM((2, rows, width), BF),
            pltpu.VMEM((LINE, rows // LINE, width), BF),
            pltpu.VMEM((LINE, rows, width), BF),
            pltpu.VMEM((2, rows, hidden), BF),
            pltpu.VMEM((2, rows, hidden), BF),
            pltpu.VMEM((2, rows, local), BF),
            pltpu.VMEM((LINE, rows, local), BF),
            pltpu.VMEM((length, local), BF),
            pltpu.VMEM((length, local), BF),
            pltpu.VMEM((2, pairs, 8, rows), F32),
            pltpu.VMEM((LINE, rows, width), BF),
            pltpu.VMEM((length, width), BF),
        ]
        + line_sum_scratch(rows, width)
        + [
            dma((2, 4)),
            dma((4,)),
            dma((2,)),
            dma((7, LINE)),
            dma((2, LINE)),
            dma((3, LINE)),
            dma((3,)),
            dma((2, LINE)),
            pltpu.VMEM((2, 8, max(width, hidden)), F32),
            dma((2,)),
        ],
        compiler_params=pltpu.CompilerParams(
            collective_id=0, has_side_effects=True, vmem_limit_bytes=63 * MIB
        ),
        cost_estimate=pl.CostEstimate(
            flops=4 * length * width * (4 * local + 2 * hidden),
            bytes_accessed=200 * MIB,
            transcendentals=0,
        ),
    )(inputs, *weights, *vectors, *tables)


class PairDots:
    def __init__(self, core, dp_rank, dp_size, left_buf, right_buf, out_buf, sems, stages, received):
        self.core, self.me, self.dp = core, dp_rank, dp_size
        self.left_buf, self.right_buf, self.out_buf = left_buf, right_buf, out_buf
        self.left_sems, self.right_sems, self.out_sems, self.send_sems, self.recv_sems = sems
        self.stages, self.received = stages, received
        self.tokens = left_buf.shape[1] // 2
        self.keep = left_buf.shape[2]
        self.groups = {}

    def add(self, index, layer, kind, left, rights):
        total = sum(near.shape[-1] for near, _ in rights)
        widths = []
        while sum(widths) < total:
            widths.append(min(TILE, total - sum(widths)))
        self.groups[index] = (layer, kind, left, rights, widths)

    def tile(self, order):
        return lax.rem(self.me + 1 + order, self.dp)

    def left_copies(self, index, order):
        near, far = self.groups[index][2]
        slot = lax.rem(order, 2)
        cols = pl.ds(pl.multiple_of(self.tile(order) * self.keep, self.keep), self.keep)
        return [
            pltpu.make_async_copy(
                src.at[:, cols],
                self.left_buf.at[slot, i * self.tokens : (i + 1) * self.tokens],
                self.left_sems.at[i, slot],
            )
            for i, src in enumerate((near, far))
        ]

    def right_copies(self, index):
        copies = []
        base = 0
        for pair in self.groups[index][3]:
            width = pair[0].shape[-1]
            for i, src in enumerate(pair):
                target = self.right_buf.at[i * self.tokens : (i + 1) * self.tokens, base : base + width]
                copies.append(pltpu.make_async_copy(src, target, self.right_sems.at[len(copies)]))
            base += width
        return copies

    def prime(self, index):
        for item in self.left_copies(index, jnp.int32(0)) + self.right_copies(index):
            item.start()

    def out_copy(self, index, order, piece):
        layer, kind, _, _, widths = self.groups[index]
        base, width, slot = sum(widths[:piece]), widths[piece], piece % 2
        stage = self.stages[kind].at[layer, self.tile(order)]
        if kind:
            return pltpu.make_async_copy(
                self.out_buf.at[slot, 0 : self.keep, 0:width],
                stage.at[:, base : base + width],
                self.out_sems.at[slot],
            )
        return pltpu.make_async_copy(
            self.out_buf.at[slot, 0:width, 0 : self.keep],
            stage.at[base : base + width],
            self.out_sems.at[slot],
        )

    def send(self, index, order, act):
        layer, kind = self.groups[index][:2]
        tile = self.tile(order)
        src = self.stages[kind].at[layer, tile]
        dst = self.received[kind].at[self.core, self.me]
        at_home = (self.core == layer) & (tile == self.me)

        @pl.when(at_home)
        def _():
            copy = pltpu.make_async_copy(src, dst, self.send_sems.at[index, order])
            copy.start() if act == "start" else copy.wait()

        @pl.when(jnp.logical_not(at_home))
        def _():
            copy = pltpu.make_async_remote_copy(
                src_ref=src,
                dst_ref=dst,
                send_sem=self.send_sems.at[index, order],
                recv_sem=self.recv_sems.at[kind, self.core],
                device_id={"pipe": jnp.int32(layer), "dp": tile},
                device_id_type=pl.DeviceIdType.MESH,
            )
            copy.start() if act == "start" else copy.wait_send()

    def run(self, index, start, stop):
        _, kind, _, _, widths = self.groups[index]

        def one(order, _):
            slot = lax.rem(order, 2)
            for item in self.left_copies(index, order):
                item.wait()

            @pl.when(order == 0)
            def _():
                for item in self.right_copies(index):
                    item.wait()

            @pl.when(order + 1 < self.dp)
            def _():
                for item in self.left_copies(index, order + 1):
                    item.start()

            base = 0
            for piece, width in enumerate(widths):
                if piece >= 2:
                    self.out_copy(index, order, piece - 2).wait()
                left, right = self.left_buf[slot], self.right_buf[:, base : base + width]
                if kind:
                    self.out_buf[piece % 2, 0 : self.keep, 0:width] = dot_tn(left, right).astype(BF)
                else:
                    self.out_buf[piece % 2, 0:width, 0 : self.keep] = dot_tn(right, left).astype(BF)
                self.out_copy(index, order, piece).start()
                base += width
            for piece in range(max(0, len(widths) - 2), len(widths)):
                self.out_copy(index, order, piece).wait()
            self.send(index, order, "start")
            return 0

        lax.fori_loop(start, stop, one, 0)

    def all_sent(self, index):
        def one(order, _):
            self.send(index, order, "wait")
            return 0

        lax.fori_loop(0, self.dp, one, 0)

    def all_received(self, kind):
        ref = self.received[kind]
        theirs = ref.at[1 - self.core]
        ours = ref.at[self.core, pl.ds(0, self.dp - 1)]
        remote(theirs, theirs, self.send_sems.at[0, 0], self.recv_sems.at[kind, 1 - self.core], "pipe", 1 - self.core).wait_recv()
        if self.dp > 1:
            remote(ours, ours, self.send_sems.at[0, 0], self.recv_sems.at[kind, self.core], "pipe", 1 - self.core).wait_recv()


class SmallSums:
    def __init__(self, core, rank, dp_rank, dp_size, sums, from_peers, from_line, final, sems):
        self.core, self.rank, self.me, self.dp = core, rank, dp_rank, dp_size
        self.sums, self.from_peers, self.from_line, self.final = sums, from_peers, from_line, final
        self.peer_send, self.peer_recv, self.line_send, self.line_recv = sems

    def to_peer(self, layer, other, act):
        src = self.sums.at[layer]
        dst = self.from_peers.at[self.core, self.me]
        sem = self.peer_send.at[layer, other]
        at_home = (self.core == layer) & (other == self.me)

        @pl.when(at_home)
        def _():
            copy = pltpu.make_async_copy(src, dst, sem)
            copy.start() if act == "start" else copy.wait()

        @pl.when(jnp.logical_not(at_home))
        def _():
            copy = pltpu.make_async_remote_copy(
                src_ref=src,
                dst_ref=dst,
                send_sem=sem,
                recv_sem=self.peer_recv.at[self.core],
                device_id={"pipe": jnp.int32(layer), "dp": other},
                device_id_type=pl.DeviceIdType.MESH,
            )
            copy.start() if act == "start" else copy.wait_send()

    def peers(self, act):
        for layer in range(2):

            def one(other, _):
                self.to_peer(layer, other, act)
                return 0

            lax.fori_loop(0, self.dp, one, 0)

    def line_copy(self, other):
        return remote(
            self.from_line.at[LINE],
            self.from_line.at[self.rank],
            self.line_send.at[other],
            self.line_recv.at[self.rank],
            "tensor",
            other,
        )

    def pass_on(self):
        self.peers("wait")
        theirs = self.from_peers.at[1 - self.core]
        remote(theirs, theirs, self.peer_send.at[0, 0], self.peer_recv.at[1 - self.core], "pipe", 1 - self.core).wait_recv()
        if self.dp > 1:
            ours = self.from_peers.at[self.core, pl.ds(0, self.dp - 1)]
            remote(ours, ours, self.peer_send.at[0, 0], self.peer_recv.at[self.core], "pipe", 1 - self.core).wait_recv()
        total = self.from_peers[0, 0] + self.from_peers[1, 0]
        for i in range(1, self.dp):
            total = total + (self.from_peers[0, i] + self.from_peers[1, i])
        self.from_line[LINE] = total
        for other in range(LINE):

            @pl.when(self.rank != other)
            def _():
                self.line_copy(other).start()

    def finish(self):
        own = self.from_line[LINE]
        self.final[2:8, :] = own[2:8, :]
        self.final[0:2, :] = own[0:2, :]
        for other in range(LINE):

            @pl.when(self.rank != other)
            def _():
                self.line_copy(other).wait_send()
                block = self.from_line.at[other]
                remote(
                    block, block, self.line_send.at[other], self.line_recv.at[other], "tensor", other
                ).wait_recv()
                self.final[0:2, :] += self.from_line[other, 0:2, :]


RING = 3


def backward_kernel(dp_size, *refs):
    at = 0

    def take(count):
        nonlocal at
        at += count
        return refs[at - count : at]

    cot_ref, in_ref, x1_ref, part1_ref = take(4)
    slope_ref, q_ref, k_ref, v_ref, o_ref, logs_ref = take(6)
    own_w = take(4)
    other_w = take(4)
    h_near, h_far, act_near, act_far, o_near, o_far = take(6)
    vectors, cos_ref, near_ref, far_ref = take(4)
    acts_out, grads_out, dy0_out, dy0_far, du_near, du_far, dp_near, dp_far = take(8)
    stages = take(2)
    received = take(2)
    (final_ref,) = take(1)
    ring, ring_qkv, dense_w = take(3)
    up_buf, x_buf, slope_buf, q_buf, o_buf, logs_buf = take(6)
    k_all, v_all, dk_all, dv_all = take(4)
    do_buf, dp_buf, du_buf, part = take(4)
    mean_buf, inverse_buf, up_share, x_share = take(4)
    (result,) = take(1)
    sum_bufs = take(4)
    sum_sems = dict(zip(SUM_NAMES, take(6)))
    share_room, left_sems, right_sems, left1_sems, right1_sems, free_sem, early_sems = take(7)
    dot_bufs = take(3)
    dot_sems = take(5)
    ring_sems, qkv_sems, dense_sem, load_sems, kv_sems, out_sems = take(6)
    far_send, far_recv, once_sems, result_send, grads_sems, acts_sems = take(6)
    sums_ref, from_peers, from_line = take(3)
    small_sems = take(4)
    assert at == len(refs)
    w_qkv, w_fc1, w_dense, w_fc2 = range(4)
    core = lax.axis_index("pipe")
    rank = lax.axis_index("tensor")
    dp_rank = lax.axis_index("dp")
    theirs = 1 - core
    rows, width = up_buf.shape
    block = rows // LINE
    local = q_buf.shape[2]
    hidden = du_buf.shape[1]
    half_hidden, half_local = hidden // 2, local // 2
    tile = ring.shape[1]
    up_tiles, out_tiles = hidden // tile, width // tile
    ring_tiles = up_tiles + out_tiles
    scale = HEAD_DIM ** (-0.5)

    def layer_of(step):
        return 1 - lax.div(step, LINE)

    def chunk_of(step):
        return LINE - 1 - lax.rem(step, LINE)

    def chunk_rows(chunk):
        return pl.ds(pl.multiple_of(chunk * rows, rows), rows)

    def weight_copy(layer, views, target, sem, act):
        if act == "wait":
            pltpu.make_async_copy(views[0], target, sem).wait()
            return

        @pl.when(core == layer)
        def _():
            pltpu.make_async_copy(views[0], target, sem).start()

        @pl.when(core != layer)
        def _():
            pltpu.make_async_copy(views[1], target, sem).start()

    def ring_copy(index, act):
        step, place = lax.div(index, ring_tiles), lax.rem(index, ring_tiles)
        slot = lax.rem(index, RING)
        target, sem = ring.at[slot], ring_sems.at[slot]
        layer = layer_of(step)
        if act == "wait":
            weight_copy(layer, [own_w[w_fc2].at[0:tile]], target, sem, act)
            return

        @pl.when(place < up_tiles)
        def _():
            span = pl.ds(pl.multiple_of(place * tile, tile), tile)
            weight_copy(layer, [own_w[w_fc2].at[span], other_w[w_fc2].at[span]], target, sem, act)

        @pl.when(place >= up_tiles)
        def _():
            span = pl.ds(pl.multiple_of((place - up_tiles) * tile, tile), tile)
            weight_copy(layer, [own_w[w_fc1].at[span], other_w[w_fc1].at[span]], target, sem, act)

    def qkv_copy(index, act):
        step, place = lax.div(index, out_tiles), lax.rem(index, out_tiles)
        slot = lax.rem(index, 2)
        span = pl.ds(pl.multiple_of(place * tile, tile), tile)
        views = [w[w_qkv].at[:, span, :] for w in (own_w, other_w)]
        weight_copy(layer_of(step), views, ring_qkv.at[slot], qkv_sems.at[slot], act)

    def dense_copy(layer, act):
        weight_copy(layer, [own_w[w_dense], other_w[w_dense]], dense_w, dense_sem.at[0], act)

    def kv_copies(layer):
        return [
            pltpu.make_async_copy(k_ref.at[layer], k_all, kv_sems.at[0]),
            pltpu.make_async_copy(v_ref.at[layer], v_all, kv_sems.at[1]),
        ]

    def early_loads(step):
        layer, slot = layer_of(step), 0
        at_rows = chunk_rows(chunk_of(step))
        return [
            pltpu.make_async_copy(q_ref.at[layer, at_rows], q_buf.at[slot], load_sems.at[0, slot]),
            pltpu.make_async_copy(o_ref.at[layer, at_rows], o_buf.at[slot], load_sems.at[1, slot]),
            pltpu.make_async_copy(
                logs_ref.at[layer, :, :, at_rows], logs_buf.at[slot], load_sems.at[2, slot]
            ),
        ]

    def slope_load(step):
        return pltpu.make_async_copy(
            slope_ref.at[layer_of(step), chunk_rows(chunk_of(step))], slope_buf, load_sems.at[3, 0]
        )

    def x_load(src):
        return pltpu.make_async_copy(src, x_buf, load_sems.at[4, 0])

    def up_load(src):
        return pltpu.make_async_copy(src, up_buf, load_sems.at[5, 0])

    def norm_back(layer, rows_x, rows_up, total):
        values = rows_x.astype(F32)
        centre = values - jnp.mean(values, axis=-1, keepdims=True)
        inverse = lax.rsqrt(jnp.mean(centre * centre, axis=-1, keepdims=True) + ln_eps)
        xhat = centre * inverse
        e = total * vectors[layer, 0:1, 0:width]
        back = e - jnp.mean(e, axis=-1, keepdims=True) - xhat * jnp.mean(
            e * xhat, axis=-1, keepdims=True
        )
        return (rows_up.astype(F32) + inverse * back).astype(BF)

    def finish(chunk, total, target):
        target[...] = norm_back(1, x_share[chunk], up_share[chunk], total)

    summed = LineSum(rank, part, *sum_bufs, result, sum_sems, finish)
    shared = LineShare(rank, part, share_room, (left_sems, right_sems), out_tiles)
    dots = PairDots(core, dp_rank, dp_size, *dot_bufs, dot_sems, stages, received)
    shared1 = LineShare(rank, part, share_room, (left1_sems, right1_sems), out_tiles)

    mine = chunk_rows(rank)
    early_loads_ = [
        pltpu.make_async_copy(part1_ref.at[(LINE - 1) * rows : LINE * rows], part.at[0], once_sems.at[0]),
        pltpu.make_async_copy(part1_ref.at[0:rows], part.at[1], once_sems.at[1]),
        pltpu.make_async_copy(x1_ref.at[mine], part.at[2], once_sems.at[2]),
    ]

    def early_copy(way, piece, first):
        slot = LINE - 1 if way == 0 else 0
        span = pl.ds(pl.multiple_of(piece * tile, tile), tile)
        src = part.at[way, :, span] if first else share_room.at[slot, :, span]
        to = jnp.clip(rank + 1 - 2 * way, 0, LINE - 1)
        return remote(
            src,
            share_room.at[slot, :, span],
            early_sems.at[way, 0, piece],
            early_sems.at[way, 1, piece],
            "tensor",
            to,
        )

    def early_emit():
        for item in early_loads_:
            item.wait()
        for way, (end, goal) in enumerate(((0, LINE - 1), (LINE - 1, 0))):

            @pl.when(rank == end)
            def _():
                for piece in range(out_tiles):
                    early_copy(way, piece, True).start()

            @pl.when(rank == goal)
            def _():
                small = rows // 8

                def one(i, _):
                    span = pl.ds(pl.multiple_of(i * small, small), small)
                    value = part[way, span, :].astype(F32) + part[2, span, :].astype(F32)
                    share_room[LINE, span, :] = (value + vectors[1, 3:4, 0:width]).astype(BF)
                    return 0

                lax.fori_loop(0, 8, one, 0)

    def early_relay(way, device):
        @pl.when(rank == device)
        def _():
            slot = LINE - 1 if way == 0 else 0

            def one(piece, _):
                copy = early_copy(way, piece, False)
                copy.wait_recv()
                span = pl.ds(pl.multiple_of(piece * tile, tile), tile)
                share_room[slot, :, span] = (
                    share_room[slot, :, span].astype(F32) + part[way, :, span].astype(F32)
                ).astype(BF)
                copy.start()
                return 0

            lax.fori_loop(0, out_tiles, one, 0)

    def early_sent(way, devices):
        for device in devices:

            @pl.when(rank == device)
            def _():
                for piece in range(out_tiles):
                    early_copy(way, piece, device == (0 if way == 0 else LINE - 1)).wait_send()

    def early_deliver(act):
        for way, goal in enumerate((LINE - 1, 0)):

            @pl.when(rank == goal)
            def _():
                deliver(core, 1, share_room.at[goal], acts_out, acts_sems, act)

    def early_finish():
        for way, goal in enumerate((LINE - 1, 0)):

            @pl.when(rank == goal)
            def _():
                for piece in range(out_tiles):
                    early_copy(way, piece, False).wait_recv()
                small = rows // 8

                def one(i, _):
                    span = pl.ds(pl.multiple_of(i * small, small), small)
                    value = share_room[LINE, span, :].astype(F32) + share_room[goal, span, :].astype(F32)
                    share_room[goal, span, :] = value.astype(BF)
                    return 0

                lax.fori_loop(0, 8, one, 0)

        early_deliver("start")

    smalls = SmallSums(
        core, rank, dp_rank, dp_size, sums_ref, from_peers, from_line, final_ref, small_sems
    )
    dots.add(0, 1, 0, (cot_ref.at[core], cot_ref.at[theirs]), [(act_near.at[1], act_far.at[1]), (o_near.at[1], o_far.at[1])])
    dots.add(2, 0, 0, (dy0_out, dy0_far), [(act_near.at[0], act_far.at[0]), (o_near.at[0], o_far.at[0])])
    for index, layer in ((1, 1), (3, 0)):
        dots.add(
            index,
            layer,
            1,
            (h_near.at[layer], h_far.at[layer]),
            [(du_near.at[layer], du_far.at[layer])]
            + [(dp_near.at[layer, c], dp_far.at[layer, c]) for c in range(3)],
        )

    def half(which, size):
        return pl.ds(pl.multiple_of(which * size, size), size)

    def dp_copies(step):
        layer, at_rows = layer_of(step), chunk_rows(chunk_of(step))
        return [
            pltpu.make_async_copy(
                dp_buf.at[:, :, half(core, half_local)], dp_near.at[layer, :, at_rows], out_sems.at[0]
            ),
            remote(
                dp_buf.at[:, :, half(theirs, half_local)],
                dp_far.at[layer, :, at_rows],
                far_send.at[0],
                far_recv.at[0, layer],
                "pipe",
                theirs,
            ),
        ]

    def du_copies(step):
        layer, at_rows = layer_of(step), chunk_rows(chunk_of(step))
        return [
            pltpu.make_async_copy(
                du_buf.at[:, half(core, half_hidden)], du_near.at[layer, at_rows], out_sems.at[1]
            ),
            remote(
                du_buf.at[:, half(theirs, half_hidden)],
                du_far.at[layer, at_rows],
                far_send.at[1],
                far_recv.at[1, layer],
                "pipe",
                theirs,
            ),
        ]

    def result_copies(chunk):
        at_rows = chunk_rows(chunk)
        return [
            pltpu.make_async_copy(result.at[at_rows], dy0_out.at[at_rows], once_sems.at[chunk]),
            remote(
                result.at[at_rows],
                dy0_far.at[at_rows],
                result_send.at[chunk],
                far_recv.at[2, 0],
                "pipe",
                theirs,
            ),
        ]

    def start_all(copies):
        for item in copies:
            item.start()

    def left_all(copies):
        copies[0].wait()
        copies[1].wait_send()

    def far_arrived(i, layer, ref):
        remote(ref, ref, far_send.at[0], far_recv.at[i, layer], "pipe", theirs).wait_recv()

    start_all(early_loads_)
    dense_copy(1, "start")
    up_load(cot_ref.at[core, (LINE - 1) * rows : LINE * rows]).start()
    start_all(early_loads(jnp.int32(0)))
    slope_load(jnp.int32(0)).start()
    start_all(kv_copies(1))
    for i in range(RING - 1):
        ring_copy(jnp.int32(i), "start")
    qkv_copy(jnp.int32(0), "start")
    dots.prime(0)

    barrier = pltpu.get_barrier_semaphore()

    def tell(where):
        pl.semaphore_signal(barrier, inc=1, device_id=where, device_id_type=pl.DeviceIdType.MESH)

    def tell_peer(other, _):
        tell({"pipe": theirs, "dp": other})

        @pl.when(other != dp_rank)
        def _():
            tell({"dp": other})

        return 0

    lax.fori_loop(0, dp_size, tell_peer, 0)

    for other in range(LINE):

        @pl.when(rank != other)
        def _():
            tell({"tensor": jnp.int32(other)})

    pl.semaphore_wait(barrier, 2 * dp_size - 1 + LINE - 1)

    early_emit()
    sums_ref[...] = jnp.zeros_like(sums_ref)

    keep = lax.broadcasted_iota(jnp.int32, (rows, rows), 0) <= lax.broadcasted_iota(
        jnp.int32, (rows, rows), 1
    )

    def attention(chunk, slot):
        here = slice(chunk * rows, (chunk + 1) * rows)
        spans = ([(slice(0, chunk * rows), False)] if chunk else []) + [(here, True)]
        tables = (cos_ref[here, :], -near_ref[here, :], -far_ref[here, :])

        def pair(j, _):
            lanes = pl.ds(pl.multiple_of(j * LANES, LANES), LANES)
            query, upstream = q_buf[slot, :, lanes], do_buf[:, lanes]
            product = upstream.astype(F32) * o_buf[slot, :, lanes].astype(F32)
            grads = []
            key_terms = [None] * len(spans)
            value_terms = [None] * len(spans)
            for which in range(LANES // HEAD_DIM):
                mask = head_mask(rows, which)
                mine = jnp.where(mask, query, jnp.zeros_like(query))
                mine_up = jnp.where(mask, upstream, jnp.zeros_like(upstream))
                logs = logs_buf[slot, j, which : which + 1, :]
                centre = as_row(jnp.sum(jnp.where(mask, product, 0.0), axis=1, keepdims=True))
                grad = None
                for i, (span, diagonal) in enumerate(spans):
                    keys = k_all[span, lanes]
                    probs = jnp.exp(dot_nt(keys, mine) - logs)
                    if diagonal:
                        probs = jnp.where(keep, probs, 0.0)
                    grad_probs = dot_nt(v_all[span, lanes], mine_up)
                    grad_scores = (probs * (grad_probs - centre)).astype(BF)
                    value_term = dot_nn(probs.astype(BF), mine_up)
                    key_term = dot_nn(grad_scores, mine)
                    term = dot_tn(grad_scores, keys)
                    grad = term if grad is None else grad + term
                    if which == 0:
                        key_terms[i], value_terms[i] = key_term, value_term
                    else:
                        dk_all[span, lanes] += key_terms[i] + key_term
                        dv_all[span, lanes] += value_terms[i] + value_term
                grads.append(grad)
            merged = jnp.where(head_mask(rows, 0), grads[0], grads[1]) * scale
            dp_buf[0, :, lanes] = turn(merged, *tables).astype(BF)
            dp_buf[1, :, lanes] = turn(dk_all[here, lanes], *tables).astype(BF)
            dp_buf[2, :, lanes] = dv_all[here, lanes].astype(BF)
            return 0

        lax.fori_loop(0, local // LANES, pair, 0)


    def step_body(step, _):
        layer, chunk, slot = layer_of(step), chunk_of(step), 0
        lead = layer == 1
        starting = lax.rem(step, LINE) == 0
        at_rows = chunk_rows(chunk)

        @pl.when(step == LINE)
        def _():
            early_deliver("wait")
            left_all(dp_copies(step - 1))
            left_all(du_copies(step - 1))
            far_arrived(0, 1, dp_far.at[1])
            far_arrived(1, 1, du_far.at[1])
            dots.prime(1)

        @pl.when(step >= LINE)
        def _():
            summed.stage_f(chunk)
            start_all(result_copies(chunk))
            up_buf[...] = result[at_rows, :]
            x_load(in_ref.at[core, at_rows]).start()

        @pl.when(lead)
        def _():
            up_load(cot_ref.at[core, at_rows]).wait()
            x_load(x1_ref.at[at_rows]).start()

        @pl.when(starting)
        def _():
            dense_copy(layer, "wait")
            dk_all[...] = jnp.zeros_like(dk_all)
            dv_all[...] = jnp.zeros_like(dv_all)

        slope_load(step).wait()

        @pl.when((step >= 1) & (step != LINE))
        def _():
            left_all(du_copies(step - 1))

        def hidden_part(i, _):
            cols = pl.ds(pl.multiple_of(i * tile, tile), tile)
            index = step * ring_tiles + i
            ring_copy(index, "wait")
            ring_copy(index + RING - 1, "start")
            weight = ring.at[lax.rem(index, RING)]
            value = dot_nt(up_buf[...], weight[...]) * slope_buf[:, cols].astype(F32)
            value = value.astype(BF)
            du_buf[:, cols] = value
            sums_ref[layer, 2:3, cols] += jnp.sum(value.astype(F32), axis=0, keepdims=True)
            return 0

        lax.fori_loop(0, up_tiles, hidden_part, 0)
        start_all(du_copies(step))

        @pl.when(step + 1 < STEPS)
        def _():
            slope_load(step + 1).start()

        @pl.when(step == STEPS - 1)
        def _():
            for c in range(LINE):
                left_all(result_copies(c))
            far_arrived(2, 0, dy0_far)
            dots.prime(2)

        do_buf[...] = dot_nt(up_buf[...], dense_w[...]).astype(BF)

        @pl.when(step == LINE - 1)
        def _():
            dense_copy(jnp.int32(0), "start")

        sums_ref[layer, 3:4, :] += jnp.sum(up_buf[...].astype(F32), axis=0, keepdims=True)

        @pl.when(lead)
        def _():
            up_share[chunk] = up_buf[pl.ds(pl.multiple_of(rank * block, block), block), :]

        @pl.when(step + 1 < LINE)
        def _():
            up_load(cot_ref.at[core, chunk_rows(chunk - 1)]).start()

        for item in early_loads(step):
            item.wait()

        @pl.when(starting)
        def _():
            for item in kv_copies(layer):
                item.wait()

        @pl.when((step >= 1) & (step != LINE))
        def _():
            left_all(dp_copies(step - 1))

        for index in range(LINE):

            @pl.when(chunk == index)
            def _():
                attention(index, slot)

        start_all(dp_copies(step))

        @pl.when(step + 1 < STEPS)
        def _():
            start_all(early_loads(step + 1))

        @pl.when(step == LINE - 1)
        def _():
            start_all(kv_copies(jnp.int32(0)))

        for i in range(3):
            sums_ref[layer, 4 + i : 5 + i, 0:local] += jnp.sum(
                dp_buf[i].astype(F32), axis=0, keepdims=True
            )

        @pl.when((step >= 1) & (step <= LINE))
        def _():
            summed.stage_b(chunk_of(step - 1))

        @pl.when((step >= 2) & (step <= LINE + 1))
        def _():
            summed.stage_d(chunk_of(step - 2))

        @pl.when((step >= 3) & (step <= LINE + 2))
        def _():
            summed.stage_e(chunk_of(step - 3), 1)

        @pl.when(step > LINE)
        def _():
            shared.relay(chunk_of(step - 1), 1)

        @pl.when(lead)
        def _():
            dots.run(0, lax.div(step * dp_size, LINE), lax.div((step + 1) * dp_size, LINE))

        @pl.when((step >= LINE) & (step < STEPS - 1))
        def _():
            begin = jnp.where(step == LINE, 0, lax.div((step - LINE + 1) * dp_size, LINE))
            dots.run(1, begin, lax.div((step - LINE + 2) * dp_size, LINE))

        @pl.when(step == STEPS - 1)
        def _():
            dots.run(2, 0, dp_size)
            left_all(dp_copies(step))
            left_all(du_copies(step))
            far_arrived(0, 0, dp_far.at[0])
            far_arrived(1, 0, du_far.at[0])
            dots.prime(3)

        @pl.when(step == 2)
        def _():
            early_sent(1, (LINE - 1,))

        @pl.when(step == 3)
        def _():
            early_finish()
            early_sent(0, (0, 1, 2))
            early_sent(1, (2, 1))

        x_load(x1_ref.at[at_rows]).wait()
        small = rows // 8

        def statistics(i, _):
            span = pl.ds(pl.multiple_of(i * small, small), small)
            values = x_buf[span, :].astype(F32)
            mean = jnp.mean(values, axis=-1, keepdims=True)
            centre = values - mean
            mean_buf[span, :] = mean
            inverse_buf[span, :] = lax.rsqrt(
                jnp.mean(centre * centre, axis=-1, keepdims=True) + ln_eps
            )
            return 0

        lax.fori_loop(0, 8, statistics, 0)

        @pl.when(lead)
        def _():
            x_share[chunk] = x_buf[pl.ds(pl.multiple_of(rank * block, block), block), :]

        @pl.when(jnp.logical_not(lead))
        def _():
            summed.sent_part(chunk)

        def normed_part(i, _):
            cols = pl.ds(pl.multiple_of(i * tile, tile), tile)
            index = step * ring_tiles + up_tiles + i
            ring_copy(index, "wait")

            @pl.when(index + RING - 1 < STEPS * ring_tiles)
            def _():
                ring_copy(index + RING - 1, "start")

            qkv_index = step * out_tiles + i
            qkv_copy(qkv_index, "wait")

            @pl.when(qkv_index + 1 < STEPS * out_tiles)
            def _():
                qkv_copy(qkv_index + 1, "start")

            value = dot_nt(du_buf[...], ring[lax.rem(index, RING)])
            for c in range(3):
                value = value + dot_nt(dp_buf[c], ring_qkv[lax.rem(qkv_index, 2), c])
            xhat = (x_buf[:, cols].astype(F32) - mean_buf[...]) * inverse_buf[...]
            sums_ref[layer, 0:1, cols] += jnp.sum(value * xhat, axis=0, keepdims=True)
            sums_ref[layer, 1:2, cols] += jnp.sum(value, axis=0, keepdims=True)
            part[chunk, :, cols] = value.astype(BF)

            @pl.when(jnp.logical_not(lead))
            def _():
                shared.emit(chunk, i)

            return 0

        lax.fori_loop(0, out_tiles, normed_part, 0)

        @pl.when(lead)
        def _():
            summed.stage_a(chunk)

        @pl.when((step >= 1) & (step <= LINE))
        def _():
            summed.stage_c(chunk_of(step - 1))

        @pl.when((step >= 2) & (step <= LINE + 1))
        def _():
            summed.stage_e(chunk_of(step - 2), 0)

        @pl.when(step == 0)
        def _():
            early_relay(0, 1)
            early_relay(1, 2)

        @pl.when(step == 1)
        def _():
            early_relay(0, 2)
            early_relay(1, 1)

        @pl.when(step > LINE)
        def _():
            shared.relay(chunk_of(step - 1), 2)

        return 0

    lax.fori_loop(0, STEPS, step_body, 0)

    smalls.peers("start")
    deliver(core, 1, result.at[mine], grads_out, grads_sems, "start")
    deliver(core, 0, x1_ref.at[mine], acts_out, acts_sems, "start")
    reload = [up_load(result.at[mine]), x_load(in_ref.at[core, mine])]
    start_all(reload)
    some = dp_size // 2
    dots.run(3, 0, some)
    shared.relay(0, 1)
    dots.run(3, some, dp_size)
    shared.relay(0, 2)
    smalls.pass_on()
    shared.arrived()
    for item in reload:
        item.wait()
    small = rows // 8

    def last(i, _):
        span = pl.ds(pl.multiple_of(i * small, small), small)
        up_buf[span, :] = norm_back(0, x_buf[span, :], up_buf[span, :], shared.total(span))
        return 0

    lax.fori_loop(0, 8, last, 0)
    deliver(core, 0, up_buf, grads_out, grads_sems, "start")
    for chunk in range(LINE):
        shared.sent(chunk)

    x1_mine = x_load(x1_ref.at[mine])
    x1_mine.start()
    part_loads = [
        pltpu.make_async_copy(
            part1_ref.at[c * rows : (c + 1) * rows], part.at[c], once_sems.at[c]
        )
        for c in (1, 2)
    ]
    start_all(part_loads)
    for offset in (-1, 1):
        other = rank + offset

        @pl.when((other >= 0) & (other < LINE))
        def _():
            pl.semaphore_signal(
                free_sem, inc=1, device_id={"tensor": other}, device_id_type=pl.DeviceIdType.MESH
            )

    for item in part_loads:
        item.wait()
    pl.semaphore_wait(
        free_sem, jnp.where(rank > 0, 1, 0) + jnp.where(rank < LINE - 1, 1, 0)
    )
    for chunk in (2, 1):

        def emit(piece, _):
            shared1.emit(chunk, piece)
            return 0

        lax.fori_loop(0, out_tiles, emit, 0)
    smalls.finish()
    for chunk in (2, 1):
        shared1.relay(chunk, 1)
    middle = (rank == 1) | (rank == 2)

    @pl.when(middle)
    def _():
        shared1.arrived()

    x1_mine.wait()
    deliver(core, 0, up_buf, grads_out, grads_sems, "wait")

    def last_rows(i, _):
        span = pl.ds(pl.multiple_of(i * small, small), small)
        value = x_buf[span, :].astype(F32) + shared1.total(span) + vectors[1, 3:4, 0:width]
        up_buf[span, :] = value.astype(BF)
        return 0

    @pl.when(middle)
    def _():
        lax.fori_loop(0, 8, last_rows, 0)
        deliver(core, 1, up_buf, acts_out, acts_sems, "start")

    deliver(core, 1, result.at[mine], grads_out, grads_sems, "wait")
    deliver(core, 0, x1_ref.at[mine], acts_out, acts_sems, "wait")

    @pl.when(middle)
    def _():
        deliver(core, 1, up_buf, acts_out, acts_sems, "wait")

    delivered(core, grads_out, grads_sems)
    delivered(core, acts_out, acts_sems)
    for chunk in range(LINE):
        summed.sent_rest(chunk)
        if chunk in (1, 2):
            shared1.sent(chunk)
    for index in range(4):
        dots.all_sent(index)
    for kind in range(2):
        dots.all_received(kind)


def backward_both(
    dp_size, cotangent, inputs, x1, part1, saved, own_w, other_w, sides, vectors, tables
):
    slope, query, key, value, merged, logs = saved
    _, length, width = inputs.shape
    w_qkv, w_fc1, w_dense, w_fc2 = own_w
    local, hidden = w_dense.shape[0], w_fc1.shape[1]
    rows = length // LINE
    block = rows // LINE
    pairs = local // LANES
    tile = min(TILE, width)
    out_tiles = width // tile
    keep = width // dp_size
    down, up = hidden // 2 + local // 2, hidden // 2 + 3 * (local // 2)

    def bf(*shape):
        return jax.ShapeDtypeStruct(shape, BF)

    def room(*shape):
        return pltpu.VMEM(shape, BF)

    whole = pl.BlockSpec(memory_space=pltpu.VMEM)
    away = pl.BlockSpec(memory_space=pl.ANY)
    dma = pltpu.SemaphoreType.DMA
    outs = [
        bf(2, rows, width),
        bf(2, rows, width),
        bf(length, width),
        bf(length, width),
        bf(2, length, hidden // 2),
        bf(2, length, hidden // 2),
        bf(2, 3, length, local // 2),
        bf(2, 3, length, local // 2),
        bf(2, dp_size, down, keep),
        bf(2, dp_size, keep, up),
        bf(2, dp_size, down, keep),
        bf(2, dp_size, keep, up),
    ]
    most = max(width, hidden)
    return pl.pallas_call(
        functools.partial(backward_kernel, dp_size),
        name="backward_both",
        in_specs=[away] * 24 + [whole] * 4,
        out_specs=[away] * len(outs) + [whole],
        out_shape=outs + [jax.ShapeDtypeStruct((8, most), F32)],
        scratch_shapes=[
            room(RING, tile, width),
            room(2, 3, tile, local),
            room(local, width),
            room(rows, width),
            room(rows, width),
            room(rows, hidden),
            room(1, rows, local),
            room(1, rows, local),
            pltpu.VMEM((1, pairs, 8, rows), F32),
            room(length, local),
            room(length, local),
            pltpu.VMEM((length, local), F32),
            pltpu.VMEM((length, local), F32),
            room(rows, local),
            room(3, rows, local),
            room(rows, hidden),
            room(LINE, rows, width),
            pltpu.VMEM((rows, 1), F32),
            pltpu.VMEM((rows, 1), F32),
            room(LINE, block, width),
            room(LINE, block, width),
            room(length, width),
        ]
        + line_sum_scratch(rows, width)
        + [room(LINE + 1, rows, width)]
        + [dma((2, LINE * out_tiles))] * 4
        + [pltpu.SemaphoreType.REGULAR, dma((2, 2, out_tiles))]
        + [
            room(2, 2 * length, keep),
            room(2 * length, max(down, up)),
            room(2, max(keep, TILE), max(keep, TILE)),
            dma((2, 2)),
            dma((8,)),
            dma((2,)),
            dma((4, dp_size)),
            dma((2, 2)),
        ]
        + [
            dma((RING,)),
            dma((2,)),
            dma((1,)),
            dma((6, 2)),
            dma((2,)),
            dma((2,)),
            dma((2,)),
            dma((3, 2)),
            dma((LINE,)),
            dma((LINE,)),
            dma((3,)),
            dma((3,)),
            pltpu.VMEM((2, 8, most), F32),
            pltpu.VMEM((2, dp_size, 8, most), F32),
            pltpu.VMEM((LINE + 1, 8, most), F32),
            dma((2, dp_size)),
            dma((2,)),
            dma((LINE,)),
            dma((LINE,)),
        ],
        compiler_params=pltpu.CompilerParams(
            collective_id=1, has_side_effects=True, vmem_limit_bytes=63 * MIB
        ),
        cost_estimate=pl.CostEstimate(
            flops=16 * length * width * (4 * local + 2 * hidden),
            bytes_accessed=400 * MIB,
            transcendentals=0,
        ),
    )(
        cotangent, inputs, x1, part1, slope, query, key, value, merged, logs, *own_w, *other_w, *sides, vectors, *tables
    )


def some_rows_total(got_ref, start):
    span = pl.ds(pl.multiple_of(start, 16), 16)
    total = got_ref[0, 0, span, :].astype(F32)
    for sender in range(1, got_ref.shape[1]):
        total = total + got_ref[0, sender, span, :].astype(F32)
    return span, total


def down_kernel(got_ref, wide_ref, narrow_ref):
    last = pl.num_programs(1) - 1

    def fill(out_ref):
        def one(i, _):
            span, total = some_rows_total(got_ref, i * 16)
            out_ref[span, :] = total
            return 0

        lax.fori_loop(0, out_ref.shape[0] // 16, one, 0)

    @pl.when(pl.program_id(1) < last)
    def _():
        fill(wide_ref)

    @pl.when(pl.program_id(1) == last)
    def _():
        fill(narrow_ref)


def down_total(got, hidden, local):
    _, peers, _, keep = got.shape
    side = local // 2
    blocks = hidden // 2 // side
    return pl.pallas_call(
        down_kernel,
        name="down_total",
        grid=(2, blocks + 1),
        in_specs=[pl.BlockSpec((1, peers, side, keep), lambda part, i: (part, 0, i, 0))],
        out_specs=[
            pl.BlockSpec((side, keep), lambda part, i: (part * blocks + jnp.minimum(i, blocks - 1), 0)),
            pl.BlockSpec((side, keep), lambda part, i: (part, 0)),
        ],
        out_shape=[
            jax.ShapeDtypeStruct((hidden, keep), F32),
            jax.ShapeDtypeStruct((local, keep), F32),
        ],
    )(got)


def up_kernel(got_ref, wide_ref, three_ref):
    cut, side = wide_ref.shape[1], three_ref.shape[2]

    def one(i, _):
        span, total = some_rows_total(got_ref, i * 16)
        wide_ref[span, :] = total[:, :cut]
        for c in range(3):
            three_ref[c, span, :] = total[:, cut + c * side : cut + (c + 1) * side]
        return 0

    lax.fori_loop(0, wide_ref.shape[0] // 16, one, 0)


def up_total(got, hidden, local):
    _, peers, keep, cols = got.shape
    some = min(128, keep)
    return pl.pallas_call(
        up_kernel,
        name="up_total",
        grid=(2, keep // some),
        in_specs=[pl.BlockSpec((1, peers, some, cols), lambda part, i: (part, 0, i, 0))],
        out_specs=[
            pl.BlockSpec((some, hidden // 2), lambda part, i: (i, part)),
            pl.BlockSpec((3, some, local // 2), lambda part, i: (0, i, part)),
        ],
        out_shape=[
            jax.ShapeDtypeStruct((keep, hidden), F32),
            jax.ShapeDtypeStruct((3, keep, local), F32),
        ],
    )(got)


def body(
    inputs, cotangent, ln_gain, ln_bias, w_qkv, b_qkv, w_dense, b_dense, w_fc1, b_fc1, w_fc2, b_fc2
):
    core = lax.axis_index("pipe")
    rank = lax.axis_index("tensor")
    dp_size = lax.axis_size("dp")
    dp_rank = lax.axis_index("dp")
    _, length, width = inputs.shape
    lines = lax.axis_size("tensor")
    local = w_qkv.shape[3]
    hidden = w_fc1.shape[2]

    tables = rotary_tables(length)
    own_w = (w_qkv[0], w_fc1[0], w_dense[0], w_fc2[0])

    results = forward_both(
        inputs, own_w, (ln_gain, ln_bias, b_qkv, b_dense, b_fc1, b_fc2), tables
    )
    other_w = results[:4]
    h, h_far, query, key, value, merged, merged_near, merged_far = results[4:12]
    act_near, act_far, slope, logs, x1, part1, vectors = results[12:]
    saved = (slope, query, key, value, merged, logs)

    sides = (h, h_far, act_near, act_far, merged_near, merged_far)
    grads = backward_both(
        dp_size, cotangent, inputs, x1, part1, saved, own_w, other_w, sides, vectors, tables
    )
    acts, grads_in = grads[:2]
    down, up, sums = grads[10:]
    out_fc2, out_dense = down_total(down, hidden, local)
    out_fc1, out_qkv = up_total(up, hidden, local)
    place = rank * dp_size + dp_rank

    def piece(rows, count, index, parts):
        size = count // parts
        return lax.dynamic_slice_in_dim(rows[:, :count], index * size, size, 1)

    out_norm = piece(sums[0:2], width, place, lines * dp_size)
    out_bfc1 = piece(sums[2:3], hidden, dp_rank, dp_size)
    out_bout = piece(sums[3:4], width, dp_rank, dp_size)
    out_bqkv = piece(sums[4:7], local, dp_rank, dp_size)
    return (
        acts[None],
        grads_in[None],
        out_norm[0:1],
        out_norm[1:2],
        out_qkv[None],
        out_bqkv[None],
        out_dense[None],
        out_bout,
        out_fc1[None],
        out_bfc1,
        out_fc2[None],
        out_bout,
    )


def solution(mesh):
    in_specs = (
        P("dp", None, None),
        P("dp", None, None),
        P("pipe", None),
        P("pipe", None),
        P("pipe", None, None, "tensor"),
        P("pipe", None, "tensor"),
        P("pipe", "tensor", None),
        P("pipe", None),
        P("pipe", None, "tensor"),
        P("pipe", "tensor"),
        P("pipe", "tensor", None),
        P("pipe", None),
    )
    out_specs = (
        P("pipe", "dp", "tensor", None),
        P("pipe", "dp", "tensor", None),
        P("pipe", ("tensor", "dp")),
        P("pipe", ("tensor", "dp")),
        P("pipe", None, "dp", "tensor"),
        P("pipe", None, ("tensor", "dp")),
        P("pipe", "tensor", "dp"),
        P("pipe", "dp"),
        P("pipe", "dp", "tensor"),
        P("pipe", ("tensor", "dp")),
        P("pipe", "tensor", "dp"),
        P("pipe", "dp"),
    )
    return jax.shard_map(body, mesh=mesh, in_specs=in_specs, out_specs=out_specs, check_vma=False)
```

```python
import functools

import jax
import jax.numpy as jnp
from jax import lax
from jax.experimental import pallas as pl
from jax.experimental.pallas import tpu as pltpu
from jax.sharding import PartitionSpec as P

HEAD_DIM = 64
ROT = 32
LANES = 128
MIB = 1024 * 1024

ln_eps = 1e-05
rope_base = 10000.0
gelu_coef = 0.7978845608028654
masked_score = -1e30

BF = jnp.bfloat16
F32 = jnp.float32


def rotary_tables(length):
    half_rot = ROT // 2
    place = jnp.arange(LANES, dtype=jnp.int32) % HEAD_DIM
    inverse = rope_base ** (-((place % half_rot).astype(F32) * 2.0 / ROT))
    angles = jnp.arange(length, dtype=F32)[:, None] * inverse[None, :]
    cosines, sines = jnp.cos(angles), jnp.sin(angles)
    place = place[None, :]
    return (
        jnp.where(place < ROT, cosines, 1.0),
        jnp.where(place < half_rot, -sines, 0.0),
        jnp.where((place >= half_rot) & (place < ROT), sines, 0.0),
    )


def turn(values, cos, near, far):
    half_rot = ROT // 2
    return (
        values * cos
        + pltpu.roll(values, LANES - half_rot, 1) * near
        + pltpu.roll(values, half_rot, 1) * far
    )


def head_mask(rows, which):
    lanes = lax.broadcasted_iota(jnp.int32, (rows, LANES), 1)
    return (lanes // HEAD_DIM) == which


def as_row(column):
    return jnp.transpose(jnp.broadcast_to(column, (column.shape[0], LANES)))[0:1, :]


def dot_nt(left, right):
    return lax.dot_general(left, right, (((1,), (1,)), ((), ())), preferred_element_type=F32)


def dot_nn(left, right):
    return lax.dot_general(left, right, (((1,), (0,)), ((), ())), preferred_element_type=F32)


def dot_tn(left, right):
    return lax.dot_general(left, right, (((0,), (0,)), ((), ())), preferred_element_type=F32)


LINE = 4
STEPS = 2 * LINE
TILE = 512
SUM_PIECES = 2


def remote(src, dst, send, recv, axis, index):
    return pltpu.make_async_remote_copy(
        src_ref=src,
        dst_ref=dst,
        send_sem=send,
        recv_sem=recv,
        device_id={axis: index},
        device_id_type=pl.DeviceIdType.MESH,
    )


def greet(core, rank):
    barrier = pltpu.get_barrier_semaphore()

    def tell(axis, index):
        pl.semaphore_signal(
            barrier, inc=1, device_id={axis: index}, device_id_type=pl.DeviceIdType.MESH
        )

    tell("pipe", 1 - core)

    @pl.when(rank > 0)
    def _():
        tell("tensor", rank - 1)

    @pl.when(rank < LINE - 1)
    def _():
        tell("tensor", rank + 1)

    ends = jnp.where(rank > 0, 1, 0) + jnp.where(rank < LINE - 1, 1, 0)
    pl.semaphore_wait(barrier, 1 + ends)


def fetch_weight(layer, core, own, other, target, sem, arrival):
    @pl.when(core == layer)
    def _():
        pltpu.make_async_copy(own, target, sem).start()

    @pl.when(core != layer)
    def _():
        if arrival is not None:
            arrival.wait_recv()
        pltpu.make_async_copy(other, target, sem).start()


class LineSum:
    def __init__(self, rank, part, first, beside, second, last, result, sems, finish):
        self.rank, self.part, self.result, self.finish = rank, part, result, finish
        self.first, self.beside, self.second, self.last = first, beside, second, last
        self.sems = sems
        self.rows = part.shape[1]
        self.block = self.rows // LINE
        self.cols = part.shape[2] // SUM_PIECES
        half = 2 * self.block
        self.left = rank < 2
        self.far = pl.multiple_of(jnp.where(self.left, half, 0), half)
        self.near = pl.multiple_of(jnp.where(self.left, 0, half), half)
        self.own = pl.multiple_of(rank * self.block, self.block)
        self.inner = (rank == 1) | (rank == 2)
        self.outer = (rank == 0) | (rank == 3)
        self.inward = jnp.where(self.left, 1, 2)
        self.outward = jnp.where(self.left, 0, 3)
        self.across = jnp.where(self.left, 2, 1)
        self.spare = pl.multiple_of(jnp.where(self.left, self.block, half), self.block)
        self.out_half = pl.multiple_of(jnp.where(self.left, 0, self.block), self.block)
        self.in_half = pl.multiple_of(jnp.where(self.left, self.block, 0), self.block)

    def copies(self, chunk, piece):
        half = 2 * self.block
        cols = slice(piece * self.cols, (piece + 1) * self.cols)
        index = chunk * SUM_PIECES + piece

        def hop(name, src, dst, to):
            sems = self.sems[name]
            return remote(
                src.at[chunk, src_rows, cols], dst, sems.at[0, index], sems.at[1, index], "tensor", to
            )

        src_rows = pl.ds(self.far, half)
        hop_first = hop("first", self.part, self.first.at[chunk, :, cols], self.inward)
        src_rows = pl.ds(self.spare, self.block)
        hop_beside = hop("beside", self.part, self.beside.at[chunk, :, cols], self.inward)
        src_rows = pl.ds(0, half)
        hop_second = hop("second", self.first, self.second.at[chunk, :, cols], self.across)
        src_rows = pl.ds(self.out_half, self.block)
        hop_last = hop("last", self.second, self.last.at[chunk, :, cols], self.outward)
        return hop_first, hop_beside, hop_second, hop_last

    def result_rows(self, chunk, shard):
        start = pl.multiple_of(chunk * self.rows + shard * self.block, self.block)
        return self.result.at[pl.ds(start, self.block)]

    def move(self, way, chunk, hop):
        step = 1 - 2 * way
        shard = jnp.clip(self.rank - step * hop, 0, LINE - 1)
        rows = self.result_rows(chunk, shard)
        name = "up" if way == 0 else "down"
        to = jnp.clip(self.rank + step, 0, LINE - 1)
        index = chunk * (LINE - 1) + hop
        return remote(rows, rows, self.sems[name].at[0, index], self.sems[name].at[1, index], "tensor", to)

    def stage_a(self, chunk):
        @pl.when(self.outer)
        def _():
            for piece in range(SUM_PIECES):
                self.copies(chunk, piece)[0].start()

    def stage_b(self, chunk):
        @pl.when(self.outer)
        def _():
            for piece in range(SUM_PIECES):
                self.copies(chunk, piece)[1].start()

        @pl.when(self.inner)
        def _():
            for piece in range(SUM_PIECES):
                hop_first, _, hop_second, _ = self.copies(chunk, piece)
                cols = slice(piece * self.cols, (piece + 1) * self.cols)
                hop_first.wait_recv()
                self.first[chunk, :, cols] = (
                    self.first[chunk, :, cols].astype(F32)
                    + self.part[chunk, pl.ds(self.far, 2 * self.block), cols].astype(F32)
                ).astype(BF)
                hop_second.start()

    def stage_c(self, chunk):
        @pl.when(self.inner)
        def _():
            out_rows = pl.ds(self.out_half, self.block)
            near_out = pl.ds(pl.multiple_of(self.near + self.out_half, self.block), self.block)
            for piece in range(SUM_PIECES):
                _, _, hop_second, hop_last = self.copies(chunk, piece)
                cols = slice(piece * self.cols, (piece + 1) * self.cols)
                hop_second.wait_recv()
                self.second[chunk, out_rows, cols] = (
                    self.second[chunk, out_rows, cols].astype(F32)
                    + self.part[chunk, near_out, cols].astype(F32)
                ).astype(BF)
                hop_last.start()
            for piece in range(SUM_PIECES):
                self.copies(chunk, piece)[1].wait_recv()
            total = (
                self.second[chunk, pl.ds(self.in_half, self.block)].astype(F32)
                + self.beside[chunk].astype(F32)
                + self.part[chunk, pl.ds(self.own, self.block)].astype(F32)
            )
            self.finish(chunk, total, self.result_rows(chunk, self.rank))
            self.move(0, chunk, 0).start()
            self.move(1, chunk, 0).start()

    def stage_d(self, chunk):
        @pl.when(self.outer)
        def _():
            for piece in range(SUM_PIECES):
                self.copies(chunk, piece)[3].wait_recv()
            total = self.last[chunk].astype(F32) + self.part[
                chunk, pl.ds(self.own, self.block)
            ].astype(F32)
            self.finish(chunk, total, self.result_rows(chunk, self.rank))

        @pl.when(self.rank == 0)
        def _():
            self.move(0, chunk, 0).start()

        @pl.when(self.rank == 3)
        def _():
            self.move(1, chunk, 0).start()

    def stage_e(self, chunk, hop):
        for way in range(2):
            behind = self.rank if way == 0 else LINE - 1 - self.rank

            @pl.when(self.inner & (behind > hop))
            def _():
                self.arrival(way, chunk, hop).wait_recv()
                self.move(way, chunk, hop + 1).start()

    def arrival(self, way, chunk, hop):
        step = 1 - 2 * way
        shard = jnp.clip(self.rank - step * (hop + 1), 0, LINE - 1)
        rows = self.result_rows(chunk, shard)
        name = "up" if way == 0 else "down"
        to = jnp.clip(self.rank + step, 0, LINE - 1)
        index = chunk * (LINE - 1) + hop
        return remote(rows, rows, self.sems[name].at[0, index], self.sems[name].at[1, index], "tensor", to)

    def stage_f(self, chunk):
        @pl.when(self.rank == 0)
        def _():
            for hop in range(LINE - 1):
                self.arrival(1, chunk, hop).wait_recv()

        @pl.when(self.rank == 3)
        def _():
            for hop in range(LINE - 1):
                self.arrival(0, chunk, hop).wait_recv()

    def sent_part(self, chunk):
        @pl.when(self.outer)
        def _():
            for piece in range(SUM_PIECES):
                hop_first, hop_beside, _, _ = self.copies(chunk, piece)
                hop_first.wait_send()
                hop_beside.wait_send()

    def sent_rest(self, chunk):
        @pl.when(self.inner)
        def _():
            for piece in range(SUM_PIECES):
                _, _, hop_second, hop_last = self.copies(chunk, piece)
                hop_second.wait_send()
                hop_last.wait_send()

        for way in range(2):
            behind = self.rank if way == 0 else LINE - 1 - self.rank
            ahead = LINE - 1 - behind
            for hop in range(LINE - 1):

                @pl.when((ahead > 0) & (behind >= hop))
                def _():
                    self.move(way, chunk, hop).wait_send()


def line_sum_scratch(rows, cols):
    block = rows // LINE
    return [
        pltpu.VMEM((LINE, 2 * block, cols), BF),
        pltpu.VMEM((LINE, block, cols), BF),
        pltpu.VMEM((LINE, 2 * block, cols), BF),
        pltpu.VMEM((LINE, block, cols), BF),
    ] + [pltpu.SemaphoreType.DMA((2, LINE * SUM_PIECES))] * 4 + [
        pltpu.SemaphoreType.DMA((2, LINE * (LINE - 1)))
    ] * 2


SUM_NAMES = ("first", "beside", "second", "last", "up", "down")


class LineShare:
    def __init__(self, rank, part, room, sems, pieces):
        self.rank, self.part, self.room, self.pieces = rank, part, room, pieces
        self.sems = sems
        self.cols = part.shape[2] // pieces

    def span(self, piece):
        return pl.ds(pl.multiple_of(piece * self.cols, self.cols), self.cols)

    def slot(self, way, chunk, device):
        return chunk if way == 0 else jnp.where(device == chunk, LINE, chunk)

    def copy(self, way, chunk, piece, own):
        to = jnp.clip(self.rank + 1 - 2 * way, 0, LINE - 1)
        span = self.span(piece)
        here = self.part.at[chunk, :, span] if own else self.room.at[self.slot(way, chunk, self.rank), :, span]
        index = chunk * self.pieces + piece
        return remote(
            here,
            self.room.at[self.slot(way, chunk, to), :, span],
            self.sems[way].at[0, index],
            self.sems[way].at[1, index],
            "tensor",
            to,
        )

    def emit(self, chunk, piece):
        @pl.when((self.rank == 0) & (chunk > 0))
        def _():
            self.copy(0, chunk, piece, True).start()

        @pl.when((self.rank == LINE - 1) & (chunk < LINE - 1))
        def _():
            self.copy(1, chunk, piece, True).start()

    def relay(self, chunk, hop):
        for way in range(2):
            at = hop if way == 0 else LINE - 1 - hop
            further = (chunk > at) if way == 0 else (chunk < at)

            @pl.when((self.rank == at) & further)
            def _():
                def one(piece, _):
                    copy = self.copy(way, chunk, piece, False)
                    copy.wait_recv()
                    span = self.span(piece)
                    slot = self.slot(way, chunk, self.rank)
                    self.room[slot, :, span] = (
                        self.room[slot, :, span].astype(F32) + self.part[chunk, :, span].astype(F32)
                    ).astype(BF)
                    copy.start()
                    return 0

                lax.fori_loop(0, self.pieces, one, 0)

    def arrived(self):
        for way in range(2):
            behind = self.rank > 0 if way == 0 else self.rank < LINE - 1

            @pl.when(behind)
            def _():
                def one(piece, _):
                    self.copy(way, self.rank, piece, False).wait_recv()
                    return 0

                lax.fori_loop(0, self.pieces, one, 0)

    def total(self, span):
        blank = jnp.zeros((span.size, self.part.shape[2]), BF)
        left = jnp.where(self.rank > 0, self.room[self.rank, span, :], blank)
        right = jnp.where(self.rank < LINE - 1, self.room[LINE, span, :], blank)
        return self.part[self.rank, span, :].astype(F32) + left.astype(F32) + right.astype(F32)

    def sent(self, chunk):
        for way in range(2):
            end = 0 if way == 0 else LINE - 1
            for hop in range(LINE - 1):
                at = hop if way == 0 else LINE - 1 - hop
                further = (chunk > at) if way == 0 else (chunk < at)

                @pl.when((self.rank == at) & further)
                def _():
                    def one(piece, _):
                        self.copy(way, chunk, piece, at == end).wait_send()
                        return 0

                    lax.fori_loop(0, self.pieces, one, 0)


def deliver(core, layer, mine, target, sems, act):
    @pl.when(core == layer)
    def _():
        copy = pltpu.make_async_copy(mine, target.at[core], sems.at[layer])
        copy.start() if act == "start" else copy.wait()

    @pl.when(core != layer)
    def _():
        copy = remote(mine, target.at[core], sems.at[layer], sems.at[2], "pipe", 1 - core)
        copy.start() if act == "start" else copy.wait_send()


def delivered(core, target, sems):
    ref = target.at[1 - core]
    remote(ref, ref, sems.at[0], sems.at[2], "pipe", 1 - core).wait_recv()


def forward_kernel(*refs):
    at = 0

    def take(count):
        nonlocal at
        at += count
        return refs[at - count : at]

    (inputs_ref,) = take(1)
    own_w = take(4)
    given = take(6)
    cos_ref, near_ref, far_ref = take(3)
    other_w = take(4)
    h_out, h_far, q_out, k_out, v_out, o_out, o_near, o_far = take(8)
    act_near, act_far, slope_out, logs_out, x1_out, part_out = take(6)
    (small_out,) = take(1)
    vmem_w = take(4)
    x_buf, x_share, h_buf, act_buf, slope_buf, q_buf, o_buf, k_all, v_all, logs_buf = take(10)
    part, x1 = take(2)
    sum_bufs = take(4)
    sum_sems = dict(zip(SUM_NAMES, take(6)))
    w_sems, fetch_sems, x_sems, out_sems, slot4_sems, far_send, far_recv, once_sems = take(8)
    small, small_sems = take(2)
    assert at == len(refs)
    core = lax.axis_index("pipe")
    rank = lax.axis_index("tensor")
    theirs = 1 - core
    rows = x_buf.shape[1]
    width = x_buf.shape[2]
    local = q_buf.shape[2]
    hidden = act_buf.shape[2]
    half_hidden = hidden // 2
    half_local = local // 2
    tile = min(TILE, width)
    scale = HEAD_DIM ** (-0.5)

    weight_moves = [
        remote(own, other, w_sems.at[0, i], w_sems.at[1, i], "pipe", 1 - core)
        for i, (own, other) in enumerate(zip(own_w, other_w))
    ]

    def fetch(layer, i):
        fetch_weight(
            layer, core, own_w[i], other_w[i], vmem_w[i], fetch_sems.at[i], weight_moves[i]
        )

    def fetched(i):
        pltpu.make_async_copy(own_w[i], vmem_w[i], fetch_sems.at[i]).wait()

    def chunk_rows(chunk):
        return pl.ds(pl.multiple_of(chunk * rows, rows), rows)

    def x_copy(chunk):
        slot = lax.rem(chunk, 2)
        return pltpu.make_async_copy(
            inputs_ref.at[core, chunk_rows(chunk)], x_buf.at[slot], x_sems.at[slot]
        )

    def finish(chunk, total, target):
        value = total + x_share[chunk].astype(F32) + small[0, 3:4, 0:width]
        target[...] = value.astype(BF)

    summed = LineSum(rank, part, *sum_bufs, x1, sum_sems, finish)

    def half(which, size):
        return pl.ds(pl.multiple_of(which * size, size), size)

    def placed(step):
        layer, chunk = lax.div(step, LINE), lax.rem(step, LINE)
        return layer, chunk_rows(chunk), lax.rem(step, 2), chunk

    def local_copy(name, src, dst, slot):
        return pltpu.make_async_copy(src, dst, out_sems.at[name, slot])

    def far_copy(name, src, dst, slot):
        return remote(src, dst, far_send.at[name, slot], far_recv.at[name], "pipe", theirs)

    def h_copies(step):
        layer, at_rows, _, slot = placed(step)
        return [
            local_copy(0, h_buf.at[slot], h_out.at[layer, at_rows], slot),
            far_copy(0, h_buf.at[slot], h_far.at[layer, at_rows], slot),
        ]

    def q_copies(step):
        layer, at_rows, slot, _ = placed(step)
        return [local_copy(1, q_buf.at[slot], q_out.at[layer, at_rows], slot)]

    def logs_copies(step):
        layer, at_rows, slot, _ = placed(step)
        return [local_copy(2, logs_buf.at[slot], logs_out.at[layer, :, :, at_rows], slot)]

    def o_copies(step):
        layer, at_rows, _, slot = placed(step)
        return [
            local_copy(3, o_buf.at[slot], o_out.at[layer, at_rows], slot),
            far_copy(1, o_buf.at[slot, :, half(theirs, half_local)], o_far.at[layer, at_rows], slot),
            local_copy(4, o_buf.at[slot, :, half(core, half_local)], o_near.at[layer, at_rows], slot),
        ]

    def act_copies(step):
        layer, at_rows, slot, _ = placed(step)
        return [
            local_copy(5, act_buf.at[slot, :, half(core, half_hidden)], act_near.at[layer, at_rows], slot),
            far_copy(2, act_buf.at[slot, :, half(theirs, half_hidden)], act_far.at[layer, at_rows], slot),
            local_copy(6, slope_buf.at[slot], slope_out.at[layer, at_rows], slot),
        ]

    def start_all(copies):
        for item in copies:
            item.start()

    def left_all(copies):
        for i, item in enumerate(copies):
            if i == 1:
                item.wait_send()
            else:
                item.wait()

    def kv_copies(step):
        layer, chunk = lax.div(step, LINE), lax.rem(step, LINE)
        at_rows = chunk_rows(chunk)
        return [
            pltpu.make_async_copy(k_all.at[at_rows], k_out.at[layer, at_rows], slot4_sems.at[0, chunk]),
            pltpu.make_async_copy(v_all.at[at_rows], v_out.at[layer, at_rows], slot4_sems.at[1, chunk]),
        ]

    def x1_copy(chunk):
        at_rows = chunk_rows(chunk)
        return pltpu.make_async_copy(x1.at[at_rows], x1_out.at[at_rows], once_sems.at[0, chunk])

    def part_copy(chunk):
        at_rows = chunk_rows(chunk)
        return pltpu.make_async_copy(part.at[chunk], part_out.at[at_rows], once_sems.at[1, chunk])

    gain_in, shift_in, bias3_in, bias_d_in, bias_u_in, bias_2_in = given
    x_copy(0).start()
    small[core, 0:1, 0:width] = gain_in[...].astype(F32)
    small[core, 1:2, 0:width] = shift_in[...].astype(F32)
    small[core, 2:3, 0:hidden] = bias_u_in[...].astype(F32)
    small[core, 3:4, 0:width] = bias_d_in[...].astype(F32) + bias_2_in[...].astype(F32)
    for c in range(3):
        small[core, 4 + c : 5 + c, 0:local] = bias3_in[0, c : c + 1, :].astype(F32)
    greet(core, rank)
    small_move = remote(
        small.at[core], small.at[core], small_sems.at[0], small_sems.at[1], "pipe", 1 - core
    )
    small_move.start()
    for move in weight_moves:
        move.start()
    x_copy(1).start()

    keep = lax.broadcasted_iota(jnp.int32, (rows, rows), 1) <= lax.broadcasted_iota(
        jnp.int32, (rows, rows), 0
    )

    def attention(chunk, slot):
        def pair(j, _):
            lanes = pl.ds(pl.multiple_of(j * LANES, LANES), LANES)
            query = q_buf[slot, :, lanes]
            outs = []
            for which in range(LANES // HEAD_DIM):
                mask = head_mask(rows, which)
                mine = jnp.where(mask, query, jnp.zeros_like(query))
                scores = []
                if chunk:
                    scores.append(dot_nt(mine, k_all[0 : chunk * rows, lanes]))
                scores.append(
                    jnp.where(keep, dot_nt(mine, k_all[chunk * rows : (chunk + 1) * rows, lanes]), masked_score)
                )
                top = functools.reduce(
                    jnp.maximum, [jnp.max(item, axis=1, keepdims=True) for item in scores]
                )
                weights = [jnp.exp(item - top) for item in scores]
                total = functools.reduce(
                    jnp.add, [jnp.sum(item, axis=1, keepdims=True) for item in weights]
                )
                values = []
                if chunk:
                    values.append(v_all[0 : chunk * rows, lanes])
                values.append(v_all[chunk * rows : (chunk + 1) * rows, lanes])
                merged = functools.reduce(
                    jnp.add, [dot_nn(w.astype(BF), v) for w, v in zip(weights, values)]
                )
                outs.append(merged / total)
                logs_buf[slot, j, which : which + 1, :] = as_row(top + jnp.log(total))
            o_buf[chunk, :, lanes] = jnp.where(head_mask(rows, 0), outs[0], outs[1]).astype(BF)
            return 0

        lax.fori_loop(0, local // LANES, pair, 0)

    def go_on(step):
        @pl.when((step >= 1) & (step <= LINE))
        def _():
            summed.stage_b(step - 1)

        @pl.when((step >= 2) & (step <= LINE + 1))
        def _():
            summed.stage_d(step - 2)

        @pl.when((step >= 3) & (step <= LINE + 2))
        def _():
            summed.stage_e(step - 3, 1)

    def attention_part(step, _):
        layer, chunk = lax.div(step, LINE), lax.rem(step, LINE)
        slot = lax.rem(step, 2)
        at_rows = chunk_rows(chunk)

        @pl.when(step >= 2)
        def _():
            left_all(q_copies(step - 2))
            left_all(logs_copies(step - 2))

        @pl.when(step >= LINE)
        def _():
            left_all(h_copies(step - LINE))
            left_all(o_copies(step - LINE))

        some_rows = rows // 8
        gain, shift = small[layer, 0:1, 0:width], small[layer, 1:2, 0:width]

        def normalise(load):
            def some(i, _):
                span = pl.ds(pl.multiple_of(i * some_rows, some_rows), some_rows)
                values = load(span).astype(F32)
                centre = values - jnp.mean(values, axis=-1, keepdims=True)
                spread = jnp.mean(centre * centre, axis=-1, keepdims=True)
                h_buf[chunk, span, :] = (centre * lax.rsqrt(spread + ln_eps) * gain + shift).astype(BF)
                return 0

            lax.fori_loop(0, 8, some, 0)

        @pl.when(layer == 0)
        def _():
            x_copy(chunk).wait()
            x_share[chunk] = x_buf[slot, pl.ds(pl.multiple_of(rank * (rows // LINE), rows // LINE), rows // LINE)]
            normalise(lambda span: x_buf[slot, span, :])

            @pl.when(step + 2 < LINE)
            def _():
                x_copy(chunk + 2).start()

        @pl.when(step == 0)
        def _():
            fetch(0, 0)

        @pl.when(layer == 1)
        def _():
            summed.stage_f(chunk)
            x1_copy(chunk).start()
            base = chunk * rows
            normalise(lambda span: x1[pl.ds(pl.multiple_of(base + span.start, some_rows), some_rows), :])

        start_all(h_copies(step))

        @pl.when(chunk == 0)
        def _():
            fetched(0)

        @pl.when(layer == 1)
        def _():
            for item in kv_copies(step - LINE):
                item.wait()

        tables = (cos_ref[at_rows, :], near_ref[at_rows, :], far_ref[at_rows, :])
        h = h_buf[chunk]
        for part3 in range(3):
            value = dot_nn(h, vmem_w[0][part3]) + small[layer, 4 + part3 : 5 + part3, 0:local]
            for j in range(local // LANES):
                lanes = slice(j * LANES, (j + 1) * LANES)
                if part3 == 0:
                    q_buf[slot, :, lanes] = (turn(value[:, lanes], *tables) * scale).astype(BF)
                elif part3 == 1:
                    k_all[at_rows, lanes] = turn(value[:, lanes], *tables).astype(BF)
                else:
                    v_all[at_rows, lanes] = value[:, lanes].astype(BF)
        start_all(q_copies(step))
        start_all(kv_copies(step))

        @pl.when(step == LINE - 1)
        def _():
            fetch(1, 0)

        @pl.when(layer == 1)
        def _():
            go_on(step)

        for index in range(LINE):

            @pl.when(chunk == index)
            def _():
                attention(index, slot)

        start_all(o_copies(step))
        start_all(logs_copies(step))

        @pl.when(step == jnp.where(core == 0, 0, LINE - 2))
        def _():
            fetch(0, 1)

        @pl.when(step == jnp.where(core == 0, 0, LINE - 1))
        def _():
            fetch(0, 2)

        return 0

    def hidden_part(step, _):
        layer, chunk = lax.div(step, LINE), lax.rem(step, LINE)
        slot = lax.rem(step, 2)

        @pl.when(step >= 2)
        def _():
            left_all(act_copies(step - 2))

        @pl.when(chunk == 0)
        def _():
            fetched(1)

        def up(i, _):
            cols = pl.ds(pl.multiple_of(i * tile, tile), tile)
            u = dot_nn(h_buf[chunk], vmem_w[1][:, cols]) + small[layer, 2:3, cols]
            square = u * u
            inner = jnp.tanh(u * (gelu_coef + (gelu_coef * 0.044715) * square))
            plus = 0.5 + 0.5 * inner
            act = u * plus
            act_buf[slot, :, cols] = act.astype(BF)
            slope_buf[slot, :, cols] = (
                plus + act * (1.0 - inner) * (gelu_coef + (3.0 * 0.044715 * gelu_coef) * square)
            ).astype(BF)
            return 0

        lax.fori_loop(0, hidden // tile, up, 0, unroll=True)
        start_all(act_copies(step))

        @pl.when(step == 0)
        def _():
            fetch(0, 3)

        @pl.when(step == LINE - 1)
        def _():
            fetch(1, 1)

        @pl.when(layer == 0)
        def _():
            go_on(step)

        @pl.when(chunk == 0)
        def _():
            fetched(2)
            fetched(3)

        @pl.when(layer == 1)
        def _():
            summed.sent_part(chunk)

        def down(i, _):
            cols = pl.ds(pl.multiple_of(i * tile, tile), tile)
            part[chunk, :, cols] = (
                dot_nn(o_buf[chunk], vmem_w[2][:, cols]) + dot_nn(act_buf[slot], vmem_w[3][:, cols])
            ).astype(BF)
            return 0

        lax.fori_loop(0, width // tile, down, 0, unroll=True)

        @pl.when(step == LINE - 1)
        def _():
            fetch(1, 2)
            fetch(1, 3)

        @pl.when(layer == 0)
        def _():
            summed.stage_a(chunk)

        @pl.when(layer == 1)
        def _():
            part_copy(chunk).start()

        @pl.when((step >= 1) & (step <= LINE))
        def _():
            summed.stage_c(step - 1)

        @pl.when((step >= 2) & (step <= LINE + 1))
        def _():
            summed.stage_e(step - 2, 0)

        return 0

    def whole_step(step, _):
        attention_part(step, 0)
        hidden_part(step, 0)
        return 0

    def first_layer(turn_, _):
        kind = jnp.where(core == 0, lax.rem(turn_, 2), lax.div(turn_, LINE))
        step = jnp.where(core == 0, lax.div(turn_, 2), lax.rem(turn_, LINE))

        @pl.when(kind == 0)
        def _():
            attention_part(step, 0)

        @pl.when(kind == 1)
        def _():
            hidden_part(step, 0)

        return 0

    remote(
        small.at[1 - core], small.at[1 - core], small_sems.at[0], small_sems.at[1], "pipe", 1 - core
    ).wait_recv()
    small_out[...] = small[...]
    lax.fori_loop(0, 2 * LINE, first_layer, 0)
    lax.fori_loop(LINE, STEPS, whole_step, 0)

    for step in range(STEPS - 2, STEPS):
        left_all(q_copies(step))
        left_all(logs_copies(step))
        left_all(act_copies(step))
    for step in range(LINE, STEPS):
        left_all(h_copies(step))
        left_all(o_copies(step))
        for item in kv_copies(step):
            item.wait()
    for chunk in range(LINE):
        x1_copy(chunk).wait()
        part_copy(chunk).wait()
        summed.sent_rest(chunk)
    for move in weight_moves:
        move.wait_send()
    small_move.wait_send()
    for i, ref in enumerate((h_far, o_far, act_far)):
        remote(ref, ref, far_send.at[i, 0], far_recv.at[i], "pipe", theirs).wait_recv()


def forward_both(inputs, weights, vectors, tables):
    _, length, width = inputs.shape
    w_qkv, w_fc1, w_dense, w_fc2 = weights
    local, hidden = w_dense.shape[0], w_fc1.shape[1]
    rows = length // LINE
    pairs = local // LANES

    def bf(*shape):
        return jax.ShapeDtypeStruct(shape, BF)

    out_shape = [bf(*w.shape) for w in weights] + [
        bf(2, length, width),
        bf(2, length, width),
        bf(2, length, local),
        bf(2, length, local),
        bf(2, length, local),
        bf(2, length, local),
        bf(2, length, local // 2),
        bf(2, length, local // 2),
        bf(2, length, hidden // 2),
        bf(2, length, hidden // 2),
        bf(2, length, hidden),
        jax.ShapeDtypeStruct((2, pairs, 8, length), F32),
        bf(length, width),
        bf(length, width),
        jax.ShapeDtypeStruct((2, 8, max(width, hidden)), F32),
    ]
    whole = pl.BlockSpec(memory_space=pltpu.VMEM)
    away = pl.BlockSpec(memory_space=pl.ANY)
    dma = pltpu.SemaphoreType.DMA
    return pl.pallas_call(
        forward_kernel,
        name="forward_both",
        in_specs=[away] * 5 + [whole] * 9,
        out_specs=[away] * (len(out_shape) - 1) + [whole],
        out_shape=out_shape,
        scratch_shapes=[pltpu.VMEM(w.shape, BF) for w in weights]
        + [
            pltpu.VMEM((2, rows, width), BF),
            pltpu.VMEM((LINE, rows // LINE, width), BF),
            pltpu.VMEM((LINE, rows, width), BF),
            pltpu.VMEM((2, rows, hidden), BF),
            pltpu.VMEM((2, rows, hidden), BF),
            pltpu.VMEM((2, rows, local), BF),
            pltpu.VMEM((LINE, rows, local), BF),
            pltpu.VMEM((length, local), BF),
            pltpu.VMEM((length, local), BF),
            pltpu.VMEM((2, pairs, 8, rows), F32),
            pltpu.VMEM((LINE, rows, width), BF),
            pltpu.VMEM((length, width), BF),
        ]
        + line_sum_scratch(rows, width)
        + [
            dma((2, 4)),
            dma((4,)),
            dma((2,)),
            dma((7, LINE)),
            dma((2, LINE)),
            dma((3, LINE)),
            dma((3,)),
            dma((2, LINE)),
            pltpu.VMEM((2, 8, max(width, hidden)), F32),
            dma((2,)),
        ],
        compiler_params=pltpu.CompilerParams(
            collective_id=0, has_side_effects=True, vmem_limit_bytes=63 * MIB
        ),
        cost_estimate=pl.CostEstimate(
            flops=4 * length * width * (4 * local + 2 * hidden),
            bytes_accessed=200 * MIB,
            transcendentals=0,
        ),
    )(inputs, *weights, *vectors, *tables)


class PairDots:
    def __init__(self, core, dp_rank, dp_size, left_buf, right_buf, out_buf, sems, stages, received):
        self.core, self.me, self.dp = core, dp_rank, dp_size
        self.left_buf, self.right_buf, self.out_buf = left_buf, right_buf, out_buf
        self.left_sems, self.right_sems, self.out_sems, self.send_sems, self.recv_sems = sems
        self.stages, self.received = stages, received
        self.tokens = left_buf.shape[1] // 2
        self.keep = left_buf.shape[2]
        self.groups = {}

    def add(self, index, layer, kind, left, rights):
        total = sum(near.shape[-1] for near, _ in rights)
        widths = []
        while sum(widths) < total:
            widths.append(min(TILE, total - sum(widths)))
        self.groups[index] = (layer, kind, left, rights, widths)

    def tile(self, order):
        return lax.rem(self.me + 1 + order, self.dp)

    def left_copies(self, index, order):
        near, far = self.groups[index][2]
        slot = lax.rem(order, 2)
        cols = pl.ds(pl.multiple_of(self.tile(order) * self.keep, self.keep), self.keep)
        return [
            pltpu.make_async_copy(
                src.at[:, cols],
                self.left_buf.at[slot, i * self.tokens : (i + 1) * self.tokens],
                self.left_sems.at[i, slot],
            )
            for i, src in enumerate((near, far))
        ]

    def right_copies(self, index):
        copies = []
        base = 0
        for pair in self.groups[index][3]:
            width = pair[0].shape[-1]
            for i, src in enumerate(pair):
                target = self.right_buf.at[i * self.tokens : (i + 1) * self.tokens, base : base + width]
                copies.append(pltpu.make_async_copy(src, target, self.right_sems.at[len(copies)]))
            base += width
        return copies

    def prime(self, index):
        for item in self.left_copies(index, jnp.int32(0)) + self.right_copies(index):
            item.start()

    def out_copy(self, index, order, piece):
        layer, kind, _, _, widths = self.groups[index]
        base, width, slot = sum(widths[:piece]), widths[piece], piece % 2
        stage = self.stages[kind].at[layer, self.tile(order)]
        if kind:
            return pltpu.make_async_copy(
                self.out_buf.at[slot, 0 : self.keep, 0:width],
                stage.at[:, base : base + width],
                self.out_sems.at[slot],
            )
        return pltpu.make_async_copy(
            self.out_buf.at[slot, 0:width, 0 : self.keep],
            stage.at[base : base + width],
            self.out_sems.at[slot],
        )

    def send(self, index, order, act):
        layer, kind = self.groups[index][:2]
        tile = self.tile(order)
        src = self.stages[kind].at[layer, tile]
        dst = self.received[kind].at[self.core, self.me]
        at_home = (self.core == layer) & (tile == self.me)

        @pl.when(at_home)
        def _():
            copy = pltpu.make_async_copy(src, dst, self.send_sems.at[index, order])
            copy.start() if act == "start" else copy.wait()

        @pl.when(jnp.logical_not(at_home))
        def _():
            copy = pltpu.make_async_remote_copy(
                src_ref=src,
                dst_ref=dst,
                send_sem=self.send_sems.at[index, order],
                recv_sem=self.recv_sems.at[kind, self.core],
                device_id={"pipe": jnp.int32(layer), "dp": tile},
                device_id_type=pl.DeviceIdType.MESH,
            )
            copy.start() if act == "start" else copy.wait_send()

    def run(self, index, start, stop):
        _, kind, _, _, widths = self.groups[index]

        def one(order, _):
            slot = lax.rem(order, 2)
            for item in self.left_copies(index, order):
                item.wait()

            @pl.when(order == 0)
            def _():
                for item in self.right_copies(index):
                    item.wait()

            @pl.when(order + 1 < self.dp)
            def _():
                for item in self.left_copies(index, order + 1):
                    item.start()

            base = 0
            for piece, width in enumerate(widths):
                if piece >= 2:
                    self.out_copy(index, order, piece - 2).wait()
                left, right = self.left_buf[slot], self.right_buf[:, base : base + width]
                if kind:
                    self.out_buf[piece % 2, 0 : self.keep, 0:width] = dot_tn(left, right).astype(BF)
                else:
                    self.out_buf[piece % 2, 0:width, 0 : self.keep] = dot_tn(right, left).astype(BF)
                self.out_copy(index, order, piece).start()
                base += width
            for piece in range(max(0, len(widths) - 2), len(widths)):
                self.out_copy(index, order, piece).wait()
            self.send(index, order, "start")
            return 0

        lax.fori_loop(start, stop, one, 0)

    def all_sent(self, index):
        def one(order, _):
            self.send(index, order, "wait")
            return 0

        lax.fori_loop(0, self.dp, one, 0)

    def all_received(self, kind):
        ref = self.received[kind]
        theirs = ref.at[1 - self.core]
        ours = ref.at[self.core, pl.ds(0, self.dp - 1)]
        remote(theirs, theirs, self.send_sems.at[0, 0], self.recv_sems.at[kind, 1 - self.core], "pipe", 1 - self.core).wait_recv()
        if self.dp > 1:
            remote(ours, ours, self.send_sems.at[0, 0], self.recv_sems.at[kind, self.core], "pipe", 1 - self.core).wait_recv()


class SmallSums:
    def __init__(self, core, rank, dp_rank, dp_size, sums, from_peers, from_line, final, sems):
        self.core, self.rank, self.me, self.dp = core, rank, dp_rank, dp_size
        self.sums, self.from_peers, self.from_line, self.final = sums, from_peers, from_line, final
        self.peer_send, self.peer_recv, self.line_send, self.line_recv = sems

    def to_peer(self, layer, other, act):
        src = self.sums.at[layer]
        dst = self.from_peers.at[self.core, self.me]
        sem = self.peer_send.at[layer, other]
        at_home = (self.core == layer) & (other == self.me)

        @pl.when(at_home)
        def _():
            copy = pltpu.make_async_copy(src, dst, sem)
            copy.start() if act == "start" else copy.wait()

        @pl.when(jnp.logical_not(at_home))
        def _():
            copy = pltpu.make_async_remote_copy(
                src_ref=src,
                dst_ref=dst,
                send_sem=sem,
                recv_sem=self.peer_recv.at[self.core],
                device_id={"pipe": jnp.int32(layer), "dp": other},
                device_id_type=pl.DeviceIdType.MESH,
            )
            copy.start() if act == "start" else copy.wait_send()

    def peers(self, act):
        for layer in range(2):

            def one(other, _):
                self.to_peer(layer, other, act)
                return 0

            lax.fori_loop(0, self.dp, one, 0)

    def line_copy(self, other):
        return remote(
            self.from_line.at[LINE],
            self.from_line.at[self.rank],
            self.line_send.at[other],
            self.line_recv.at[self.rank],
            "tensor",
            other,
        )

    def pass_on(self):
        self.peers("wait")
        theirs = self.from_peers.at[1 - self.core]
        remote(theirs, theirs, self.peer_send.at[0, 0], self.peer_recv.at[1 - self.core], "pipe", 1 - self.core).wait_recv()
        if self.dp > 1:
            ours = self.from_peers.at[self.core, pl.ds(0, self.dp - 1)]
            remote(ours, ours, self.peer_send.at[0, 0], self.peer_recv.at[self.core], "pipe", 1 - self.core).wait_recv()
        total = self.from_peers[0, 0] + self.from_peers[1, 0]
        for i in range(1, self.dp):
            total = total + (self.from_peers[0, i] + self.from_peers[1, i])
        self.from_line[LINE] = total
        for other in range(LINE):

            @pl.when(self.rank != other)
            def _():
                self.line_copy(other).start()

    def finish(self):
        own = self.from_line[LINE]
        self.final[2:8, :] = own[2:8, :]
        self.final[0:2, :] = own[0:2, :]
        for other in range(LINE):

            @pl.when(self.rank != other)
            def _():
                self.line_copy(other).wait_send()
                block = self.from_line.at[other]
                remote(
                    block, block, self.line_send.at[other], self.line_recv.at[other], "tensor", other
                ).wait_recv()
                self.final[0:2, :] += self.from_line[other, 0:2, :]


RING = 3


def backward_kernel(dp_size, *refs):
    at = 0

    def take(count):
        nonlocal at
        at += count
        return refs[at - count : at]

    cot_ref, in_ref, x1_ref, part1_ref = take(4)
    slope_ref, q_ref, k_ref, v_ref, o_ref, logs_ref = take(6)
    own_w = take(4)
    other_w = take(4)
    h_near, h_far, act_near, act_far, o_near, o_far = take(6)
    vectors, cos_ref, near_ref, far_ref = take(4)
    acts_out, grads_out, dy0_out, dy0_far, du_near, du_far, dp_near, dp_far = take(8)
    stages = take(2)
    received = take(2)
    (final_ref,) = take(1)
    ring, ring_qkv, dense_w = take(3)
    up_buf, x_buf, slope_buf, q_buf, o_buf, logs_buf = take(6)
    k_all, v_all, dk_all, dv_all = take(4)
    do_buf, dp_buf, du_buf, part = take(4)
    mean_buf, inverse_buf, up_share, x_share = take(4)
    (result,) = take(1)
    sum_bufs = take(4)
    sum_sems = dict(zip(SUM_NAMES, take(6)))
    share_room, left_sems, right_sems, left1_sems, right1_sems, free_sem, early_sems = take(7)
    dot_bufs = take(3)
    dot_sems = take(5)
    ring_sems, qkv_sems, dense_sem, load_sems, kv_sems, out_sems = take(6)
    far_send, far_recv, once_sems, result_send, grads_sems, acts_sems = take(6)
    sums_ref, from_peers, from_line = take(3)
    small_sems = take(4)
    assert at == len(refs)
    w_qkv, w_fc1, w_dense, w_fc2 = range(4)
    core = lax.axis_index("pipe")
    rank = lax.axis_index("tensor")
    dp_rank = lax.axis_index("dp")
    theirs = 1 - core
    rows, width = up_buf.shape
    block = rows // LINE
    local = q_buf.shape[2]
    hidden = du_buf.shape[1]
    half_hidden, half_local = hidden // 2, local // 2
    tile = ring.shape[1]
    up_tiles, out_tiles = hidden // tile, width // tile
    ring_tiles = up_tiles + out_tiles
    scale = HEAD_DIM ** (-0.5)

    def layer_of(step):
        return 1 - lax.div(step, LINE)

    def chunk_of(step):
        return LINE - 1 - lax.rem(step, LINE)

    def chunk_rows(chunk):
        return pl.ds(pl.multiple_of(chunk * rows, rows), rows)

    def weight_copy(layer, views, target, sem, act):
        if act == "wait":
            pltpu.make_async_copy(views[0], target, sem).wait()
            return

        @pl.when(core == layer)
        def _():
            pltpu.make_async_copy(views[0], target, sem).start()

        @pl.when(core != layer)
        def _():
            pltpu.make_async_copy(views[1], target, sem).start()

    def ring_copy(index, act):
        step, place = lax.div(index, ring_tiles), lax.rem(index, ring_tiles)
        slot = lax.rem(index, RING)
        target, sem = ring.at[slot], ring_sems.at[slot]
        layer = layer_of(step)
        if act == "wait":
            weight_copy(layer, [own_w[w_fc2].at[0:tile]], target, sem, act)
            return

        @pl.when(place < up_tiles)
        def _():
            span = pl.ds(pl.multiple_of(place * tile, tile), tile)
            weight_copy(layer, [own_w[w_fc2].at[span], other_w[w_fc2].at[span]], target, sem, act)

        @pl.when(place >= up_tiles)
        def _():
            span = pl.ds(pl.multiple_of((place - up_tiles) * tile, tile), tile)
            weight_copy(layer, [own_w[w_fc1].at[span], other_w[w_fc1].at[span]], target, sem, act)

    def qkv_copy(index, act):
        step, place = lax.div(index, out_tiles), lax.rem(index, out_tiles)
        slot = lax.rem(index, 2)
        span = pl.ds(pl.multiple_of(place * tile, tile), tile)
        views = [w[w_qkv].at[:, span, :] for w in (own_w, other_w)]
        weight_copy(layer_of(step), views, ring_qkv.at[slot], qkv_sems.at[slot], act)

    def dense_copy(layer, act):
        weight_copy(layer, [own_w[w_dense], other_w[w_dense]], dense_w, dense_sem.at[0], act)

    def kv_copies(layer):
        return [
            pltpu.make_async_copy(k_ref.at[layer], k_all, kv_sems.at[0]),
            pltpu.make_async_copy(v_ref.at[layer], v_all, kv_sems.at[1]),
        ]

    def early_loads(step):
        layer, slot = layer_of(step), 0
        at_rows = chunk_rows(chunk_of(step))
        return [
            pltpu.make_async_copy(q_ref.at[layer, at_rows], q_buf.at[slot], load_sems.at[0, slot]),
            pltpu.make_async_copy(o_ref.at[layer, at_rows], o_buf.at[slot], load_sems.at[1, slot]),
            pltpu.make_async_copy(
                logs_ref.at[layer, :, :, at_rows], logs_buf.at[slot], load_sems.at[2, slot]
            ),
        ]

    def slope_load(step):
        return pltpu.make_async_copy(
            slope_ref.at[layer_of(step), chunk_rows(chunk_of(step))], slope_buf, load_sems.at[3, 0]
        )

    def x_load(src):
        return pltpu.make_async_copy(src, x_buf, load_sems.at[4, 0])

    def up_load(src):
        return pltpu.make_async_copy(src, up_buf, load_sems.at[5, 0])

    def norm_back(layer, rows_x, rows_up, total):
        values = rows_x.astype(F32)
        centre = values - jnp.mean(values, axis=-1, keepdims=True)
        inverse = lax.rsqrt(jnp.mean(centre * centre, axis=-1, keepdims=True) + ln_eps)
        xhat = centre * inverse
        e = total * vectors[layer, 0:1, 0:width]
        back = e - jnp.mean(e, axis=-1, keepdims=True) - xhat * jnp.mean(
            e * xhat, axis=-1, keepdims=True
        )
        return (rows_up.astype(F32) + inverse * back).astype(BF)

    def finish(chunk, total, target):
        target[...] = norm_back(1, x_share[chunk], up_share[chunk], total)

    summed = LineSum(rank, part, *sum_bufs, result, sum_sems, finish)
    shared = LineShare(rank, part, share_room, (left_sems, right_sems), out_tiles)
    dots = PairDots(core, dp_rank, dp_size, *dot_bufs, dot_sems, stages, received)
    shared1 = LineShare(rank, part, share_room, (left1_sems, right1_sems), out_tiles)

    mine = chunk_rows(rank)
    early_loads_ = [
        pltpu.make_async_copy(part1_ref.at[(LINE - 1) * rows : LINE * rows], part.at[0], once_sems.at[0]),
        pltpu.make_async_copy(part1_ref.at[0:rows], part.at[1], once_sems.at[1]),
        pltpu.make_async_copy(x1_ref.at[mine], part.at[2], once_sems.at[2]),
    ]

    def early_copy(way, piece, first):
        slot = LINE - 1 if way == 0 else 0
        span = pl.ds(pl.multiple_of(piece * tile, tile), tile)
        src = part.at[way, :, span] if first else share_room.at[slot, :, span]
        to = jnp.clip(rank + 1 - 2 * way, 0, LINE - 1)
        return remote(
            src,
            share_room.at[slot, :, span],
            early_sems.at[way, 0, piece],
            early_sems.at[way, 1, piece],
            "tensor",
            to,
        )

    def early_emit():
        for item in early_loads_:
            item.wait()
        for way, (end, goal) in enumerate(((0, LINE - 1), (LINE - 1, 0))):

            @pl.when(rank == end)
            def _():
                for piece in range(out_tiles):
                    early_copy(way, piece, True).start()

            @pl.when(rank == goal)
            def _():
                small = rows // 8

                def one(i, _):
                    span = pl.ds(pl.multiple_of(i * small, small), small)
                    value = part[way, span, :].astype(F32) + part[2, span, :].astype(F32)
                    share_room[LINE, span, :] = (value + vectors[1, 3:4, 0:width]).astype(BF)
                    return 0

                lax.fori_loop(0, 8, one, 0)

    def early_relay(way, device):
        @pl.when(rank == device)
        def _():
            slot = LINE - 1 if way == 0 else 0

            def one(piece, _):
                copy = early_copy(way, piece, False)
                copy.wait_recv()
                span = pl.ds(pl.multiple_of(piece * tile, tile), tile)
                share_room[slot, :, span] = (
                    share_room[slot, :, span].astype(F32) + part[way, :, span].astype(F32)
                ).astype(BF)
                copy.start()
                return 0

            lax.fori_loop(0, out_tiles, one, 0)

    def early_sent(way, devices):
        for device in devices:

            @pl.when(rank == device)
            def _():
                for piece in range(out_tiles):
                    early_copy(way, piece, device == (0 if way == 0 else LINE - 1)).wait_send()

    def early_deliver(act):
        for way, goal in enumerate((LINE - 1, 0)):

            @pl.when(rank == goal)
            def _():
                deliver(core, 1, share_room.at[goal], acts_out, acts_sems, act)

    def early_finish():
        for way, goal in enumerate((LINE - 1, 0)):

            @pl.when(rank == goal)
            def _():
                for piece in range(out_tiles):
                    early_copy(way, piece, False).wait_recv()
                small = rows // 8

                def one(i, _):
                    span = pl.ds(pl.multiple_of(i * small, small), small)
                    value = share_room[LINE, span, :].astype(F32) + share_room[goal, span, :].astype(F32)
                    share_room[goal, span, :] = value.astype(BF)
                    return 0

                lax.fori_loop(0, 8, one, 0)

        early_deliver("start")

    smalls = SmallSums(
        core, rank, dp_rank, dp_size, sums_ref, from_peers, from_line, final_ref, small_sems
    )
    dots.add(0, 1, 0, (cot_ref.at[core], cot_ref.at[theirs]), [(act_near.at[1], act_far.at[1]), (o_near.at[1], o_far.at[1])])
    dots.add(2, 0, 0, (dy0_out, dy0_far), [(act_near.at[0], act_far.at[0]), (o_near.at[0], o_far.at[0])])
    for index, layer in ((1, 1), (3, 0)):
        dots.add(
            index,
            layer,
            1,
            (h_near.at[layer], h_far.at[layer]),
            [(du_near.at[layer], du_far.at[layer])]
            + [(dp_near.at[layer, c], dp_far.at[layer, c]) for c in range(3)],
        )

    def half(which, size):
        return pl.ds(pl.multiple_of(which * size, size), size)

    def dp_copies(step):
        layer, at_rows = layer_of(step), chunk_rows(chunk_of(step))
        return [
            pltpu.make_async_copy(
                dp_buf.at[:, :, half(core, half_local)], dp_near.at[layer, :, at_rows], out_sems.at[0]
            ),
            remote(
                dp_buf.at[:, :, half(theirs, half_local)],
                dp_far.at[layer, :, at_rows],
                far_send.at[0],
                far_recv.at[0, layer],
                "pipe",
                theirs,
            ),
        ]

    def du_copies(step):
        layer, at_rows = layer_of(step), chunk_rows(chunk_of(step))
        return [
            pltpu.make_async_copy(
                du_buf.at[:, half(core, half_hidden)], du_near.at[layer, at_rows], out_sems.at[1]
            ),
            remote(
                du_buf.at[:, half(theirs, half_hidden)],
                du_far.at[layer, at_rows],
                far_send.at[1],
                far_recv.at[1, layer],
                "pipe",
                theirs,
            ),
        ]

    def result_copies(chunk):
        at_rows = chunk_rows(chunk)
        return [
            pltpu.make_async_copy(result.at[at_rows], dy0_out.at[at_rows], once_sems.at[chunk]),
            remote(
                result.at[at_rows],
                dy0_far.at[at_rows],
                result_send.at[chunk],
                far_recv.at[2, 0],
                "pipe",
                theirs,
            ),
        ]

    def start_all(copies):
        for item in copies:
            item.start()

    def left_all(copies):
        copies[0].wait()
        copies[1].wait_send()

    def far_arrived(i, layer, ref):
        remote(ref, ref, far_send.at[0], far_recv.at[i, layer], "pipe", theirs).wait_recv()

    start_all(early_loads_)
    dense_copy(1, "start")
    up_load(cot_ref.at[core, (LINE - 1) * rows : LINE * rows]).start()
    start_all(early_loads(jnp.int32(0)))
    slope_load(jnp.int32(0)).start()
    start_all(kv_copies(1))
    for i in range(RING - 1):
        ring_copy(jnp.int32(i), "start")
    qkv_copy(jnp.int32(0), "start")
    dots.prime(0)

    barrier = pltpu.get_barrier_semaphore()

    def tell(where):
        pl.semaphore_signal(barrier, inc=1, device_id=where, device_id_type=pl.DeviceIdType.MESH)

    def tell_peer(other, _):
        tell({"pipe": theirs, "dp": other})

        @pl.when(other != dp_rank)
        def _():
            tell({"dp": other})

        return 0

    lax.fori_loop(0, dp_size, tell_peer, 0)

    for other in range(LINE):

        @pl.when(rank != other)
        def _():
            tell({"tensor": jnp.int32(other)})

    pl.semaphore_wait(barrier, 2 * dp_size - 1 + LINE - 1)

    early_emit()
    sums_ref[...] = jnp.zeros_like(sums_ref)

    keep = lax.broadcasted_iota(jnp.int32, (rows, rows), 0) <= lax.broadcasted_iota(
        jnp.int32, (rows, rows), 1
    )

    def attention(chunk, slot):
        here = slice(chunk * rows, (chunk + 1) * rows)
        spans = ([(slice(0, chunk * rows), False)] if chunk else []) + [(here, True)]
        tables = (cos_ref[here, :], -near_ref[here, :], -far_ref[here, :])

        def pair(j, _):
            lanes = pl.ds(pl.multiple_of(j * LANES, LANES), LANES)
            query, upstream = q_buf[slot, :, lanes], do_buf[:, lanes]
            product = upstream.astype(F32) * o_buf[slot, :, lanes].astype(F32)
            grads = []
            key_terms = [None] * len(spans)
            value_terms = [None] * len(spans)
            for which in range(LANES // HEAD_DIM):
                mask = head_mask(rows, which)
                mine = jnp.where(mask, query, jnp.zeros_like(query))
                mine_up = jnp.where(mask, upstream, jnp.zeros_like(upstream))
                logs = logs_buf[slot, j, which : which + 1, :]
                centre = as_row(jnp.sum(jnp.where(mask, product, 0.0), axis=1, keepdims=True))
                grad = None
                for i, (span, diagonal) in enumerate(spans):
                    keys = k_all[span, lanes]
                    probs = jnp.exp(dot_nt(keys, mine) - logs)
                    if diagonal:
                        probs = jnp.where(keep, probs, 0.0)
                    grad_probs = dot_nt(v_all[span, lanes], mine_up)
                    grad_scores = (probs * (grad_probs - centre)).astype(BF)
                    value_term = dot_nn(probs.astype(BF), mine_up)
                    key_term = dot_nn(grad_scores, mine)
                    term = dot_tn(grad_scores, keys)
                    grad = term if grad is None else grad + term
                    if which == 0:
                        key_terms[i], value_terms[i] = key_term, value_term
                    else:
                        dk_all[span, lanes] += key_terms[i] + key_term
                        dv_all[span, lanes] += value_terms[i] + value_term
                grads.append(grad)
            merged = jnp.where(head_mask(rows, 0), grads[0], grads[1]) * scale
            dp_buf[0, :, lanes] = turn(merged, *tables).astype(BF)
            dp_buf[1, :, lanes] = turn(dk_all[here, lanes], *tables).astype(BF)
            dp_buf[2, :, lanes] = dv_all[here, lanes].astype(BF)
            return 0

        lax.fori_loop(0, local // LANES, pair, 0)


    def step_body(step, _):
        layer, chunk, slot = layer_of(step), chunk_of(step), 0
        lead = layer == 1
        starting = lax.rem(step, LINE) == 0
        at_rows = chunk_rows(chunk)

        @pl.when(step == LINE)
        def _():
            early_deliver("wait")
            left_all(dp_copies(step - 1))
            left_all(du_copies(step - 1))
            far_arrived(0, 1, dp_far.at[1])
            far_arrived(1, 1, du_far.at[1])
            dots.prime(1)

        @pl.when(step >= LINE)
        def _():
            summed.stage_f(chunk)
            start_all(result_copies(chunk))
            up_buf[...] = result[at_rows, :]
            x_load(in_ref.at[core, at_rows]).start()

        @pl.when(lead)
        def _():
            up_load(cot_ref.at[core, at_rows]).wait()
            x_load(x1_ref.at[at_rows]).start()

        @pl.when(starting)
        def _():
            dense_copy(layer, "wait")
            dk_all[...] = jnp.zeros_like(dk_all)
            dv_all[...] = jnp.zeros_like(dv_all)

        slope_load(step).wait()

        @pl.when((step >= 1) & (step != LINE))
        def _():
            left_all(du_copies(step - 1))

        def hidden_part(i, _):
            cols = pl.ds(pl.multiple_of(i * tile, tile), tile)
            index = step * ring_tiles + i
            ring_copy(index, "wait")
            ring_copy(index + RING - 1, "start")
            weight = ring.at[lax.rem(index, RING)]
            value = dot_nt(up_buf[...], weight[...]) * slope_buf[:, cols].astype(F32)
            value = value.astype(BF)
            du_buf[:, cols] = value
            sums_ref[layer, 2:3, cols] += jnp.sum(value.astype(F32), axis=0, keepdims=True)
            return 0

        lax.fori_loop(0, up_tiles, hidden_part, 0)
        start_all(du_copies(step))

        @pl.when(step + 1 < STEPS)
        def _():
            slope_load(step + 1).start()

        @pl.when(step == STEPS - 1)
        def _():
            for c in range(LINE):
                left_all(result_copies(c))
            far_arrived(2, 0, dy0_far)
            dots.prime(2)
            dots.run(2, 0, dp_size // 2)

        do_buf[...] = dot_nt(up_buf[...], dense_w[...]).astype(BF)

        @pl.when(step == LINE - 1)
        def _():
            dense_copy(jnp.int32(0), "start")

        sums_ref[layer, 3:4, :] += jnp.sum(up_buf[...].astype(F32), axis=0, keepdims=True)

        @pl.when(lead)
        def _():
            up_share[chunk] = up_buf[pl.ds(pl.multiple_of(rank * block, block), block), :]

        @pl.when(step + 1 < LINE)
        def _():
            up_load(cot_ref.at[core, chunk_rows(chunk - 1)]).start()

        for item in early_loads(step):
            item.wait()

        @pl.when(starting)
        def _():
            for item in kv_copies(layer):
                item.wait()

        @pl.when((step >= 1) & (step != LINE))
        def _():
            left_all(dp_copies(step - 1))

        for index in range(LINE):

            @pl.when(chunk == index)
            def _():
                attention(index, slot)

        start_all(dp_copies(step))

        @pl.when(step + 1 < STEPS)
        def _():
            start_all(early_loads(step + 1))

        @pl.when(step == LINE - 1)
        def _():
            start_all(kv_copies(jnp.int32(0)))

        for i in range(3):
            sums_ref[layer, 4 + i : 5 + i, 0:local] += jnp.sum(
                dp_buf[i].astype(F32), axis=0, keepdims=True
            )

        @pl.when((step >= 1) & (step <= LINE))
        def _():
            summed.stage_b(chunk_of(step - 1))

        @pl.when((step >= 2) & (step <= LINE + 1))
        def _():
            summed.stage_d(chunk_of(step - 2))

        @pl.when((step >= 3) & (step <= LINE + 2))
        def _():
            summed.stage_e(chunk_of(step - 3), 1)

        @pl.when(step > LINE)
        def _():
            shared.relay(chunk_of(step - 1), 1)

        @pl.when(lead)
        def _():
            dots.run(0, lax.div(step * dp_size, LINE), lax.div((step + 1) * dp_size, LINE))

        @pl.when((step >= LINE) & (step < STEPS - 1))
        def _():
            begin = jnp.where(step == LINE, 0, lax.div((step - LINE + 1) * dp_size, LINE))
            dots.run(1, begin, lax.div((step - LINE + 2) * dp_size, LINE))

        @pl.when(step == 2)
        def _():
            early_sent(1, (LINE - 1,))

        @pl.when(step == 3)
        def _():
            early_finish()
            early_sent(0, (0, 1, 2))
            early_sent(1, (2, 1))

        x_load(x1_ref.at[at_rows]).wait()
        small = rows // 8

        def statistics(i, _):
            span = pl.ds(pl.multiple_of(i * small, small), small)
            values = x_buf[span, :].astype(F32)
            mean = jnp.mean(values, axis=-1, keepdims=True)
            centre = values - mean
            mean_buf[span, :] = mean
            inverse_buf[span, :] = lax.rsqrt(
                jnp.mean(centre * centre, axis=-1, keepdims=True) + ln_eps
            )
            return 0

        lax.fori_loop(0, 8, statistics, 0)

        @pl.when(lead)
        def _():
            x_share[chunk] = x_buf[pl.ds(pl.multiple_of(rank * block, block), block), :]

        @pl.when(jnp.logical_not(lead))
        def _():
            summed.sent_part(chunk)

        def normed_part(i, _):
            cols = pl.ds(pl.multiple_of(i * tile, tile), tile)
            index = step * ring_tiles + up_tiles + i
            ring_copy(index, "wait")

            @pl.when(index + RING - 1 < STEPS * ring_tiles)
            def _():
                ring_copy(index + RING - 1, "start")

            qkv_index = step * out_tiles + i
            qkv_copy(qkv_index, "wait")

            @pl.when(qkv_index + 1 < STEPS * out_tiles)
            def _():
                qkv_copy(qkv_index + 1, "start")

            value = dot_nt(du_buf[...], ring[lax.rem(index, RING)])
            for c in range(3):
                value = value + dot_nt(dp_buf[c], ring_qkv[lax.rem(qkv_index, 2), c])
            xhat = (x_buf[:, cols].astype(F32) - mean_buf[...]) * inverse_buf[...]
            sums_ref[layer, 0:1, cols] += jnp.sum(value * xhat, axis=0, keepdims=True)
            sums_ref[layer, 1:2, cols] += jnp.sum(value, axis=0, keepdims=True)
            part[chunk, :, cols] = value.astype(BF)

            @pl.when(jnp.logical_not(lead))
            def _():
                shared.emit(chunk, i)

            return 0

        lax.fori_loop(0, out_tiles, normed_part, 0)

        @pl.when(lead)
        def _():
            summed.stage_a(chunk)

        @pl.when((step >= 1) & (step <= LINE))
        def _():
            summed.stage_c(chunk_of(step - 1))

        @pl.when((step >= 2) & (step <= LINE + 1))
        def _():
            summed.stage_e(chunk_of(step - 2), 0)

        @pl.when(step == 0)
        def _():
            early_relay(0, 1)
            early_relay(1, 2)

        @pl.when(step == 1)
        def _():
            early_relay(0, 2)
            early_relay(1, 1)

        @pl.when(step > LINE)
        def _():
            shared.relay(chunk_of(step - 1), 2)

        return 0

    lax.fori_loop(0, STEPS, step_body, 0)

    smalls.peers("start")
    deliver(core, 1, result.at[mine], grads_out, grads_sems, "start")
    deliver(core, 0, x1_ref.at[mine], acts_out, acts_sems, "start")
    reload = [up_load(result.at[mine]), x_load(in_ref.at[core, mine])]
    start_all(reload)
    some = dp_size // 2
    dots.run(2, some, dp_size)
    last_step = jnp.int32(STEPS - 1)
    left_all(dp_copies(last_step))
    left_all(du_copies(last_step))
    far_arrived(0, 0, dp_far.at[0])
    far_arrived(1, 0, du_far.at[0])
    dots.prime(3)
    shared.relay(0, 1)
    dots.run(3, 0, some)
    shared.relay(0, 2)
    dots.run(3, some, dp_size)
    smalls.pass_on()
    shared.arrived()
    for item in reload:
        item.wait()
    small = rows // 8

    def last(i, _):
        span = pl.ds(pl.multiple_of(i * small, small), small)
        up_buf[span, :] = norm_back(0, x_buf[span, :], up_buf[span, :], shared.total(span))
        return 0

    lax.fori_loop(0, 8, last, 0)
    deliver(core, 0, up_buf, grads_out, grads_sems, "start")
    for chunk in range(LINE):
        shared.sent(chunk)

    x1_mine = x_load(x1_ref.at[mine])
    x1_mine.start()
    part_loads = [
        pltpu.make_async_copy(
            part1_ref.at[c * rows : (c + 1) * rows], part.at[c], once_sems.at[c]
        )
        for c in (1, 2)
    ]
    start_all(part_loads)
    for offset in (-1, 1):
        other = rank + offset

        @pl.when((other >= 0) & (other < LINE))
        def _():
            pl.semaphore_signal(
                free_sem, inc=1, device_id={"tensor": other}, device_id_type=pl.DeviceIdType.MESH
            )

    for item in part_loads:
        item.wait()
    pl.semaphore_wait(
        free_sem, jnp.where(rank > 0, 1, 0) + jnp.where(rank < LINE - 1, 1, 0)
    )
    for chunk in (2, 1):

        def emit(piece, _):
            shared1.emit(chunk, piece)
            return 0

        lax.fori_loop(0, out_tiles, emit, 0)
    smalls.finish()
    for chunk in (2, 1):
        shared1.relay(chunk, 1)
    middle = (rank == 1) | (rank == 2)

    @pl.when(middle)
    def _():
        shared1.arrived()

    x1_mine.wait()
    deliver(core, 0, up_buf, grads_out, grads_sems, "wait")

    def last_rows(i, _):
        span = pl.ds(pl.multiple_of(i * small, small), small)
        value = x_buf[span, :].astype(F32) + shared1.total(span) + vectors[1, 3:4, 0:width]
        up_buf[span, :] = value.astype(BF)
        return 0

    @pl.when(middle)
    def _():
        lax.fori_loop(0, 8, last_rows, 0)
        deliver(core, 1, up_buf, acts_out, acts_sems, "start")

    deliver(core, 1, result.at[mine], grads_out, grads_sems, "wait")
    deliver(core, 0, x1_ref.at[mine], acts_out, acts_sems, "wait")

    @pl.when(middle)
    def _():
        deliver(core, 1, up_buf, acts_out, acts_sems, "wait")

    delivered(core, grads_out, grads_sems)
    delivered(core, acts_out, acts_sems)
    for chunk in range(LINE):
        summed.sent_rest(chunk)
        if chunk in (1, 2):
            shared1.sent(chunk)
    for index in range(4):
        dots.all_sent(index)
    for kind in range(2):
        dots.all_received(kind)


def backward_both(
    dp_size, cotangent, inputs, x1, part1, saved, own_w, other_w, sides, vectors, tables
):
    slope, query, key, value, merged, logs = saved
    _, length, width = inputs.shape
    w_qkv, w_fc1, w_dense, w_fc2 = own_w
    local, hidden = w_dense.shape[0], w_fc1.shape[1]
    rows = length // LINE
    block = rows // LINE
    pairs = local // LANES
    tile = min(TILE, width)
    out_tiles = width // tile
    keep = width // dp_size
    down, up = hidden // 2 + local // 2, hidden // 2 + 3 * (local // 2)

    def bf(*shape):
        return jax.ShapeDtypeStruct(shape, BF)

    def room(*shape):
        return pltpu.VMEM(shape, BF)

    whole = pl.BlockSpec(memory_space=pltpu.VMEM)
    away = pl.BlockSpec(memory_space=pl.ANY)
    dma = pltpu.SemaphoreType.DMA
    outs = [
        bf(2, rows, width),
        bf(2, rows, width),
        bf(length, width),
        bf(length, width),
        bf(2, length, hidden // 2),
        bf(2, length, hidden // 2),
        bf(2, 3, length, local // 2),
        bf(2, 3, length, local // 2),
        bf(2, dp_size, down, keep),
        bf(2, dp_size, keep, up),
        bf(2, dp_size, down, keep),
        bf(2, dp_size, keep, up),
    ]
    most = max(width, hidden)
    return pl.pallas_call(
        functools.partial(backward_kernel, dp_size),
        name="backward_both",
        in_specs=[away] * 24 + [whole] * 4,
        out_specs=[away] * len(outs) + [whole],
        out_shape=outs + [jax.ShapeDtypeStruct((8, most), F32)],
        scratch_shapes=[
            room(RING, tile, width),
            room(2, 3, tile, local),
            room(local, width),
            room(rows, width),
            room(rows, width),
            room(rows, hidden),
            room(1, rows, local),
            room(1, rows, local),
            pltpu.VMEM((1, pairs, 8, rows), F32),
            room(length, local),
            room(length, local),
            pltpu.VMEM((length, local), F32),
            pltpu.VMEM((length, local), F32),
            room(rows, local),
            room(3, rows, local),
            room(rows, hidden),
            room(LINE, rows, width),
            pltpu.VMEM((rows, 1), F32),
            pltpu.VMEM((rows, 1), F32),
            room(LINE, block, width),
            room(LINE, block, width),
            room(length, width),
        ]
        + line_sum_scratch(rows, width)
        + [room(LINE + 1, rows, width)]
        + [dma((2, LINE * out_tiles))] * 4
        + [pltpu.SemaphoreType.REGULAR, dma((2, 2, out_tiles))]
        + [
            room(2, 2 * length, keep),
            room(2 * length, max(down, up)),
            room(2, max(keep, TILE), max(keep, TILE)),
            dma((2, 2)),
            dma((8,)),
            dma((2,)),
            dma((4, dp_size)),
            dma((2, 2)),
        ]
        + [
            dma((RING,)),
            dma((2,)),
            dma((1,)),
            dma((6, 2)),
            dma((2,)),
            dma((2,)),
            dma((2,)),
            dma((3, 2)),
            dma((LINE,)),
            dma((LINE,)),
            dma((3,)),
            dma((3,)),
            pltpu.VMEM((2, 8, most), F32),
            pltpu.VMEM((2, dp_size, 8, most), F32),
            pltpu.VMEM((LINE + 1, 8, most), F32),
            dma((2, dp_size)),
            dma((2,)),
            dma((LINE,)),
            dma((LINE,)),
        ],
        compiler_params=pltpu.CompilerParams(
            collective_id=1, has_side_effects=True, vmem_limit_bytes=63 * MIB
        ),
        cost_estimate=pl.CostEstimate(
            flops=16 * length * width * (4 * local + 2 * hidden),
            bytes_accessed=400 * MIB,
            transcendentals=0,
        ),
    )(
        cotangent, inputs, x1, part1, slope, query, key, value, merged, logs, *own_w, *other_w, *sides, vectors, *tables
    )


def some_rows_total(got_ref, start):
    span = pl.ds(pl.multiple_of(start, 16), 16)
    total = got_ref[0, 0, span, :].astype(F32)
    for sender in range(1, got_ref.shape[1]):
        total = total + got_ref[0, sender, span, :].astype(F32)
    return span, total


def down_kernel(got_ref, wide_ref, narrow_ref):
    cut = wide_ref.shape[0]

    def fill(out_ref, base):
        def one(i, _):
            _, total = some_rows_total(got_ref, base + i * 16)
            out_ref[pl.ds(pl.multiple_of(i * 16, 16), 16), :] = total
            return 0

        lax.fori_loop(0, out_ref.shape[0] // 16, one, 0)

    fill(wide_ref, 0)
    fill(narrow_ref, cut)


def down_total(got, hidden, local):
    _, peers, rows, keep = got.shape
    some = min(256, keep)
    return pl.pallas_call(
        down_kernel,
        name="down_total",
        compiler_params=pltpu.CompilerParams(vmem_limit_bytes=40 * MIB),
        grid=(2, keep // some),
        in_specs=[pl.BlockSpec((1, peers, rows, some), lambda part, i: (part, 0, 0, i))],
        out_specs=[
            pl.BlockSpec((hidden // 2, some), lambda part, i: (part, i)),
            pl.BlockSpec((local // 2, some), lambda part, i: (part, i)),
        ],
        out_shape=[
            jax.ShapeDtypeStruct((hidden, keep), F32),
            jax.ShapeDtypeStruct((local, keep), F32),
        ],
    )(got)


def up_kernel(got_ref, wide_ref, three_ref):
    cut, side = wide_ref.shape[1], three_ref.shape[2]

    def one(i, _):
        span, total = some_rows_total(got_ref, i * 16)
        wide_ref[span, :] = total[:, :cut]
        for c in range(3):
            three_ref[c, span, :] = total[:, cut + c * side : cut + (c + 1) * side]
        return 0

    lax.fori_loop(0, wide_ref.shape[0] // 16, one, 0)


def up_total(got, hidden, local):
    _, peers, keep, cols = got.shape
    some = min(256, keep)
    return pl.pallas_call(
        up_kernel,
        name="up_total",
        compiler_params=pltpu.CompilerParams(vmem_limit_bytes=40 * MIB),
        grid=(2, keep // some),
        in_specs=[pl.BlockSpec((1, peers, some, cols), lambda part, i: (part, 0, i, 0))],
        out_specs=[
            pl.BlockSpec((some, hidden // 2), lambda part, i: (i, part)),
            pl.BlockSpec((3, some, local // 2), lambda part, i: (0, i, part)),
        ],
        out_shape=[
            jax.ShapeDtypeStruct((keep, hidden), F32),
            jax.ShapeDtypeStruct((3, keep, local), F32),
        ],
    )(got)


def body(
    inputs, cotangent, ln_gain, ln_bias, w_qkv, b_qkv, w_dense, b_dense, w_fc1, b_fc1, w_fc2, b_fc2
):
    core = lax.axis_index("pipe")
    rank = lax.axis_index("tensor")
    dp_size = lax.axis_size("dp")
    dp_rank = lax.axis_index("dp")
    _, length, width = inputs.shape
    lines = lax.axis_size("tensor")
    local = w_qkv.shape[3]
    hidden = w_fc1.shape[2]

    tables = rotary_tables(length)
    own_w = (w_qkv[0], w_fc1[0], w_dense[0], w_fc2[0])

    results = forward_both(
        inputs, own_w, (ln_gain, ln_bias, b_qkv, b_dense, b_fc1, b_fc2), tables
    )
    other_w = results[:4]
    h, h_far, query, key, value, merged, merged_near, merged_far = results[4:12]
    act_near, act_far, slope, logs, x1, part1, vectors = results[12:]
    saved = (slope, query, key, value, merged, logs)

    sides = (h, h_far, act_near, act_far, merged_near, merged_far)
    grads = backward_both(
        dp_size, cotangent, inputs, x1, part1, saved, own_w, other_w, sides, vectors, tables
    )
    acts, grads_in = grads[:2]
    down, up, sums = grads[10:]
    out_fc2, out_dense = down_total(down, hidden, local)
    out_fc1, out_qkv = up_total(up, hidden, local)
    place = rank * dp_size + dp_rank

    def piece(rows, count, index, parts):
        size = count // parts
        return lax.dynamic_slice_in_dim(rows[:, :count], index * size, size, 1)

    out_norm = piece(sums[0:2], width, place, lines * dp_size)
    out_bfc1 = piece(sums[2:3], hidden, dp_rank, dp_size)
    out_bout = piece(sums[3:4], width, dp_rank, dp_size)
    out_bqkv = piece(sums[4:7], local, dp_rank, dp_size)
    return (
        acts[None],
        grads_in[None],
        out_norm[0:1],
        out_norm[1:2],
        out_qkv[None],
        out_bqkv[None],
        out_dense[None],
        out_bout,
        out_fc1[None],
        out_bfc1,
        out_fc2[None],
        out_bout,
    )


def solution(mesh):
    in_specs = (
        P("dp", None, None),
        P("dp", None, None),
        P("pipe", None),
        P("pipe", None),
        P("pipe", None, None, "tensor"),
        P("pipe", None, "tensor"),
        P("pipe", "tensor", None),
        P("pipe", None),
        P("pipe", None, "tensor"),
        P("pipe", "tensor"),
        P("pipe", "tensor", None),
        P("pipe", None),
    )
    out_specs = (
        P("pipe", "dp", "tensor", None),
        P("pipe", "dp", "tensor", None),
        P("pipe", ("tensor", "dp")),
        P("pipe", ("tensor", "dp")),
        P("pipe", None, "dp", "tensor"),
        P("pipe", None, ("tensor", "dp")),
        P("pipe", "tensor", "dp"),
        P("pipe", "dp"),
        P("pipe", "dp", "tensor"),
        P("pipe", ("tensor", "dp")),
        P("pipe", "tensor", "dp"),
        P("pipe", "dp"),
    )
    return jax.shard_map(body, mesh=mesh, in_specs=in_specs, out_specs=out_specs, check_vma=False)
```
